128 devices in a mesh: dp: 8 (over z_lo, x), ctx: 16 (over z_hi, y, core).
Axes of the slice: x: 4, y: 4, z: 4 (z_hi: 2, z_lo: 2; z = z_hi * 2 + z_lo), core: 2. Of those that a mesh axis runs over, the one named last changes fastest.
Arguments:
- hidden_in: bfloat16 [16384, 576], P(('dp', 'ctx')), may hold values from -6 to 6
- positions: int32 [16384], P('dp'), may hold values from 0 to 2047, as said below
- attn_gain: bfloat16 [2, 576], P(None, 'dp'), may hold values from 0.25 to 1.75
- w_query: bfloat16 [2, 576, 576], P(None, 'dp'), may hold values from -0.25 to 0.25
- w_key: bfloat16 [2, 576, 192], P(None, 'dp'), may hold values from -0.25 to 0.25
- w_value: bfloat16 [2, 576, 192], P(None, 'dp'), may hold values from -0.25 to 0.25
- w_output: bfloat16 [2, 576, 576], P(None, 'dp'), may hold values from -4 to 4
- ffn_gain: bfloat16 [2, 576], P(None, 'dp'), may hold values from 0.25 to 1.75
- w_gate: bfloat16 [2, 576, 1536], P(None, 'dp'), may hold values from -0.25 to 0.25
- w_up: bfloat16 [2, 576, 1536], P(None, 'dp'), may hold values from -0.25 to 0.25
- w_down: bfloat16 [2, 1536, 576], P(None, 'dp'), may hold values from -0.15625 to 0.15625
- grad_out: bfloat16 [16384, 576], P(('dp', 'ctx')), may hold values from -6 to 6
Outputs:
- hidden_out: bfloat16 [16384, 576], P(('dp', 'ctx'))
- grad_hidden: float32 [16384, 576], P(('dp', 'ctx'))
- grad_attn_gain: float32 [2, 576], P(None, 'dp')
- grad_query: float32 [2, 576, 576], P(None, 'dp')
- grad_key: float32 [2, 576, 192], P(None, 'dp')
- grad_value: float32 [2, 576, 192], P(None, 'dp')
- grad_output: float32 [2, 576, 576], P(None, 'dp')
- grad_ffn_gain: float32 [2, 576], P(None, 'dp')
- grad_gate: float32 [2, 576, 1536], P(None, 'dp')
- grad_up: float32 [2, 576, 1536], P(None, 'dp')
- grad_down: float32 [2, 1536, 576], P(None, 'dp')
The draws below stay inside these ranges and needn't reach their ends.
Inputs may be any that keep to these rules, and one draw needn't show every extreme that they name: Rows s*2048 to (s+1)*2048 - 1 form sequence s and hold each of its positions once. Its positions are cut into 32 blocks of 64 consecutive positions; each aligned run of 128 rows holds, in increasing order, block j followed by block 31-j, with a different j in each run of a sequence.
All inputs are finite; a program needn't handle non-finite values.
Results may differ from the reference program's by a relative error of at most 0.028.
Values may be sent and summed in bfloat16 or wider, within the bound.
A program may use at most 192 MiB of HBM per device.

```python
import jax
import jax.numpy as jnp
from jax import lax

D = 576
HEADS = 9
KV_HEADS = 3
HEAD_DIM = 64
FF = 1536
LAYERS = 2
TOK_DEV = 128
SEQ = 2048
TOKENS = 16384


def draw_positions(key, part):
    key = jax.random.fold_in(key, 17)
    count = TOKENS // SEQ
    pairs = SEQ // TOK_DEV
    half = TOK_DEV // 2
    orders = jax.vmap(lambda single: jax.random.permutation(single, pairs))(jax.random.split(key, count))
    orders = orders.astype(jnp.int32)[:, :, None]
    offsets = jnp.arange(half, dtype=jnp.int32)[None, None, :]
    lower = orders * half + offsets
    upper = (2 * pairs - 1 - orders) * half + offsets
    return jnp.concatenate([lower, upper], axis=2).reshape(TOKENS).astype(jnp.int32)


def block_scale(key, extent, pieces, least, top_value):
    level, own = 1.0, jax.random.fold_in(key, 6)
    for position, shards_of in pieces:
        heights = jnp.exp(jax.random.uniform(jax.random.fold_in(own, position), (shards_of,), jnp.float32, least / len(pieces), top_value / len(pieces)))
        level = level * jnp.repeat(heights, extent[position] // shards_of).reshape([-1 if axis == position else 1 for axis in range(len(extent))])
    return level


def scatter_about(key, dims, deviation, limit, pieces=(), kind=jnp.bfloat16):
    values = deviation * jax.random.normal(key, dims, jnp.float32)
    if pieces:
        values = values * block_scale(key, dims, pieces, -0.22, 0.18)
    return jnp.clip(values, -limit, limit).astype(kind)


def setup_inputs(seed: int = 0) -> dict:
    key_of = jax.random.split(jax.random.key(seed), 13)
    return {
        "hidden_in": scatter_about(key_of[0], (TOKENS, D), 1.0, 6.0, ((0, 128),)),
        "positions": draw_positions(jax.random.fold_in(key_of[12], 71), 0),
        "attn_gain": jnp.clip(1.0 + 0.15 * jax.random.normal(key_of[2], (LAYERS, D), jnp.float32), 0.25, 1.75).astype(jnp.bfloat16),
        "w_query": scatter_about(key_of[3], (LAYERS, D, D), D ** -0.5, 0.25, ((1, 8),)),
        "w_key": scatter_about(key_of[4], (LAYERS, D, KV_HEADS * HEAD_DIM), D ** -0.5, 0.25, ((1, 8),)),
        "w_value": scatter_about(key_of[5], (LAYERS, D, KV_HEADS * HEAD_DIM), D ** -0.5, 0.25, ((1, 8),)),
        "w_output": scatter_about(key_of[6], (LAYERS, D, D), (max(1, D * 8 // SEQ)) ** -0.5, 4.0, ((1, 8),)),
        "ffn_gain": jnp.clip(1.0 + 0.15 * jax.random.normal(key_of[7], (LAYERS, D), jnp.float32), 0.25, 1.75).astype(jnp.bfloat16),
        "w_gate": scatter_about(key_of[8], (LAYERS, D, FF), D ** -0.5, 0.25, ((1, 8),)),
        "w_up": scatter_about(key_of[9], (LAYERS, D, FF), D ** -0.5, 0.25, ((1, 8),)),
        "w_down": scatter_about(key_of[10], (LAYERS, FF, D), FF ** -0.5, 0.15625, ((1, 8),)),
        "grad_out": scatter_about(key_of[11], (TOKENS, D), 1.0, 6.0, ((0, 128),)),
    }


@jax.custom_vjp
def low(v):
    return lax.optimization_barrier(v.astype(jnp.bfloat16)).astype(jnp.float32)

@jax.custom_vjp
def low_back(v):
    return v

def low_keep(v):
    return (low(v), None)

def low_pass(kept, grad):
    return (grad,)

def back_keep(v):
    return (v, None)

def back_low(kept, grad):
    return (low(grad),)
low.defvjp(low_keep, low_pass)
low_back.defvjp(back_keep, back_low)
eps_norm = 1e-05
rope_base = 100000.0

def matmul(left, right):
    return jnp.dot(left, right, preferred_element_type=jnp.float32, precision=lax.Precision.HIGHEST)

def normed(values, gain):
    factor = lax.rsqrt(lax.optimization_barrier(jnp.mean(values * values, axis=-1, keepdims=True)) + eps_norm)
    return values * factor * gain

def angles(place, head_dim):
    half = head_dim // 2
    freq = jnp.exp(-jnp.log(rope_base) * (2.0 * jnp.arange(half, dtype=jnp.float32) / head_dim))
    angle = place.astype(jnp.float32)[:, None] * freq[None, :]
    return (jnp.cos(angle)[:, None, :], jnp.sin(angle)[:, None, :])

def rotate(values, cosine, sine):
    half = values.shape[-1] // 2
    first = values[..., :half]
    second = values[..., half:]
    return jnp.concatenate([first * cosine - second * sine, second * cosine + first * sine], axis=-1)

def attend(inputs):
    query, keys, values, place = inputs
    length = query.shape[0]
    group = HEADS // KV_HEADS
    grouped = query.reshape(length, KV_HEADS, group, HEAD_DIM)
    scores = jnp.einsum('qhgd,khd->hgqk', grouped, keys, precision=lax.Precision.HIGHEST)
    scores = low_back(scores) * HEAD_DIM ** (-0.5)
    allowed = place[:, None] >= place[None, :]
    scores = jnp.where(allowed[None, None], scores, -1000000000.0)
    top = lax.optimization_barrier(jnp.max(scores, axis=-1, keepdims=True))
    expo = jnp.exp(scores - top)
    probs = low(expo / lax.optimization_barrier(jnp.sum(expo, axis=-1, keepdims=True)))
    mixed = jnp.einsum('hgqk,khd->qhgd', probs, values, precision=lax.Precision.HIGHEST)
    return mixed.reshape(length, HEADS * HEAD_DIM)

def layer(hidden, params, cosine, sine, place_seq):
    gain_attn, query_w, key_w, value_w, output_w, gain_ffn, gate_w, up_w, down_w = params
    rows = hidden.shape[0]
    count = rows // SEQ
    normal_a = low(normed(hidden, gain_attn))
    query = low_back(matmul(normal_a, query_w)).reshape(rows, HEADS, HEAD_DIM)
    keys = low_back(matmul(normal_a, key_w)).reshape(rows, KV_HEADS, HEAD_DIM)
    values = low(low_back(matmul(normal_a, value_w))).reshape(rows, KV_HEADS, HEAD_DIM)
    query = low(rotate(query, cosine, sine))
    keys = low(rotate(keys, cosine, sine))
    mixed = lax.map(jax.checkpoint(attend), (query.reshape(count, SEQ, HEADS, HEAD_DIM), keys.reshape(count, SEQ, KV_HEADS, HEAD_DIM), values.reshape(count, SEQ, KV_HEADS, HEAD_DIM), place_seq))
    mixed = low(low_back(mixed.reshape(rows, D)))
    hidden = hidden + low_back(matmul(mixed, output_w))
    normal_b = low(normed(hidden, gain_ffn))
    gate = low_back(matmul(normal_b, gate_w))
    upper = low_back(matmul(normal_b, up_w))
    middle = low(jax.nn.silu(gate) * upper)
    return hidden + low_back(matmul(middle, down_w))

def reference(hidden_in, positions, attn_gain, w_query, w_key, w_value, w_output, ffn_gain, w_gate, w_up, w_down, grad_out):
    cosine, sine = angles(positions, HEAD_DIM)
    place_seq = positions.reshape(TOKENS // SEQ, SEQ)
    weights = tuple((item.astype(jnp.float32) for item in (attn_gain, w_query, w_key, w_value, w_output, ffn_gain, w_gate, w_up, w_down)))

    def forward(hidden, *stacked):
        for index in range(LAYERS):
            hidden = layer(hidden, tuple((item[index] for item in stacked)), cosine, sine, place_seq)
        return hidden
    result, pull = jax.vjp(forward, hidden_in.astype(jnp.float32), *weights)
    grads = pull(grad_out.astype(jnp.float32))
    return (result.astype(jnp.bfloat16), grads[0], grads[1], grads[2], grads[3], grads[4], grads[5], grads[6], grads[7], grads[8], grads[9])
```

```python
import jax
import jax.numpy as jnp
import numpy as np
from jax import lax
from jax.experimental import pallas as pl
from jax.experimental.pallas import tpu as pltpu
from jax.sharding import PartitionSpec as P

D = 576
HEADS = 9
KV_HEADS = 3
HEAD_DIM = 64
FF = 1536
LAYERS = 2
ROWS = 128
ND = 8
NC = 16
NCHIP = 8
R = 80
PD = 640
MESH = pl.DeviceIdType.MESH
bf16 = jnp.bfloat16
f32 = jnp.float32
NEG = -1e30
eps_norm = 1e-05
rope_base = 100000.0


def nn(a, b):
    return lax.dot_general(a, b, (((1,), (0,)), ((), ())), preferred_element_type=f32)


def nt(a, b):
    return lax.dot_general(a, b, (((1,), (1,)), ((), ())), preferred_element_type=f32)


def tn(a, b):
    return lax.dot_general(a, b, (((0,), (0,)), ((), ())), preferred_element_type=f32)


def kernel(
    hid, gout, cosm, sinm, mlow, e1, e2, gains, wgate, wup, wdown, wattn,
    hout, ghid, ggains, ggate, gup, gdown, gattn,
    land, wd, kvl, dkv, dkr1, dkr2, rs1, rs2, dpb, dpr, fin,
    mid, hs, h1s, apad, bpad, mixp, qc, doc, oT, lse, oz, dqz,
    s1, s2, bias, mk, zpad, gain, acc1, acc2, go4,
    send, recv,
):
    d = lax.axis_index("dp")
    c = lax.axis_index("ctx")
    k = lax.rem(c, 2)
    i = c // 2
    sib = {"ctx": i * 2 + 1 - k}
    count = [0]

    def sems(n):
        count[0] += n
        return count[0] - n

    def dplus(m):
        return lax.rem(d + m, ND)

    def dminus(m):
        return lax.rem(d - m + ND, ND)

    def iplus(m):
        return lax.rem(i + m, NCHIP)

    def iminus(m):
        return lax.rem(i - m + NCHIP, NCHIP)

    def chip(j):
        return {"ctx": j * 2 + k}

    def rc(src, dst, s, dev):
        return pltpu.make_async_remote_copy(
            src_ref=src, dst_ref=dst, send_sem=send.at[s], recv_sem=recv.at[s],
            device_id=dev, device_id_type=MESH,
        )

    def each(f, lo=1, hi=8):
        def step(m, carry):
            f(m)
            return carry
        lax.fori_loop(lo, hi, step, 0)

    def put(l, u, val):
        full = jnp.concatenate([val.astype(f32), jnp.zeros((8, 128), f32)], axis=0)
        land[l, u, d] = full.astype(bf16)

    def pack_attn(l):
        val = wattn[l]
        for t in range(12):
            put(l, 36 + t, val[:, 128 * t:128 * t + 128])
        first = wattn[l, :, 0:128].astype(f32)
        land[l, 36, d] = jnp.concatenate([first, gains[l]], axis=0).astype(bf16)

    def pack_ffn(l):
        for t in range(12):
            put(l, t, wgate[l, :, 128 * t:128 * t + 128])
            put(l, 12 + t, wup[l, :, 128 * t:128 * t + 128])
        for g in range(12):
            for lt in range(5):
                rows = slice(16 * lt, 16 * lt + 16)
                if lt < 4:
                    land[l, 24 + g, d, rows, :] = wdown[l, 16 * g:16 * g + 16, 128 * lt:128 * lt + 128]
                else:
                    land[l, 24 + g, d, rows, :] = jnp.concatenate(
                        [wdown[l, 16 * g:16 * g + 16, 512:576].astype(f32), jnp.zeros((16, 64), f32)], axis=1
                    ).astype(bf16)

    def wref(l, base, n, half, slot):
        return land.at[l, pl.ds(base + n * half, n), slot]

    def w_start(l, base, n, s0):
        def go(m):
            ref = wref(l, base, n, k, d)
            rc(ref, ref, s0 + m - 1, {"dp": dplus(m)}).start()
        each(go)

    def w_forward(l, base, n, s0, s1_):
        def go(m):
            ref = wref(l, base, n, k, dminus(m))
            rc(ref, ref, s0 + m - 1, {"dp": dplus(m)}).wait_recv()
            rc(ref, ref, s1_ + m - 1, sib).start()
        each(go)

    def w_finish(l, base, n, s0, s1_):
        def go(m):
            ref = wref(l, base, n, 1 - k, dminus(m))
            rc(ref, ref, s1_ + m - 1, sib).wait_recv()
            mine = wref(l, base, n, k, dminus(m))
            rc(mine, mine, s1_ + m - 1, sib).wait_send()
            own = wref(l, base, n, k, d)
            rc(own, own, s0 + m - 1, {"dp": dplus(m)}).wait_send()
        each(go)

    wsem = {}
    for l in range(LAYERS):
        for name in ("A", "F"):
            wsem[l, name] = (sems(7), sems(7))
    span = {"A": (36, 6), "F": (0, 18)}

    kv_s = [(sems(7), sems(8)) for _ in range(LAYERS)]

    def kv_start(l):
        own = kvl.at[l, c]
        rc(own, own, kv_s[l][1] + 7, sib).start()
        def go(m):
            rc(own, own, kv_s[l][0] + m - 1, chip(iplus(m))).start()
        each(go)

    def kv_finish(l):
        def go(m):
            ref = kvl.at[l, iminus(m) * 2 + k]
            rc(ref, ref, kv_s[l][0] + m - 1, chip(iplus(m))).wait_recv()
            rc(ref, ref, kv_s[l][1] + m - 1, sib).start()
        each(go)
        own = kvl.at[l, c]
        other = kvl.at[l, i * 2 + 1 - k]
        rc(other, other, kv_s[l][1] + 7, sib).wait_recv()
        rc(own, own, kv_s[l][1] + 7, sib).wait_send()
        def done(m):
            ref = kvl.at[l, iminus(m) * 2 + 1 - k]
            rc(ref, ref, kv_s[l][1] + m - 1, sib).wait_recv()
            mine = kvl.at[l, iminus(m) * 2 + k]
            rc(mine, mine, kv_s[l][1] + m - 1, sib).wait_send()
            rc(own, own, kv_s[l][0] + m - 1, chip(iplus(m))).wait_send()
        each(done)

    dk_s = [(sems(1), sems(7)) for _ in range(LAYERS)]

    def dk_sib(l):
        return rc(dkv.at[:, 1 - k], dkr1.at[l], dk_s[l][0], sib)

    def dk_sum(l):
        def go(j):
            for h in range(KV_HEADS):
                total = dkv[j, k, h].astype(f32) + dkr1[l, j, h].astype(f32)
                dkv[j, k, h] = total.astype(bf16)
        each(go, 0, 8)

    def dk_chip(l, m):
        return rc(dkv.at[iplus(m), k], dkr2.at[l, m - 1], dk_s[l][1] + m - 1, chip(iplus(m)))

    g_s = [((sems(1), sems(7)), (sems(1), sems(7))) for _ in range(LAYERS)]
    gspan = ((0, 16, 2), (32, 8, 1))

    def g_sib(l, q):
        base, n, _ = gspan[q]
        return rc(
            land.at[l, pl.ds(base + n * (1 - k), n)], rs1.at[l, pl.ds(16 * q, n)], g_s[l][q][0], sib
        )

    def g_sum(l, q):
        base, n, _ = gspan[q]
        def go(u):
            total = land[l, base + n * k + u].astype(f32) + rs1[l, 16 * q + u].astype(f32)
            land[l, base + n * k + u] = total.astype(bf16)
        each(go, 0, n)

    def g_chip(l, q, m):
        base, n, per = gspan[q]
        return rc(
            land.at[l, pl.ds(base + n * k + per * iplus(m), per)],
            rs2.at[l, m - 1, pl.ds(2 * q, per)],
            g_s[l][q][1] + m - 1,
            chip(iplus(m)),
        )

    def g_step(l, q):
        g_sib(l, q).wait()
        g_sum(l, q)
        each(lambda m: g_chip(l, q, m).start())

    def g_total(l, q):
        base, n, per = gspan[q]
        each(lambda m: g_chip(l, q, m).wait())
        for s in range(per):
            total = land[l, base + n * k + per * i + s].astype(f32)
            for m in range(7):
                total = total + rs2[l, m, 2 * q + s].astype(f32)
            dpb[:, l, 2 * q + s] = total.astype(bf16)

    dp_s = sems(7)
    ag_s = (sems(7), sems(8))

    barrier = pltpu.get_barrier_semaphore()
    def hello(m):
        pl.semaphore_signal(barrier, inc=1, device_id={"dp": dplus(m)}, device_id_type=MESH)
        pl.semaphore_signal(barrier, inc=1, device_id=chip(iplus(m)), device_id_type=MESH)
    each(hello)
    pl.semaphore_signal(barrier, inc=1, device_id=sib, device_id_type=MESH)
    pack_attn(0)
    pl.semaphore_wait(barrier, 15)
    w_start(0, *span["A"], wsem[0, "A"][0])
    pack_ffn(0)
    w_start(0, *span["F"], wsem[0, "F"][0])
    pack_attn(1)
    w_start(1, *span["A"], wsem[1, "A"][0])
    pack_ffn(1)
    w_start(1, *span["F"], wsem[1, "F"][0])

    lane = lax.broadcasted_iota(jnp.int32, (128, 128), 1)
    low_half = lane < 64
    first_quarter = lax.rem(lane, 64) < 32
    cos_q = cosm[...]
    sin_q = sinm[...]
    cos_kv = jnp.where(low_half, cos_q, 1.0)
    sin_kv = jnp.where(low_half, sin_q, 0.0)

    def swap(x):
        return jnp.where(first_quarter, pltpu.roll(x, 96, axis=1), pltpu.roll(x, 32, axis=1))

    row = lax.broadcasted_iota(jnp.int32, (1024, 192), 0) - 64 * c
    col = lax.rem(lax.broadcasted_iota(jnp.int32, (1024, 192), 1), 64)
    bias[...] = jnp.where((row > col) & (row < 64), NEG, 0.0)
    mk[...] = jnp.concatenate([mlow[...], mlow[:, 0:64]], axis=1).astype(f32)
    row = lax.broadcasted_iota(jnp.int32, (64, 192), 0)
    col = lax.rem(lax.broadcasted_iota(jnp.int32, (64, 192), 1), 64)
    tri = jnp.where(row > col, NEG, 0.0)
    zpad[...] = jnp.zeros((128, PD), bf16)

    def unit(l, u):
        return land[l, u].reshape(PD, 128)

    def pair(l, u):
        return jnp.concatenate([unit(l, u), unit(l, u + 1)], axis=1)

    def units(l, u, n):
        return jnp.concatenate([unit(l, u + j) for j in range(n)], axis=1)

    def norm_scale(h):
        return lax.rsqrt(jnp.mean(h * h, axis=-1, keepdims=True) + eps_norm)

    def spread(x):
        return nn(x.astype(bf16), e1[...]).astype(bf16)

    def unspread(x):
        hi = x.astype(bf16)
        lo = (x - hi.astype(f32)).astype(bf16)
        return nt(hi, e1[...]) + nt(lo, e1[...])

    def load_gains(l):
        total = jnp.zeros((8, PD), f32)
        for s in range(ND):
            part = land[l, 36, s].astype(f32)[72:80, :]
            wide = jnp.concatenate([part, jnp.zeros((8, PD - 128), f32)], axis=1)
            total = total + (pltpu.roll(wide, 72 * s, axis=1) if s else wide)
        gain[l] = total

    def regroup_down(l):
        def go(j):
            src = lax.rem(j, 12)
            for lt in range(5):
                wd[j // 16, pl.ds(pl.multiple_of(lax.rem(j, 16) * 16, 16), 16), 128 * lt:128 * lt + 128] = land[
                    l, 24 + src, j // 12, 16 * lt:16 * lt + 16, :
                ]
        each(go, 0, 96)

    def scatter_down(l):
        def go(j):
            src = lax.rem(j, 12)
            for lt in range(5):
                land[l, 24 + src, j // 12, 16 * lt:16 * lt + 16, :] = wd[
                    j // 16, pl.ds(pl.multiple_of(lax.rem(j, 16) * 16, 16), 16), 128 * lt:128 * lt + 128
                ]
        each(go, 0, 96)

    def tiles(l, h, j):
        tlo = kvl[l, pl.ds(4 * j, 4), h, 0].reshape(256, 128)
        thi = kvl[l, pl.ds(4 * j, 4), h, 1].reshape(256, 128)
        m = mlow[pl.ds(pl.multiple_of(256 * j, 256), 256), :]
        x2 = jnp.concatenate([tlo * m, thi * (1 - m)], axis=1)
        return tlo, x2, m

    def swiglu_parts(l, t, x):
        g = nn(x, pair(l, 2 * t))
        u = nn(x, pair(l, 12 + 2 * t))
        return g, u

    def forward(l, h):
        hs[l] = h
        w_forward(l, *span["A"], *wsem[l, "A"])
        w_finish(l, *span["A"], *wsem[l, "A"])
        load_gains(l)
        apad[l] = spread(h * norm_scale(h) * gain[l, 0:1, 0:D])
        a = apad[l]
        for s in range(KV_HEADS):
            kv = nn(a, unit(l, 45 + s))
            kv = kv * cos_kv + swap(kv) * sin_kv
            kvl[l, c, s] = kv.astype(bf16).reshape(2, 64, 128)
        kv_start(l)
        for t in range(5):
            q = nn(a, unit(l, 40 + t))
            q = (q * cos_q + swap(q) * sin_q) * HEAD_DIM ** (-0.5)
            for j in ((2 * t - 1, 2 * t) if t else (0,)):
                part = q if j % 2 else pltpu.roll(q, 64, axis=1)
                part = jnp.where(low_half, part, 0.0).astype(bf16)
                g = j % 3
                qc[l, j // 3, 64 * g:64 * g + 64, 0:128] = part[0:64]
                qc[l, j // 3, 64 * g:64 * g + 64, 128:256] = part[64:128]
        w_forward(l, *span["F"], *wsem[l, "F"])
        kv_finish(l)

        def head(s):
            qcat = qc[l, s]
            qT = qcat.astype(f32).T.astype(bf16)
            qhT = qT[128:256]
            top_own = kvl[l, c, s, 1]
            se = nn(top_own, qhT) + tri

            def scores(j, carry):
                ml, mh = carry
                tlo, x2, _ = tiles(l, s, j)
                at = pl.ds(pl.multiple_of(256 * j, 256), 256)
                a1 = nn(tlo, qhT)
                a2 = nn(x2, qT) + bias[at, :]
                s1[at, 0:192] = a1
                s2[at, 0:192] = a2
                is_low = mk[at, :] > 0.5
                ml = jnp.maximum(ml, jnp.max(jnp.where(is_low, a2, NEG), axis=0, keepdims=True))
                mh = jnp.maximum(
                    mh, jnp.max(jnp.maximum(a1, jnp.where(is_low, NEG, a2)), axis=0, keepdims=True)
                )
                return ml, mh

            ml, mh = lax.fori_loop(
                0, 4, scores,
                (jnp.full((1, 192), NEG, f32), jnp.max(se, axis=0, keepdims=True)),
            )
            pe = jnp.exp(se - mh)
            acc1[...] = tn(top_own, pe.astype(bf16))
            acc2[...] = jnp.zeros((256, 192), f32)

            def weigh(j, carry):
                ll, lh = carry
                tlo, x2, _ = tiles(l, s, j)
                at = pl.ds(pl.multiple_of(256 * j, 256), 256)
                is_low = mk[at, :] > 0.5
                p1 = jnp.exp(s1[at, 0:192] - mh)
                p2 = jnp.exp(s2[at, 0:192] - jnp.where(is_low, ml, mh))
                ll = ll + jnp.sum(jnp.where(is_low, p2, 0.0), axis=0, keepdims=True)
                lh = lh + jnp.sum(p1 + jnp.where(is_low, 0.0, p2), axis=0, keepdims=True)
                acc1[...] += tn(tlo, p1.astype(bf16))
                acc2[...] += tn(x2, p2.astype(bf16))
                return ll, lh

            ll, lh = lax.fori_loop(
                0, 4, weigh, (jnp.zeros((1, 192), f32), jnp.sum(pe, axis=0, keepdims=True))
            )
            olow = acc2[64:128, :] / ll
            ohigh = (acc2[192:256, :] + acc1[64:128, :]) / lh
            oT[l, s, 0:64, :] = olow
            oT[l, s, 64:128, :] = ohigh
            lse[l, s, 0:1, :] = ml + jnp.log(ll)
            lse[l, s, 1:2, :] = mh + jnp.log(lh)
            zero = jnp.zeros((64, 192), f32)
            tl = jnp.concatenate([zero, olow], axis=0).T.astype(bf16)
            th = jnp.concatenate([zero, ohigh], axis=0).T.astype(bf16)
            for g in range(3):
                oz[3 * s + g, 0:64, :] = tl[64 * g:64 * g + 64]
                oz[3 * s + g, 64:128, :] = th[64 * g:64 * g + 64]

        each(head, 0, KV_HEADS)
        mixp[l] = nt(jnp.concatenate([oz[j] for j in range(HEADS)], axis=1), e2[...]).astype(bf16)
        y = nn(mixp[l], units(l, 36, 5))
        h1 = h + y[:, 0:D]
        h1s[l] = h1
        bpad[l] = spread(h1 * norm_scale(h1) * gain[l, 1:2, 0:D])
        w_finish(l, *span["F"], *wsem[l, "F"])
        regroup_down(l)

        def ffn(t, total):
            g, u = swiglu_parts(l, t, bpad[l])
            if l == LAYERS - 1:
                s1[pl.ds(pl.multiple_of(128 * t, 128), 128), :] = g
                s2[pl.ds(pl.multiple_of(128 * t, 128), 128), :] = u
            m = (g / (1.0 + jnp.exp(-g)) * u).astype(bf16)
            mid[l, t] = m
            return total + nn(m, wd[t])

        total = lax.fori_loop(0, 6, ffn, jnp.zeros((128, PD), f32))
        return h1 + total[:, 0:D]

    def norm_back(h, g, dn, gain_row):
        r = norm_scale(h)
        xn = h * r
        cc = dn * gain_row
        return (
            g + r * (cc - xn * jnp.mean(cc * xn, axis=-1, keepdims=True)),
            jnp.sum(dn * xn, axis=0, keepdims=True),
        )

    def backward(l, g):
        zpad[:, 0:D] = g.astype(bf16)
        if l < LAYERS - 1:
            regroup_down(l)
        bT = bpad[l].T

        def ffn(t, total):
            dz = zpad[...]
            if l == LAYERS - 1:
                at = pl.ds(pl.multiple_of(128 * t, 128), 128)
                ga, u = s1[at, :], s2[at, :]
            else:
                ga, u = swiglu_parts(l, t, bpad[l])
            dm = nt(dz, wd[t])
            sg = 1.0 / (1.0 + jnp.exp(-ga))
            silu = ga * sg
            dg = (dm * u * (sg * (1.0 + ga * (1.0 - sg)))).astype(bf16)
            du = (dm * silu).astype(bf16)
            total = total + nt(dg, pair(l, 2 * t)) + nt(du, pair(l, 12 + 2 * t))
            wd[t] = tn(mid[l, t], dz).astype(bf16)
            gw = nn(bT, dg).astype(bf16)
            land[l, 2 * t] = gw[:, 0:128].reshape(8, R, 128)
            land[l, 2 * t + 1] = gw[:, 128:256].reshape(8, R, 128)
            gw = nn(bT, du).astype(bf16)
            land[l, 12 + 2 * t] = gw[:, 0:128].reshape(8, R, 128)
            land[l, 13 + 2 * t] = gw[:, 128:256].reshape(8, R, 128)
            return total

        total = lax.fori_loop(0, 6, ffn, jnp.zeros((128, PD), f32))
        scatter_down(l)
        g_sib(l, 0).start()
        if l < LAYERS - 1:
            g_step(l + 1, 1)
        dh1, dgain_ffn = norm_back(h1s[l], g, unspread(total), gain[l, 1:2, 0:D])
        zpad[:, 0:D] = dh1.astype(bf16)
        do = nt(zpad[...], units(l, 36, 5)).astype(bf16)
        go = nn(mixp[l].T, zpad[...]).astype(bf16)
        for t in range(4):
            land[l, 36 + t] = go[:, 128 * t:128 * t + 128].reshape(8, R, 128)
        go4[...] = go[:, 512:640]
        for j in range(HEADS):
            part = nn(do, e2[:, 128 * j:128 * j + 128]).astype(bf16)
            gidx = j % 3
            doc[j // 3, 64 * gidx:64 * gidx + 64, 0:128] = part[0:64]
            doc[j // 3, 64 * gidx:64 * gidx + 64, 128:256] = part[64:128]

        def head(s):
            qcat = qc[l, s]
            qh = qcat[:, 128:256]
            qT = qcat.astype(f32).T.astype(bf16)
            qhT = qT[128:256]
            docat = doc[s]
            doh = docat[:, 128:256]
            doT = docat.astype(f32).T
            doTb = doT.astype(bf16)
            dohT = doTb[128:256]
            dl = jnp.sum(oT[l, s, 0:64, :] * doT[64:128, :], axis=0, keepdims=True)
            dh = jnp.sum(oT[l, s, 64:128, :] * doT[192:256, :], axis=0, keepdims=True)
            lsl = lse[l, s, 0:1, :]
            lsh = lse[l, s, 1:2, :]
            own = kvl[l, c, s, 1]
            pe = jnp.exp(nn(own, qhT) + tri - lsh)
            dse = (pe * (nn(own, dohT) - dh)).astype(bf16)
            dxe = nn(dse, qh) + nn(pe.astype(bf16), doh)
            acc1[...] = tn(own, dse)
            acc2[...] = jnp.zeros((256, 192), f32)

            def chunk(j):
                tlo, x2, m = tiles(l, s, j)
                at = pl.ds(pl.multiple_of(256 * j, 256), 256)
                is_low = mk[at, :] > 0.5
                p1 = jnp.exp(nn(tlo, qhT) - lsh)
                p2 = jnp.exp(nn(x2, qT) + bias[at, :] - jnp.where(is_low, lsl, lsh))
                ds1 = (p1 * (nn(tlo, dohT) - dh)).astype(bf16)
                ds2 = (p2 * (nn(x2, doTb) - jnp.where(is_low, dl, dh))).astype(bf16)
                p1 = p1.astype(bf16)
                p2 = p2.astype(bf16)
                dx1 = nn(ds1, qh) + nn(p1, doh)
                dx2 = nn(ds2, qcat) + nn(p2, docat)
                mf = m.astype(f32)
                lo = dx1 + mf * dx2[:, 0:128]
                hi = (1.0 - mf) * dx2[:, 128:256]
                dkv[pl.ds(2 * j, 2), :, s, 0] = lo.astype(bf16).reshape(2, 2, 64, 128)
                dkv[pl.ds(2 * j, 2), :, s, 1] = hi.astype(bf16).reshape(2, 2, 64, 128)
                acc1[...] += tn(tlo, ds1)
                acc2[...] += tn(x2, ds2)

            each(chunk, 0, 4)
            dkv[i, k, s, 1] = dxe.astype(bf16)
            zero = jnp.zeros((64, 192), f32)
            tl = jnp.concatenate([acc2[0:64, :], zero], axis=0).T
            th = jnp.concatenate([acc2[128:192, :] + acc1[0:64, :], zero], axis=0).T
            scale = HEAD_DIM ** (-0.5)
            for gidx in range(3):
                dqz[3 * s + gidx, 0:64, :] = tl[64 * gidx:64 * gidx + 64] * scale
                dqz[3 * s + gidx, 64:128, :] = th[64 * gidx:64 * gidx + 64] * scale

        each(head, 0, KV_HEADS)
        dk_sib(l).start()
        g_step(l, 0)
        dk_sib(l).wait()
        dk_sum(l)
        each(lambda m: dk_chip(l, m).start())

        rot = []
        for j in range(HEADS):
            x = dqz[j]
            rot.append(x * cos_q - swap(x) * sin_q)
        dq = [pltpu.roll(rot[0], 64, axis=1).astype(bf16)]
        for t in range(1, 5):
            dq.append((rot[2 * t - 1] + pltpu.roll(rot[2 * t], 64, axis=1)).astype(bf16))
        dq = jnp.concatenate(dq, axis=1)
        aT = apad[l].T

        each(lambda m: dk_chip(l, m).wait())
        dkv_in = []
        for s in range(KV_HEADS):
            x = dkv[i, k, s].astype(f32)
            for m in range(7):
                x = x + dkr2[l, m, s].astype(f32)
            x = x.reshape(128, 128)
            dkv_in.append((x * cos_kv - swap(x) * sin_kv).astype(bf16))
        dkv_in = jnp.concatenate(dkv_in, axis=1)
        da = nt(dq, units(l, 40, 5)) + nt(dkv_in, units(l, 45, 3))
        gq = nn(aT, dq).astype(bf16)
        land[l, 40] = (gq[:, 0:128] + go4[...]).reshape(8, R, 128)
        for t in range(1, 5):
            land[l, 40 + t] = gq[:, 128 * t:128 * t + 128].reshape(8, R, 128)
        gkv = nn(aT, dkv_in).astype(bf16)
        for t in range(3):
            land[l, 45 + t] = gkv[:, 128 * t:128 * t + 128].reshape(8, R, 128)
        dh, dgain_attn = norm_back(hs[l], dh1, unspread(da), gain[l, 0:1, 0:D])
        rows = jnp.concatenate([dgain_attn, dgain_ffn, jnp.zeros((6, D), f32)], axis=0)
        rows = jnp.concatenate([rows, jnp.zeros((8, PD - D), f32)], axis=1)
        for s in range(ND):
            part = (pltpu.roll(rows, PD - 72 * s, axis=1) if s else rows)[:, 0:128]
            keep = land[l, 36, s].astype(f32)[0:72, :]
            land[l, 36, s] = jnp.concatenate([keep, part], axis=0).astype(bf16)
        g_sib(l, 1).start()
        return dh

    h = hid[...].astype(f32)
    h = forward(0, h)
    h = forward(1, h)
    hout[...] = h.astype(bf16)
    g = backward(1, gout[...].astype(f32))
    g = backward(0, g)
    ghid[...] = g
    g_step(0, 1)
    g_total(1, 0)
    g_total(1, 1)
    g_total(0, 0)
    g_total(0, 1)

    def dp_copy(m):
        return rc(dpb.at[dplus(m)], dpr.at[m - 1], dp_s + m - 1, {"dp": dplus(m)})
    each(lambda m: dp_copy(m).start())
    each(lambda m: dp_copy(m).wait())
    for l in range(LAYERS):
        for s in range(3):
            total = dpb[d, l, s].astype(f32)
            for m in range(7):
                total = total + dpr[m, l, s].astype(f32)
            fin[c, l, s] = total.astype(bf16)
    own = fin.at[c]
    rc(own, own, ag_s[1] + 7, sib).start()
    each(lambda m: rc(own, own, ag_s[0] + m - 1, chip(iplus(m))).start())
    def pass_on(m):
        ref = fin.at[iminus(m) * 2 + k]
        rc(ref, ref, ag_s[0] + m - 1, chip(iplus(m))).wait_recv()
        rc(ref, ref, ag_s[1] + m - 1, sib).start()
    each(pass_on)
    other = fin.at[i * 2 + 1 - k]
    rc(other, other, ag_s[1] + 7, sib).wait_recv()
    rc(own, own, ag_s[1] + 7, sib).wait_send()
    def done(m):
        ref = fin.at[iminus(m) * 2 + 1 - k]
        rc(ref, ref, ag_s[1] + m - 1, sib).wait_recv()
        mine = fin.at[iminus(m) * 2 + k]
        rc(mine, mine, ag_s[1] + m - 1, sib).wait_send()
        rc(own, own, ag_s[0] + m - 1, chip(iplus(m))).wait_send()
    each(done)

    for l in range(LAYERS):
        for cc in range(NC):
            ii, kk = cc // 2, cc % 2
            for s, u in enumerate((16 * kk + 2 * ii, 16 * kk + 2 * ii + 1, 32 + 8 * kk + ii)):
                val = fin[cc, l, s].astype(f32)
                if u < 12:
                    ggate[l, :, 128 * u:128 * u + 128] = val[0:72]
                elif u < 24:
                    gup[l, :, 128 * (u - 12):128 * (u - 12) + 128] = val[0:72]
                elif u < 36:
                    at = slice(16 * (u - 24), 16 * (u - 24) + 16)
                    for lt in range(4):
                        gdown[l, at, 128 * lt:128 * lt + 128] = val[16 * lt:16 * lt + 16]
                    gdown[l, at, 512:576] = val[64:80, 0:64]
                else:
                    gattn[l, :, 128 * (u - 36):128 * (u - 36) + 128] = val[0:72]
                    if u == 36:
                        ggains[l] = val[72:80]


def body(
    hidden_in, positions, attn_gain, w_query, w_key, w_value, w_output, ffn_gain, w_gate, w_up, w_down, grad_out
):
    own = lax.dynamic_slice_in_dim(positions, lax.axis_index("ctx") * ROWS, ROWS)
    half = HEAD_DIM // 2
    freq = jnp.exp(-jnp.log(rope_base) * (2.0 * jnp.arange(half, dtype=f32) / HEAD_DIM))
    angle = own.astype(f32)[:, None] * jnp.tile(freq, 4)[None, :]
    sign = jnp.tile(jnp.where(jnp.arange(HEAD_DIM) < half, -1.0, 1.0), 2).astype(f32)
    cosm, sinm = jnp.cos(angle), jnp.sin(angle) * sign[None, :]
    low = (positions.reshape(NC, ROWS)[:, 0] <= own[0]).astype(bf16)
    mlow = jnp.broadcast_to(low[:, None, None], (NC, 64, 128)).reshape(NC * 64, 128)
    spread = np.zeros((D, PD), np.float32)
    for s in range(ND):
        spread[72 * s + np.arange(72), R * s + np.arange(72)] = 1
    heads = np.zeros((PD, 128 * HEADS), np.float32)
    for t in range(D):
        heads[R * (t // 72) + t % 72, 128 * (t // 64) + 64 + t % 64] = 1
    gains = jnp.stack([attn_gain, ffn_gain], axis=1).astype(f32)
    gains = jnp.pad(gains, ((0, 0), (0, 6), (0, 56)))
    kv = jnp.stack(
        [w_key.reshape(LAYERS, 72, KV_HEADS, HEAD_DIM), w_value.reshape(LAYERS, 72, KV_HEADS, HEAD_DIM)], axis=3
    ).reshape(LAYERS, 72, 2 * KV_HEADS * HEAD_DIM)
    wattn = jnp.concatenate([w_output, w_query, kv], axis=2)
    outs = pl.pallas_call(
        kernel,
        out_shape=(
            jax.ShapeDtypeStruct((ROWS, D), bf16),
            jax.ShapeDtypeStruct((ROWS, D), f32),
            jax.ShapeDtypeStruct((LAYERS, 8, 128), f32),
            jax.ShapeDtypeStruct((LAYERS, 72, FF), f32),
            jax.ShapeDtypeStruct((LAYERS, 72, FF), f32),
            jax.ShapeDtypeStruct((LAYERS, 192, D), f32),
            jax.ShapeDtypeStruct((LAYERS, 72, FF), f32),
        ),
        in_specs=[pl.BlockSpec(memory_space=pltpu.VMEM)] * 12,
        out_specs=tuple([pl.BlockSpec(memory_space=pltpu.VMEM)] * 7),
        scratch_shapes=[
            pltpu.VMEM((LAYERS, 48, ND, R, 128), bf16),
            pltpu.VMEM((6, 256, PD), bf16),
            pltpu.VMEM((LAYERS, NC, KV_HEADS, 2, 64, 128), bf16),
            pltpu.VMEM((NCHIP, 2, KV_HEADS, 2, 64, 128), bf16),
            pltpu.VMEM((LAYERS, NCHIP, KV_HEADS, 2, 64, 128), bf16),
            pltpu.VMEM((LAYERS, 7, KV_HEADS, 2, 64, 128), bf16),
            pltpu.VMEM((LAYERS, 24, ND, R, 128), bf16),
            pltpu.VMEM((LAYERS, 7, 3, ND, R, 128), bf16),
            pltpu.VMEM((ND, LAYERS, 3, R, 128), bf16),
            pltpu.VMEM((7, LAYERS, 3, R, 128), bf16),
            pltpu.VMEM((NC, LAYERS, 3, R, 128), bf16),
            pltpu.VMEM((LAYERS, 6, 128, 256), bf16),
            pltpu.VMEM((LAYERS, 128, D), f32),
            pltpu.VMEM((LAYERS, 128, D), f32),
            pltpu.VMEM((LAYERS, 128, PD), bf16),
            pltpu.VMEM((LAYERS, 128, PD), bf16),
            pltpu.VMEM((LAYERS, 128, PD), bf16),
            pltpu.VMEM((LAYERS, KV_HEADS, 192, 256), bf16),
            pltpu.VMEM((KV_HEADS, 192, 256), bf16),
            pltpu.VMEM((LAYERS, KV_HEADS, 128, 192), f32),
            pltpu.VMEM((LAYERS, KV_HEADS, 8, 192), f32),
            pltpu.VMEM((HEADS, 128, 128), bf16),
            pltpu.VMEM((HEADS, 128, 128), f32),
            pltpu.VMEM((1024, 256), f32),
            pltpu.VMEM((1024, 256), f32),
            pltpu.VMEM((1024, 192), f32),
            pltpu.VMEM((1024, 192), f32),
            pltpu.VMEM((128, PD), bf16),
            pltpu.VMEM((LAYERS, 8, PD), f32),
            pltpu.VMEM((128, 192), f32),
            pltpu.VMEM((256, 192), f32),
            pltpu.VMEM((PD, 128), bf16),
            pltpu.SemaphoreType.DMA((192,)),
            pltpu.SemaphoreType.DMA((192,)),
        ],
        compiler_params=pltpu.CompilerParams(
            collective_id=0, has_side_effects=True, vmem_limit_bytes=63 * 1024 * 1024
        ),
    )(
        hidden_in, grad_out, cosm, sinm, mlow, jnp.asarray(spread, bf16), jnp.asarray(heads, bf16), gains,
        w_gate, w_up, w_down, wattn,
    )
    hout, ghid, ggains, ggate, gup, gdown, gattn = outs
    gkv = gattn[:, :, 2 * D:].reshape(LAYERS, 72, KV_HEADS, 2, HEAD_DIM)
    return (
        hout,
        ghid,
        ggains[:, 0, 0:72],
        gattn[:, :, D:2 * D],
        gkv[:, :, :, 0].reshape(LAYERS, 72, KV_HEADS * HEAD_DIM),
        gkv[:, :, :, 1].reshape(LAYERS, 72, KV_HEADS * HEAD_DIM),
        gattn[:, :, 0:D],
        ggains[:, 1, 0:72],
        ggate,
        gup,
        gdown,
    )


def solution(mesh):
    placed = (
        P(("dp", "ctx"), None),
        P("dp"),
        P(None, "dp"),
        P(None, "dp", None),
        P(None, "dp", None),
        P(None, "dp", None),
        P(None, "dp", None),
        P(None, "dp"),
        P(None, "dp", None),
        P(None, "dp", None),
        P(None, "dp", None),
        P(("dp", "ctx"), None),
    )
    out = (
        P(("dp", "ctx"), None),
        P(("dp", "ctx"), None),
        P(None, "dp"),
        P(None, "dp", None),
        P(None, "dp", None),
        P(None, "dp", None),
        P(None, "dp", None),
        P(None, "dp"),
        P(None, "dp", None),
        P(None, "dp", None),
        P(None, "dp", None),
    )
    return jax.shard_map(body, mesh=mesh, in_specs=placed, out_specs=out, check_vma=False)
```

```python
import jax
import jax.numpy as jnp
import numpy as np
from jax import lax
from jax.experimental import pallas as pl
from jax.experimental.pallas import tpu as pltpu
from jax.sharding import PartitionSpec as P

D = 576
HEADS = 9
KV_HEADS = 3
HEAD_DIM = 64
FF = 1536
LAYERS = 2
ROWS = 128
ND = 8
NC = 16
NCHIP = 8
R = 80
PD = 640
MESH = pl.DeviceIdType.MESH
bf16 = jnp.bfloat16
f32 = jnp.float32
NEG = -1e30
eps_norm = 1e-05
rope_base = 100000.0


def nn(a, b):
    return lax.dot_general(a, b, (((1,), (0,)), ((), ())), preferred_element_type=f32)


def nt(a, b):
    return lax.dot_general(a, b, (((1,), (1,)), ((), ())), preferred_element_type=f32)


def tn(a, b):
    return lax.dot_general(a, b, (((0,), (0,)), ((), ())), preferred_element_type=f32)


class Move:
    def __init__(self, make, src, dst, inc, s, dev):
        self.out = lambda: make(src, dst, s, dev)
        self.inc = lambda: make(inc, inc, s, dev)

    def start(self):
        self.out().start()

    def recv(self):
        self.inc().wait_recv()

    def sent(self):
        self.out().wait_send()


def kernel(
    hid, gout, cosm, sinm, mlow, e1, e2, gains, wgate, wup, wdown, wattn,
    hout, ghid, ggains, ggate, gup, gdown, gattn,
    land, wd, kvl, dkv, dkr0, dkr1,
    rs0, r1e, rz, r2e, r1l, r2l, fine, finl,
    mid, hs, h1s, apad, bpad, mixp, qc, doc, oT, lse, oz, dqz,
    s1, s2, bias, mk, zpad, gain, acc1, acc2, go4,
    send, recv,
):
    d = lax.axis_index("dp")
    c = lax.axis_index("ctx")
    k, y = lax.rem(c, 2), lax.rem(c // 2, 4)
    x, zl = lax.rem(d, 4), d // 4
    i = c // 2
    sib = {"ctx": i * 2 + 1 - k}
    count = [0]

    def dplus(m):
        return lax.rem(d + m, ND)

    def dminus(m):
        return lax.rem(d - m + ND, ND)

    def iplus(m):
        return lax.rem(i + m, NCHIP)

    def iminus(m):
        return lax.rem(i - m + NCHIP, NCHIP)

    def shard(m):
        return {"dp": dplus(m)}

    def chip(m):
        return {"ctx": iplus(m) * 2 + k}

    def near(at, o):
        return lax.rem(at + o + 4, 4)

    def Y(o):
        return {"ctx": ((i // 4) * 4 + near(y, o)) * 2 + k}

    def rc(src, dst, s, to):
        return pltpu.make_async_remote_copy(
            src_ref=src, dst_ref=dst, send_sem=send.at[s], recv_sem=recv.at[s],
            device_id=to, device_id_type=MESH,
        )

    def sems(n):
        count[0] += n
        return count[0] - n

    def move(src, dst, inc, to, s=None):
        return Move(rc, src, dst, inc, sems(1) if s is None else s, to)

    def starts(*moves):
        for m in moves:
            m.start()

    def recvs(*moves):
        for m in moves:
            m.recv()

    def sents(*moves):
        for m in moves:
            m.sent()

    def each(f, lo=1, hi=8):
        def step(m, carry):
            f(m)
            return carry
        lax.fori_loop(lo, hi, step, 0)

    def put(l, j, val, last=None, k=k):
        last = jnp.zeros((8, 128), f32) if last is None else last
        land[l, k, j, d] = jnp.concatenate([val.astype(f32), last], axis=0).astype(bf16)

    def column(t):
        return pl.ds(pl.multiple_of(128 * t, 128), 128)

    def pack_attn(l):
        if l == 0:
            for t in range(12):
                put(l, 18 + t % 6, wattn[l, :, 128 * t:128 * t + 128], gains[l], t // 6)
        else:
            put(l, 18 + y, wattn[l, :, column(6 * k + y)], gains[l])
            put(l, 22, wattn[l, :, column(6 * k + 4)])
            put(l, 23, wattn[l, :, column(6 * k + 5)])

    def pack_ffn(l):
        @pl.when(y < 2)
        def _():
            for r in range(3):
                put(l, 3 * y + r, wgate[l, :, column(6 * k + 3 * y + r)])

        @pl.when(y >= 2)
        def _():
            for r in range(3):
                put(l, 3 * y + r, wup[l, :, column(6 * k + 3 * (y - 2) + r)])

        for g in range(6):
            val = wdown[l, pl.ds(pl.multiple_of(16 * (6 * k + g), 16), 16), :]
            val = jnp.concatenate([val.astype(f32), jnp.zeros((16, 64), f32)], axis=1).astype(bf16)
            for lt in range(5):
                land[l, k, 12 + g, d, 16 * lt:16 * lt + 16, :] = val[:, 128 * lt:128 * lt + 128]

    class Weights:
        def __init__(self, l, shared, direct):
            self.shared = shared is not None
            db, nd = direct

            def straight(slot):
                return land.at[l, k, pl.ds(db, nd), slot]

            self.parts = [(straight, sems(7))]
            here, there = land.at[l, k, pl.ds(db, nd)], land.at[l, 1 - k, pl.ds(db, nd)]
            self.u = []
            if not self.shared:
                self.v = None
                self.base = sems(7)
                self.slot = lambda k_, slot: land.at[l, k_, pl.ds(db, nd), slot]
                return
            sb, ns = shared
            self.parts.append((lambda slot: land.at[l, k, pl.ds(sb + ns * y, ns), slot], sems(7)))
            self.v = [move(here, here, there, sib)]

            def block(y_, k_=k, half=None):
                ref = land.at[l, k_, pl.ds(sb + ns * y_, ns)]
                return ref if half is None else ref.at[:, pl.ds(4 * half, 4)]

            yp, ym, y2 = near(y, 1), near(y, -1), near(y, 2)
            self.u = [
                move(block(y), block(y), block(ym), Y(1)), move(block(y), block(y), block(yp), Y(-1)),
                move(block(ym, half=0), block(ym, half=0), block(y2, half=0), Y(1)),
                move(block(yp, half=1), block(yp, half=1), block(y2, half=1), Y(-1)),
            ]
            self.v += [move(block(y_), block(y_), block(y_, 1 - k), sib) for y_ in (y, ym, yp, y2)]

        def one(self, part):
            ref, s = self.parts[part]
            each(lambda m: rc(ref(d), ref(d), s + m - 1, shard(m)).start())

        def two(self):
            def go(m):
                for ref, s in self.parts:
                    own = ref(dminus(m))
                    rc(own, own, s + m - 1, shard(m)).wait_recv()
                    if not self.shared:
                        rc(own, own, self.base + m - 1, sib).start()
            each(go)
            if self.shared:
                starts(self.u[0], self.u[1], self.v[0], self.v[1])

        def three(self):
            recvs(self.u[0])
            starts(self.u[2], self.v[2])
            recvs(self.u[1])
            starts(self.u[3], self.v[3])

        def four(self):
            recvs(self.u[2], self.u[3])
            starts(self.v[4])

        def five(self):
            if self.shared:
                recvs(*self.v)
                sents(*self.u)
                sents(*self.v)

            def go(m):
                for ref, s in self.parts:
                    rc(ref(d), ref(d), s + m - 1, shard(m)).wait_send()
                if not self.shared:
                    got, gave = self.slot(1 - k, dminus(m)), self.slot(k, dminus(m))
                    rc(got, got, self.base + m - 1, sib).wait_recv()
                    rc(gave, gave, self.base + m - 1, sib).wait_send()
            each(go)

    class Keys:
        def __init__(self, l):
            self.l, self.a, self.b = l, sems(7), sems(7)
            own = kvl.at[l, i, k]
            self.s = move(own, own, kvl.at[l, i, 1 - k], sib)

        def one(self):
            own = kvl.at[self.l, i, k]
            each(lambda m: rc(own, own, self.a + m - 1, chip(m)).start())
            starts(self.s)

        def two(self):
            def go(m):
                ref = kvl.at[self.l, iminus(m), k]
                rc(ref, ref, self.a + m - 1, chip(m)).wait_recv()
                rc(ref, ref, self.b + m - 1, sib).start()
            each(go)

        def three(self):
            recvs(self.s)
            sents(self.s)

            def go(m):
                got, gave, own = kvl.at[self.l, iminus(m), 1 - k], kvl.at[self.l, iminus(m), k], kvl.at[self.l, i, k]
                rc(got, got, self.b + m - 1, sib).wait_recv()
                rc(gave, gave, self.b + m - 1, sib).wait_send()
                rc(own, own, self.a + m - 1, chip(m)).wait_send()
            each(go)

    class KeyGrads:
        def __init__(self, l):
            self.l = l
            self.s = move(dkv.at[:, 1 - k], dkr0.at[l], dkr0.at[l], sib)
            self.a = sems(7)

        def out(self, m):
            return rc(dkv.at[iplus(m), k], dkr1.at[self.l, m - 1], self.a + m - 1, chip(m))

        def one(self):
            starts(self.s)

        def two(self):
            recvs(self.s)

            def go(m):
                j = iplus(m)
                for h in range(KV_HEADS):
                    total = dkv[j, k, h].astype(f32) + dkr0[self.l, j, h].astype(f32)
                    dkv[j, k, h] = total.astype(bf16)
                self.out(m).start()

            each(go)

        def three(self):
            each(lambda m: self.out(m).wait())
            sents(self.s)

        def total(self, h):
            val = dkv[i, k, h].astype(f32) + dkr0[self.l, i, h].astype(f32)
            for m in range(7):
                val = val + dkr1[self.l, m, h].astype(f32)
            return val

    class Grads:
        def __init__(self, l, early):
            self.l, self.early = l, early
            self.base, self.n = (0, 16) if early else (16, 8)
            there = rs0.at[l, pl.ds(self.base, self.n)]
            self.s = move(land.at[l, 1 - k, pl.ds(self.base, self.n)], there, there, sib)
            self.r1, self.r2, self.fin = (r1e, r2e, fine) if early else (r1l, r2l, finl)
            self.a, self.b, self.c, self.v, self.z = sems(7), sems(7), sems(7), sems(7), sems(1)
            own = self.fin.at[l, i, k]
            self.t = move(own, own, self.fin.at[l, i, 1 - k], sib)

        def out1(self, m):
            l = self.l
            if self.early:
                q, o = lax.rem(m - 1, 2), (m - 1) // 2
                x_ = near(x, o + 1)
                src, to = land.at[l, k, pl.ds(0, 16), 4 * q + x_], {"dp": zl * 4 + x_}
                return rc(src, r1e.at[l, q, o], self.a + m - 1, to)
            return rc(land.at[l, k, 16 + iplus(m)], r1l.at[l, m - 1], self.a + m - 1, chip(m))

        def outz(self):
            src = land.at[self.l, k, pl.ds(0, 16), 4 * (1 - zl) + x]
            return rc(src, rz.at[self.l], self.z, {"dp": 4 * (1 - zl) + x})

        def out2(self, m):
            l = self.l
            if self.early:
                src, to = land.at[l, k, pl.ds(2 * iplus(m), 2), d], chip(m)
            else:
                src, to = land.at[l, k, 16 + i, dplus(m)], shard(m)
            return rc(src, self.r2.at[l, m - 1], self.b + m - 1, to)

        def zero(self):
            starts(self.s)

        def one(self):
            recvs(self.s)
            l = self.l

            def go(u):
                total = land[l, k, self.base + u].astype(f32) + rs0[l, self.base + u].astype(f32)
                land[l, k, self.base + u] = total.astype(bf16)

            each(go, 0, self.n)

        def send(self):
            each(lambda m: self.out1(m).start(), 1, 7 if self.early else 8)

        def two(self):
            each(lambda m: self.out1(m).wait(), 1, 7 if self.early else 8)
            l = self.l
            if self.early:
                def go(u):
                    for q in range(2):
                        total = land[l, k, u, 4 * q + x].astype(f32)
                        for o in range(3):
                            total = total + r1e[l, q, o, u].astype(f32)
                        land[l, k, u, 4 * q + x] = total.astype(bf16)

                each(go, 0, 16)
                self.outz().start()
            else:
                def go(u):
                    total = land[l, k, 16 + i, u].astype(f32)
                    for m in range(7):
                        total = total + r1l[l, m, u].astype(f32)
                    land[l, k, 16 + i, u] = total.astype(bf16)

                each(go, 0, 8)
                each(lambda m: self.out2(m).start())

        def pair(self):
            self.outz().wait()
            l = self.l

            def go(u):
                land[l, k, u, d] = (land[l, k, u, d].astype(f32) + rz[l, u].astype(f32)).astype(bf16)

            each(go, 0, 16)
            each(lambda m: self.out2(m).start())

        def three(self):
            each(lambda m: self.out2(m).wait())
            l = self.l
            for u in range(2 if self.early else 1):
                total = (land[l, k, 2 * i + u, d] if self.early else land[l, k, 16 + i, d]).astype(f32)
                for m in range(7):
                    total = total + (self.r2[l, m, u] if self.early else self.r2[l, m]).astype(f32)
                self.fin[l, i, k, u] = total.astype(bf16)
            own = self.fin.at[l, i, k]
            each(lambda m: rc(own, own, self.c + m - 1, chip(m)).start())
            starts(self.t)

        def four(self):
            def go(m):
                ref = self.fin.at[self.l, iminus(m), k]
                rc(ref, ref, self.c + m - 1, chip(m)).wait_recv()
                rc(ref, ref, self.v + m - 1, sib).start()
            each(go)

        def five(self):
            l = self.l
            recvs(self.t)
            sents(self.t, self.s)

            def go(m):
                got, gave = self.fin.at[l, iminus(m), 1 - k], self.fin.at[l, iminus(m), k]
                own = self.fin.at[l, i, k]
                rc(got, got, self.v + m - 1, sib).wait_recv()
                rc(gave, gave, self.v + m - 1, sib).wait_send()
                rc(own, own, self.c + m - 1, chip(m)).wait_send()
            each(go)
            for cc in range(NC):
                i_, k_ = cc // 2, cc % 2
                for q, j in enumerate((2 * i_, 2 * i_ + 1) if self.early else (16 + i_,)):
                    val = self.fin[l, i_, k_, q].astype(f32)
                    kind, t = j // 6, 6 * k_ + j % 6
                    cols = slice(128 * t, 128 * t + 128)
                    if kind == 0:
                        ggate[l, :, cols] = val[0:72]
                    elif kind == 1:
                        gup[l, :, cols] = val[0:72]
                    elif kind == 2:
                        at = slice(16 * t, 16 * t + 16)
                        for lt in range(4):
                            gdown[l, at, 128 * lt:128 * lt + 128] = val[16 * lt:16 * lt + 16]
                        gdown[l, at, 512:576] = val[64:80, 0:64]
                    else:
                        gattn[l, :, cols] = val[0:72]
                        if t == 0:
                            ggains[l] = val[72:80]

    weights = {
        (0, "A"): Weights(0, None, (18, 6)), (0, "F"): Weights(0, (0, 3), (12, 6)),
        (1, "A"): Weights(1, (18, 1), (22, 2)), (1, "F"): Weights(1, (0, 3), (12, 6)),
    }
    keys = [Keys(l) for l in range(LAYERS)]
    key_grads = [KeyGrads(l) for l in range(LAYERS)]
    grads = {(l, e): Grads(l, e) for l in range(LAYERS) for e in (True, False)}

    barrier = pltpu.get_barrier_semaphore()

    def hello(m):
        pl.semaphore_signal(barrier, inc=1, device_id=shard(m), device_id_type=MESH)
        pl.semaphore_signal(barrier, inc=1, device_id=chip(m), device_id_type=MESH)

    each(hello)
    pl.semaphore_signal(barrier, inc=1, device_id=sib, device_id_type=MESH)
    pack_attn(0)
    pl.semaphore_wait(barrier, 15)
    weights[0, "A"].one(0)
    pack_ffn(0)
    weights[0, "F"].one(0)
    pack_attn(1)
    pack_ffn(1)

    lane = lax.broadcasted_iota(jnp.int32, (128, 128), 1)
    low_half = lane < 64
    first_quarter = lax.rem(lane, 64) < 32
    cos_q = cosm[...]
    sin_q = sinm[...]
    cos_kv = jnp.where(low_half, cos_q, 1.0)
    sin_kv = jnp.where(low_half, sin_q, 0.0)

    def swap(x):
        return jnp.where(first_quarter, pltpu.roll(x, 96, axis=1), pltpu.roll(x, 32, axis=1))

    row = lax.broadcasted_iota(jnp.int32, (1024, 192), 0) - 64 * c
    col = lax.rem(lax.broadcasted_iota(jnp.int32, (1024, 192), 1), 64)
    bias[...] = jnp.where((row > col) & (row < 64), NEG, 0.0).astype(bf16)
    mk[...] = jnp.concatenate([mlow[...], mlow[:, 0:64]], axis=1).astype(f32)
    row = lax.broadcasted_iota(jnp.int32, (64, 192), 0)
    col = lax.rem(lax.broadcasted_iota(jnp.int32, (64, 192), 1), 64)
    tri = jnp.where(row > col, NEG, 0.0)
    zpad[...] = jnp.zeros((128, PD), bf16)

    def unit(l, u):
        return land[l, lax.rem(u, 12) // 6, 6 * (u // 12) + lax.rem(u, 6)].reshape(PD, 128)

    def pair(l, u):
        return jnp.concatenate([unit(l, u), unit(l, u + 1)], axis=1)

    def units(l, u, n):
        return jnp.concatenate([unit(l, u + j) for j in range(n)], axis=1)

    def norm_scale(h):
        return lax.rsqrt(jnp.mean(h * h, axis=-1, keepdims=True) + eps_norm)

    def spread(x):
        return nn(x.astype(bf16), e1[...]).astype(bf16)

    def unspread(x):
        hi = x.astype(bf16)
        lo = (x - hi.astype(f32)).astype(bf16)
        return nt(hi, e1[...]) + nt(lo, e1[...])

    def set_unit(l, u, val):
        land[l, lax.rem(u, 12) // 6, 6 * (u // 12) + lax.rem(u, 6)] = val.reshape(8, R, 128)

    def load_gains(l):
        total = jnp.zeros((8, PD), f32)
        for s in range(ND):
            part = land[l, 0, 18, s].astype(f32)[72:80, :]
            wide = jnp.concatenate([part, jnp.zeros((8, PD - 128), f32)], axis=1)
            total = total + (pltpu.roll(wide, 72 * s, axis=1) if s else wide)
        gain[l] = total

    def regroup_down(l):
        def go(j):
            src = lax.rem(j, 12)
            for lt in range(5):
                wd[j // 16, pl.ds(pl.multiple_of(lax.rem(j, 16) * 16, 16), 16), 128 * lt:128 * lt + 128] = land[
                    l, src // 6, 12 + lax.rem(src, 6), j // 12, 16 * lt:16 * lt + 16, :
                ]
        each(go, 0, 96)

    def scatter_down(l):
        def go(j):
            src = lax.rem(j, 12)
            for lt in range(5):
                land[l, src // 6, 12 + lax.rem(src, 6), j // 12, 16 * lt:16 * lt + 16, :] = wd[
                    j // 16, pl.ds(pl.multiple_of(lax.rem(j, 16) * 16, 16), 16), 128 * lt:128 * lt + 128
                ]
        each(go, 0, 96)

    def tiles(l, h, j):
        tlo = kvl[l, pl.ds(2 * j, 2), :, h, 0].reshape(256, 128)
        thi = kvl[l, pl.ds(2 * j, 2), :, h, 1].reshape(256, 128)
        m = mlow[pl.ds(pl.multiple_of(256 * j, 256), 256), :]
        x2 = jnp.concatenate([tlo * m, thi * (1 - m)], axis=1)
        return tlo, x2, m

    def swiglu_parts(l, t, x):
        g = nn(x, pair(l, 2 * t))
        u = nn(x, pair(l, 12 + 2 * t))
        return g, u

    def forward(l, h):
        hs[l] = h
        if l == 0:
            weights[0, "A"].two()
        weights[l, "A"].five()
        load_gains(l)
        apad[l] = spread(h * norm_scale(h) * gain[l, 0:1, 0:D])
        a = apad[l]
        for s in range(KV_HEADS):
            kv = nn(a, unit(l, 45 + s))
            kv = kv * cos_kv + swap(kv) * sin_kv
            kvl[l, i, k, s] = kv.astype(bf16).reshape(2, 64, 128)
        keys[l].one()
        if l == 0:
            weights[0, "F"].one(1)
        else:
            weights[1, "F"].two()
        for t in range(5):
            q = nn(a, unit(l, 40 + t))
            q = (q * cos_q + swap(q) * sin_q) * HEAD_DIM ** (-0.5)
            for j in ((2 * t - 1, 2 * t) if t else (0,)):
                part = q if j % 2 else pltpu.roll(q, 64, axis=1)
                part = jnp.where(low_half, part, 0.0).astype(bf16)
                g = j % 3
                qc[l, j // 3, 64 * g:64 * g + 64, 0:128] = part[0:64]
                qc[l, j // 3, 64 * g:64 * g + 64, 128:256] = part[64:128]
        keys[l].two()
        if l == 0:
            for name in ("A", "F"):
                weights[1, name].one(0)
                weights[1, name].one(1)
        keys[l].three()

        def head(s):
            qcat = qc[l, s]
            qT = qcat.astype(f32).T.astype(bf16)
            qhT = qT[128:256]
            top_own = kvl[l, i, k, s, 1]
            se = nn(top_own, qhT) + tri

            def scores(j, carry):
                ml, mh = carry
                tlo, x2, _ = tiles(l, s, j)
                at = pl.ds(pl.multiple_of(256 * j, 256), 256)
                a1 = nn(tlo, qhT)
                a2 = nn(x2, qT) + bias[at, :].astype(f32)
                s1[at, 0:192] = a1
                s2[at, 0:192] = a2
                is_low = mk[at, :] > 0.5
                ml = jnp.maximum(ml, jnp.max(jnp.where(is_low, a2, NEG), axis=0, keepdims=True))
                mh = jnp.maximum(
                    mh, jnp.max(jnp.maximum(a1, jnp.where(is_low, NEG, a2)), axis=0, keepdims=True)
                )
                return ml, mh

            ml, mh = lax.fori_loop(
                0, 4, scores,
                (jnp.full((1, 192), NEG, f32), jnp.max(se, axis=0, keepdims=True)),
            )
            pe = jnp.exp(se - mh)
            acc1[...] = tn(top_own, pe.astype(bf16))
            acc2[...] = jnp.zeros((256, 192), f32)

            def weigh(j, carry):
                ll, lh = carry
                tlo, x2, _ = tiles(l, s, j)
                at = pl.ds(pl.multiple_of(256 * j, 256), 256)
                is_low = mk[at, :] > 0.5
                p1 = jnp.exp(s1[at, 0:192] - mh)
                p2 = jnp.exp(s2[at, 0:192] - jnp.where(is_low, ml, mh))
                ll = ll + jnp.sum(jnp.where(is_low, p2, 0.0), axis=0, keepdims=True)
                lh = lh + jnp.sum(p1 + jnp.where(is_low, 0.0, p2), axis=0, keepdims=True)
                acc1[...] += tn(tlo, p1.astype(bf16))
                acc2[...] += tn(x2, p2.astype(bf16))
                return ll, lh

            ll, lh = lax.fori_loop(
                0, 4, weigh, (jnp.zeros((1, 192), f32), jnp.sum(pe, axis=0, keepdims=True))
            )
            olow = acc2[64:128, :] / ll
            ohigh = (acc2[192:256, :] + acc1[64:128, :]) / lh
            oT[l, s, 0:64, :] = olow
            oT[l, s, 64:128, :] = ohigh
            lse[l, s, 0:1, :] = ml + jnp.log(ll)
            lse[l, s, 1:2, :] = mh + jnp.log(lh)
            zero = jnp.zeros((64, 192), f32)
            tl = jnp.concatenate([zero, olow], axis=0).T.astype(bf16)
            th = jnp.concatenate([zero, ohigh], axis=0).T.astype(bf16)
            for g in range(3):
                oz[3 * s + g, 0:64, :] = tl[64 * g:64 * g + 64]
                oz[3 * s + g, 64:128, :] = th[64 * g:64 * g + 64]

            if l == 0:
                @pl.when(s == 0)
                def _():
                    weights[0, "F"].two()

                @pl.when(s == 1)
                def _():
                    weights[0, "F"].three()
            else:
                @pl.when(s == 1)
                def _():
                    weights[1, "F"].three()

        each(head, 0, KV_HEADS)
        mixp[l] = nt(jnp.concatenate([oz[j] for j in range(HEADS)], axis=1), e2[...]).astype(bf16)
        out = nn(mixp[l], units(l, 36, 5))
        h1 = h + out[:, 0:D]
        h1s[l] = h1
        bpad[l] = spread(h1 * norm_scale(h1) * gain[l, 1:2, 0:D])
        weights[l, "F"].four()
        weights[l, "F"].five()
        if l == 0:
            weights[1, "A"].two()
        regroup_down(l)

        def ffn(t, total):
            g, u = swiglu_parts(l, t, bpad[l])
            if l == LAYERS - 1:
                s1[pl.ds(pl.multiple_of(128 * t, 128), 128), :] = g
                s2[pl.ds(pl.multiple_of(128 * t, 128), 128), :] = u
            m = (g / (1.0 + jnp.exp(-g)) * u).astype(bf16)
            mid[l, t] = m
            if l == 0:
                @pl.when(t == 3)
                def _():
                    weights[1, "A"].three()

            return total + nn(m, wd[t])

        total = lax.fori_loop(0, 6, ffn, jnp.zeros((128, PD), f32))
        if l == 0:
            weights[1, "A"].four()
        return h1 + total[:, 0:D]

    def norm_back(h, g, dn, gain_row):
        r = norm_scale(h)
        xn = h * r
        cc = dn * gain_row
        return (
            g + r * (cc - xn * jnp.mean(cc * xn, axis=-1, keepdims=True)),
            jnp.sum(dn * xn, axis=0, keepdims=True),
        )

    def backward(l, g):
        zpad[:, 0:D] = g.astype(bf16)
        if l < LAYERS - 1:
            regroup_down(l)
        bT = bpad[l].T

        def ffn(t, total):
            dz = zpad[...]
            if l == LAYERS - 1:
                at = pl.ds(pl.multiple_of(128 * t, 128), 128)
                ga, u = s1[at, :], s2[at, :]
            else:
                ga, u = swiglu_parts(l, t, bpad[l])
            dm = nt(dz, wd[t])
            sg = 1.0 / (1.0 + jnp.exp(-ga))
            silu = ga * sg
            dg = (dm * u * (sg * (1.0 + ga * (1.0 - sg)))).astype(bf16)
            du = (dm * silu).astype(bf16)
            total = total + nt(dg, pair(l, 2 * t)) + nt(du, pair(l, 12 + 2 * t))
            wd[t] = tn(mid[l, t], dz).astype(bf16)
            gw = nn(bT, dg).astype(bf16)
            set_unit(l, 2 * t, gw[:, 0:128])
            set_unit(l, 2 * t + 1, gw[:, 128:256])
            gw = nn(bT, du).astype(bf16)
            set_unit(l, 12 + 2 * t, gw[:, 0:128])
            set_unit(l, 13 + 2 * t, gw[:, 128:256])
            return total

        total = lax.fori_loop(0, 6, ffn, jnp.zeros((128, PD), f32))
        scatter_down(l)
        grads[l, True].zero()
        if l < LAYERS - 1:
            grads[l + 1, True].two()
            grads[l + 1, False].one()
            grads[l + 1, False].send()
        dh1, dgain_ffn = norm_back(h1s[l], g, unspread(total), gain[l, 1:2, 0:D])
        zpad[:, 0:D] = dh1.astype(bf16)
        do = nt(zpad[...], units(l, 36, 5)).astype(bf16)
        go = nn(mixp[l].T, zpad[...]).astype(bf16)
        for t in range(4):
            set_unit(l, 36 + t, go[:, 128 * t:128 * t + 128])
        go4[...] = go[:, 512:640]
        for j in range(HEADS):
            part = nn(do, e2[:, 128 * j:128 * j + 128]).astype(bf16)
            gidx = j % 3
            doc[j // 3, 64 * gidx:64 * gidx + 64, 0:128] = part[0:64]
            doc[j // 3, 64 * gidx:64 * gidx + 64, 128:256] = part[64:128]

        def head(s):
            qcat = qc[l, s]
            qh = qcat[:, 128:256]
            qT = qcat.astype(f32).T.astype(bf16)
            qhT = qT[128:256]
            docat = doc[s]
            doh = docat[:, 128:256]
            doT = docat.astype(f32).T
            doTb = doT.astype(bf16)
            dohT = doTb[128:256]
            dl = jnp.sum(oT[l, s, 0:64, :] * doT[64:128, :], axis=0, keepdims=True)
            dh = jnp.sum(oT[l, s, 64:128, :] * doT[192:256, :], axis=0, keepdims=True)
            lsl = lse[l, s, 0:1, :]
            lsh = lse[l, s, 1:2, :]
            own = kvl[l, i, k, s, 1]
            pe = jnp.exp(nn(own, qhT) + tri - lsh)
            dse = (pe * (nn(own, dohT) - dh)).astype(bf16)
            dxe = nn(dse, qh) + nn(pe.astype(bf16), doh)
            acc1[...] = tn(own, dse)
            acc2[...] = jnp.zeros((256, 192), f32)

            def chunk(j):
                tlo, x2, m = tiles(l, s, j)
                at = pl.ds(pl.multiple_of(256 * j, 256), 256)
                is_low = mk[at, :] > 0.5
                p1 = jnp.exp(nn(tlo, qhT) - lsh)
                p2 = jnp.exp(nn(x2, qT) + bias[at, :].astype(f32) - jnp.where(is_low, lsl, lsh))
                ds1 = (p1 * (nn(tlo, dohT) - dh)).astype(bf16)
                ds2 = (p2 * (nn(x2, doTb) - jnp.where(is_low, dl, dh))).astype(bf16)
                p1 = p1.astype(bf16)
                p2 = p2.astype(bf16)
                dx1 = nn(ds1, qh) + nn(p1, doh)
                dx2 = nn(ds2, qcat) + nn(p2, docat)
                mf = m.astype(f32)
                lo = dx1 + mf * dx2[:, 0:128]
                hi = (1.0 - mf) * dx2[:, 128:256]
                dkv[pl.ds(2 * j, 2), :, s, 0] = lo.astype(bf16).reshape(2, 2, 64, 128)
                dkv[pl.ds(2 * j, 2), :, s, 1] = hi.astype(bf16).reshape(2, 2, 64, 128)
                acc1[...] += tn(tlo, ds1)
                acc2[...] += tn(x2, ds2)

            each(chunk, 0, 4)
            dkv[i, k, s, 1] = dxe.astype(bf16)
            zero = jnp.zeros((64, 192), f32)
            tl = jnp.concatenate([acc2[0:64, :], zero], axis=0).T
            th = jnp.concatenate([acc2[128:192, :] + acc1[0:64, :], zero], axis=0).T
            scale = HEAD_DIM ** (-0.5)
            for gidx in range(3):
                dqz[3 * s + gidx, 0:64, :] = tl[64 * gidx:64 * gidx + 64] * scale
                dqz[3 * s + gidx, 64:128, :] = th[64 * gidx:64 * gidx + 64] * scale

            @pl.when(s == 1)
            def _():
                grads[l, True].one()
                if l < LAYERS - 1:
                    grads[l + 1, True].pair()

        each(head, 0, KV_HEADS)
        kg = key_grads[l]
        kg.one()
        kg.two()
        grads[l, True].send()

        rot = []
        for j in range(HEADS):
            t = dqz[j]
            rot.append(t * cos_q - swap(t) * sin_q)
        dq = [pltpu.roll(rot[0], 64, axis=1).astype(bf16)]
        for t in range(1, 5):
            dq.append((rot[2 * t - 1] + pltpu.roll(rot[2 * t], 64, axis=1)).astype(bf16))
        dq = jnp.concatenate(dq, axis=1)
        aT = apad[l].T
        gq = nn(aT, dq).astype(bf16)
        if l < LAYERS - 1:
            grads[l + 1, True].three()
        kg.three()
        dkv_in = []
        for s in range(KV_HEADS):
            t = kg.total(s).reshape(128, 128)
            dkv_in.append((t * cos_kv - swap(t) * sin_kv).astype(bf16))
        dkv_in = jnp.concatenate(dkv_in, axis=1)
        da = nt(dq, units(l, 40, 5)) + nt(dkv_in, units(l, 45, 3))
        set_unit(l, 40, gq[:, 0:128] + go4[...])
        for t in range(1, 5):
            set_unit(l, 40 + t, gq[:, 128 * t:128 * t + 128])
        gkv = nn(aT, dkv_in).astype(bf16)
        for t in range(3):
            set_unit(l, 45 + t, gkv[:, 128 * t:128 * t + 128])
        dh, dgain_attn = norm_back(hs[l], dh1, unspread(da), gain[l, 0:1, 0:D])
        rows = jnp.concatenate([dgain_attn, dgain_ffn, jnp.zeros((6, D), f32)], axis=0)
        rows = jnp.concatenate([rows, jnp.zeros((8, PD - D), f32)], axis=1)
        for s in range(ND):
            part = (pltpu.roll(rows, PD - 72 * s, axis=1) if s else rows)[:, 0:128]
            keep = land[l, 0, 18, s].astype(f32)[0:72, :]
            land[l, 0, 18, s] = jnp.concatenate([keep, part], axis=0).astype(bf16)
        grads[l, False].zero()
        return dh

    h = hid[...].astype(f32)
    h = forward(0, h)
    h = forward(1, h)
    hout[...] = h.astype(bf16)
    g = backward(1, gout[...].astype(f32))
    g = backward(0, g)
    ghid[...] = g
    grads[1, False].two()
    grads[0, False].one()
    grads[0, False].send()
    grads[1, True].four()
    grads[0, True].two()
    grads[1, True].five()
    grads[1, False].three()
    grads[0, True].pair()
    grads[1, False].four()
    grads[0, False].two()
    grads[0, True].three()
    grads[1, False].five()
    grads[0, False].three()
    grads[0, True].four()
    grads[0, True].five()
    grads[0, False].four()
    grads[0, False].five()


def body(
    hidden_in, positions, attn_gain, w_query, w_key, w_value, w_output, ffn_gain, w_gate, w_up, w_down, grad_out
):
    own = lax.dynamic_slice_in_dim(positions, lax.axis_index("ctx") * ROWS, ROWS)
    half = HEAD_DIM // 2
    freq = jnp.exp(-jnp.log(rope_base) * (2.0 * jnp.arange(half, dtype=f32) / HEAD_DIM))
    angle = own.astype(f32)[:, None] * jnp.tile(freq, 4)[None, :]
    sign = jnp.tile(jnp.where(jnp.arange(HEAD_DIM) < half, -1.0, 1.0), 2).astype(f32)
    cosm, sinm = jnp.cos(angle), jnp.sin(angle) * sign[None, :]
    low = (positions.reshape(NC, ROWS)[:, 0] <= own[0]).astype(bf16)
    mlow = jnp.broadcast_to(low[:, None, None], (NC, 64, 128)).reshape(NC * 64, 128)
    spread = np.zeros((D, PD), np.float32)
    for s in range(ND):
        spread[72 * s + np.arange(72), R * s + np.arange(72)] = 1
    heads = np.zeros((PD, 128 * HEADS), np.float32)
    for t in range(D):
        heads[R * (t // 72) + t % 72, 128 * (t // 64) + 64 + t % 64] = 1
    gains = jnp.stack([attn_gain, ffn_gain], axis=1).astype(f32)
    gains = jnp.pad(gains, ((0, 0), (0, 6), (0, 56)))
    kv = jnp.stack(
        [w_key.reshape(LAYERS, 72, KV_HEADS, HEAD_DIM), w_value.reshape(LAYERS, 72, KV_HEADS, HEAD_DIM)], axis=3
    ).reshape(LAYERS, 72, 2 * KV_HEADS * HEAD_DIM)
    wattn = jnp.concatenate([w_output, w_query, kv], axis=2)
    outs = pl.pallas_call(
        kernel,
        out_shape=(
            jax.ShapeDtypeStruct((ROWS, D), bf16),
            jax.ShapeDtypeStruct((ROWS, D), f32),
            jax.ShapeDtypeStruct((LAYERS, 8, 128), f32),
            jax.ShapeDtypeStruct((LAYERS, 72, FF), f32),
            jax.ShapeDtypeStruct((LAYERS, 72, FF), f32),
            jax.ShapeDtypeStruct((LAYERS, 192, D), f32),
            jax.ShapeDtypeStruct((LAYERS, 72, FF), f32),
        ),
        in_specs=[pl.BlockSpec(memory_space=pltpu.VMEM)] * 12,
        out_specs=tuple([pl.BlockSpec(memory_space=pltpu.VMEM)] * 7),
        scratch_shapes=[
            pltpu.VMEM((LAYERS, 2, 24, ND, R, 128), bf16),
            pltpu.VMEM((6, 256, PD), bf16),
            pltpu.VMEM((LAYERS, NCHIP, 2, KV_HEADS, 2, 64, 128), bf16),
            pltpu.VMEM((NCHIP, 2, KV_HEADS, 2, 64, 128), bf16),
            pltpu.VMEM((LAYERS, NCHIP, KV_HEADS, 2, 64, 128), bf16),
            pltpu.VMEM((LAYERS, 7, KV_HEADS, 2, 64, 128), bf16),
            pltpu.VMEM((LAYERS, 24, ND, R, 128), bf16),
            pltpu.VMEM((LAYERS, 2, 3, 16, R, 128), bf16),
            pltpu.VMEM((LAYERS, 16, R, 128), bf16),
            pltpu.VMEM((LAYERS, 7, 2, R, 128), bf16),
            pltpu.VMEM((LAYERS, 7, ND, R, 128), bf16),
            pltpu.VMEM((LAYERS, 7, R, 128), bf16),
            pltpu.VMEM((LAYERS, NCHIP, 2, 2, R, 128), bf16),
            pltpu.VMEM((LAYERS, NCHIP, 2, 1, R, 128), bf16),
            pltpu.VMEM((LAYERS, 6, 128, 256), bf16),
            pltpu.VMEM((LAYERS, 128, D), f32),
            pltpu.VMEM((LAYERS, 128, D), f32),
            pltpu.VMEM((LAYERS, 128, PD), bf16),
            pltpu.VMEM((LAYERS, 128, PD), bf16),
            pltpu.VMEM((LAYERS, 128, PD), bf16),
            pltpu.VMEM((LAYERS, KV_HEADS, 192, 256), bf16),
            pltpu.VMEM((KV_HEADS, 192, 256), bf16),
            pltpu.VMEM((LAYERS, KV_HEADS, 128, 192), f32),
            pltpu.VMEM((LAYERS, KV_HEADS, 8, 192), f32),
            pltpu.VMEM((HEADS, 128, 128), bf16),
            pltpu.VMEM((HEADS, 128, 128), f32),
            pltpu.VMEM((1024, 256), f32),
            pltpu.VMEM((1024, 256), f32),
            pltpu.VMEM((1024, 192), bf16),
            pltpu.VMEM((1024, 192), f32),
            pltpu.VMEM((128, PD), bf16),
            pltpu.VMEM((LAYERS, 8, PD), f32),
            pltpu.VMEM((128, 192), f32),
            pltpu.VMEM((256, 192), f32),
            pltpu.VMEM((PD, 128), bf16),
            pltpu.SemaphoreType.DMA((288,)),
            pltpu.SemaphoreType.DMA((288,)),
        ],
        compiler_params=pltpu.CompilerParams(
            collective_id=0, has_side_effects=True, vmem_limit_bytes=63 * 1024 * 1024
        ),
    )(
        hidden_in, grad_out, cosm, sinm, mlow, jnp.asarray(spread, bf16), jnp.asarray(heads, bf16), gains,
        w_gate, w_up, w_down, wattn,
    )
    hout, ghid, ggains, ggate, gup, gdown, gattn = outs
    gkv = gattn[:, :, 2 * D:].reshape(LAYERS, 72, KV_HEADS, 2, HEAD_DIM)
    return (
        hout,
        ghid,
        ggains[:, 0, 0:72],
        gattn[:, :, D:2 * D],
        gkv[:, :, :, 0].reshape(LAYERS, 72, KV_HEADS * HEAD_DIM),
        gkv[:, :, :, 1].reshape(LAYERS, 72, KV_HEADS * HEAD_DIM),
        gattn[:, :, 0:D],
        ggains[:, 1, 0:72],
        ggate,
        gup,
        gdown,
    )


def solution(mesh):
    placed = (
        P(("dp", "ctx"), None),
        P("dp"),
        P(None, "dp"),
        P(None, "dp", None),
        P(None, "dp", None),
        P(None, "dp", None),
        P(None, "dp", None),
        P(None, "dp"),
        P(None, "dp", None),
        P(None, "dp", None),
        P(None, "dp", None),
        P(("dp", "ctx"), None),
    )
    out = (
        P(("dp", "ctx"), None),
        P(("dp", "ctx"), None),
        P(None, "dp"),
        P(None, "dp", None),
        P(None, "dp", None),
        P(None, "dp", None),
        P(None, "dp", None),
        P(None, "dp"),
        P(None, "dp", None),
        P(None, "dp", None),
        P(None, "dp", None),
    )
    return jax.shard_map(body, mesh=mesh, in_specs=placed, out_specs=out, check_vma=False)
```

```python
import jax
import jax.numpy as jnp
from jax import lax
from jax.experimental import pallas as pl
from jax.experimental.pallas import tpu as pltpu
from jax.sharding import PartitionSpec as P

D = 576
HEADS = 9
KV_HEADS = 3
HEAD_DIM = 64
FF = 1536
LAYERS = 2
ROWS = 128
ND = 8
NC = 16
NCHIP = 8
R = 80
PD = 640
MESH = pl.DeviceIdType.MESH
bf16 = jnp.bfloat16
f32 = jnp.float32
NEG = -1e30
eps_norm = 1e-05
rope_base = 100000.0


def nn(a, b):
    return lax.dot_general(a, b, (((1,), (0,)), ((), ())), preferred_element_type=f32)


def nt(a, b):
    return lax.dot_general(a, b, (((1,), (1,)), ((), ())), preferred_element_type=f32)


def tn(a, b):
    return lax.dot_general(a, b, (((0,), (0,)), ((), ())), preferred_element_type=f32)


class Move:
    def __init__(self, make, src, dst, inc, s, dev):
        self.out = lambda: make(src, dst, s, dev)
        self.inc = lambda: make(inc, inc, s, dev)

    def start(self):
        self.out().start()

    def recv(self):
        self.inc().wait_recv()

    def sent(self):
        self.out().wait_send()


def slot_of(shard):
    return (shard % 4) * 2 + shard // 4


def attn_place(t):
    return (t // 2, 18 + t % 2) if t < 4 else ((t - 4) // 4, 20 + (t - 4) % 4)


def kernel(
    hidT, goutT, pos, freq, again, fgain, wgate, wup, wdown, wo, wq, wk, wv,
    hout, ghid, oute, outl,
    mlow, e1, e2, gains, wattn,
    land, wd, kvl, dkv, dkr0, dkr1,
    rs0, r1e, rz, r2e, r1l, rzl, r2l, fine, finl,
    mid, hs, h1s, apad, bpad, mixp, qc, doc, oT, lse, oz, dqz,
    s1, s2, bias, mk, zpad, gain, acc1, acc2, go4,
    send, recv,
):
    d = lax.axis_index("dp")
    c = lax.axis_index("ctx")
    k, y = lax.rem(c, 2), lax.rem(c // 2, 4)
    x, zl = lax.rem(d, 4), d // 4
    mine = 2 * x + zl
    i = c // 2
    sib = {"ctx": i * 2 + 1 - k}
    count = [0]

    def dplus(m):
        return lax.rem(d + m, ND)

    def dminus(m):
        return lax.rem(d - m + ND, ND)

    def iplus(m):
        return lax.rem(i + m, NCHIP)

    def iminus(m):
        return lax.rem(i - m + NCHIP, NCHIP)

    def shard(m):
        return {"dp": dplus(m)}

    def slot(j):
        return lax.rem(j, 4) * 2 + j // 4

    def chip(m):
        return {"ctx": iplus(m) * 2 + k}

    def near(at, o):
        return lax.rem(at + o + 4, 4)

    def Y(o):
        return {"ctx": ((i // 4) * 4 + near(y, o)) * 2 + k}

    def rc(src, dst, s, to):
        return pltpu.make_async_remote_copy(
            src_ref=src, dst_ref=dst, send_sem=send.at[s], recv_sem=recv.at[s],
            device_id=to, device_id_type=MESH,
        )

    def sems(n):
        count[0] += n
        return count[0] - n

    def move(src, dst, inc, to, s=None):
        return Move(rc, src, dst, inc, sems(1) if s is None else s, to)

    def starts(*moves):
        for m in moves:
            m.start()

    def recvs(*moves):
        for m in moves:
            m.recv()

    def sents(*moves):
        for m in moves:
            m.sent()

    def each(f, lo=1, hi=8):
        def step(m, carry):
            f(m)
            return carry
        lax.fori_loop(lo, hi, step, 0)

    def put(l, j, val, last=None, k=k):
        last = jnp.zeros((8, 128), f32) if last is None else last
        land[l, k, j, mine] = jnp.concatenate([val.astype(f32), last], axis=0).astype(bf16)

    def column(t):
        return pl.ds(pl.multiple_of(128 * t, 128), 128)

    def pack_attn(l):
        key, value = wk[l].astype(f32), wv[l].astype(f32)
        parts = [wo[l].astype(f32), wq[l].astype(f32)]
        for h in range(KV_HEADS):
            parts += [key[:, 64 * h:64 * h + 64], value[:, 64 * h:64 * h + 64]]
        wattn[...] = jnp.concatenate(parts, axis=1).astype(bf16)
        gains[l] = jnp.zeros((8, 128), f32)
        gains[l, 0:1, 0:72] = again[l:l + 1, :].astype(f32)
        gains[l, 1:2, 0:72] = fgain[l:l + 1, :].astype(f32)
        if l == 0:
            for t in range(12):
                k_, j = attn_place(t)
                put(l, j, wattn[:, 128 * t:128 * t + 128], gains[l], k_)
        else:
            put(l, 18 + y, wattn[:, column(jnp.where(y < 2, 2 * k + y, 2 + 4 * k + y))], gains[l])
            put(l, 22, wattn[:, column(6 + 4 * k)])
            put(l, 23, wattn[:, column(7 + 4 * k)])

    def pack_ffn(l):
        @pl.when(y < 2)
        def _():
            for r in range(3):
                put(l, 3 * y + r, wgate[l, :, column(6 * k + 3 * y + r)])

        @pl.when(y >= 2)
        def _():
            for r in range(3):
                put(l, 3 * y + r, wup[l, :, column(6 * k + 3 * (y - 2) + r)])

        for g in range(6):
            val = wdown[l, pl.ds(pl.multiple_of(16 * (6 * k + g), 16), 16), :]
            val = jnp.concatenate([val.astype(f32), jnp.zeros((16, 64), f32)], axis=1).astype(bf16)
            for lt in range(5):
                land[l, k, 12 + g, mine, 16 * lt:16 * lt + 16, :] = val[:, 128 * lt:128 * lt + 128]

    class Weights:
        def __init__(self, l, shared, direct):
            self.shared = shared is not None
            db, nd = direct

            def straight(slot):
                return land.at[l, k, pl.ds(db, nd), slot]

            self.parts = [(straight, sems(7))]
            here, there = land.at[l, k, pl.ds(db, nd)], land.at[l, 1 - k, pl.ds(db, nd)]
            self.u = []
            if not self.shared:
                self.v = None
                self.base = sems(7)
                self.slot = lambda k_, slot: land.at[l, k_, pl.ds(db, nd), slot]
                return
            sb, ns = shared
            self.parts.append((lambda slot: land.at[l, k, pl.ds(sb + ns * y, ns), slot], sems(7)))
            self.v = [move(here, here, there, sib)]

            def block(y_, k_=k, half=None):
                ref = land.at[l, k_, pl.ds(sb + ns * y_, ns)]
                return ref if half is None else ref.at[:, pl.ds(4 * half, 4)]

            yp, ym, y2 = near(y, 1), near(y, -1), near(y, 2)
            self.u = [
                move(block(y), block(y), block(ym), Y(1)), move(block(y), block(y), block(yp), Y(-1)),
                move(block(ym, half=0), block(ym, half=0), block(y2, half=0), Y(1)),
                move(block(yp, half=1), block(yp, half=1), block(y2, half=1), Y(-1)),
            ]
            self.v += [move(block(y_), block(y_), block(y_, 1 - k), sib) for y_ in (y, ym, yp, y2)]

        def one(self, part):
            ref, s = self.parts[part]
            each(lambda m: rc(ref(mine), ref(mine), s + m - 1, shard(m)).start())

        def two(self, part):
            ref, s = self.parts[part]

            def go(m):
                own = ref(slot(dminus(m)))
                rc(own, own, s + m - 1, shard(m)).wait_recv()
                if not self.shared:
                    rc(own, own, self.base + m - 1, sib).start()

            each(go)
            if part:
                starts(self.u[0], self.u[1], self.v[1])
            elif self.shared:
                starts(self.v[0])

        def three(self):
            recvs(self.u[0])
            starts(self.u[2], self.v[2])
            recvs(self.u[1])
            starts(self.u[3], self.v[3])

        def four(self):
            recvs(self.u[2], self.u[3])
            starts(self.v[4])

        def five(self):
            if self.shared:
                recvs(*self.v)
                sents(*self.u)
                sents(*self.v)

            def go(m):
                for ref, s in self.parts:
                    rc(ref(mine), ref(mine), s + m - 1, shard(m)).wait_send()
                if not self.shared:
                    got, gave = self.slot(1 - k, slot(dminus(m))), self.slot(k, slot(dminus(m)))
                    rc(got, got, self.base + m - 1, sib).wait_recv()
                    rc(gave, gave, self.base + m - 1, sib).wait_send()
            each(go)

    class Keys:
        def __init__(self, l):
            self.l, self.a, self.b = l, sems(7), sems(7)
            own = kvl.at[l, i, k]
            self.s = move(own, own, kvl.at[l, i, 1 - k], sib)

        def one(self):
            own = kvl.at[self.l, i, k]
            each(lambda m: rc(own, own, self.a + m - 1, chip(m)).start())
            starts(self.s)

        def two(self):
            def go(m):
                ref = kvl.at[self.l, iminus(m), k]
                rc(ref, ref, self.a + m - 1, chip(m)).wait_recv()
                rc(ref, ref, self.b + m - 1, sib).start()
            each(go)

        def three(self):
            recvs(self.s)
            sents(self.s)

            def go(m):
                got, gave, own = kvl.at[self.l, iminus(m), 1 - k], kvl.at[self.l, iminus(m), k], kvl.at[self.l, i, k]
                rc(got, got, self.b + m - 1, sib).wait_recv()
                rc(gave, gave, self.b + m - 1, sib).wait_send()
                rc(own, own, self.a + m - 1, chip(m)).wait_send()
            each(go)

    class KeyGrads:
        def __init__(self, l):
            self.l = l
            self.s = move(dkv.at[:, 1 - k], dkr0.at[l], dkr0.at[l], sib)
            self.a = sems(7)

        def out(self, m):
            return rc(dkv.at[iplus(m), k], dkr1.at[self.l, m - 1], self.a + m - 1, chip(m))

        def one(self):
            starts(self.s)

        def two(self):
            recvs(self.s)

            def go(m):
                j = iplus(m)
                for h in range(KV_HEADS):
                    total = dkv[j, k, h].astype(f32) + dkr0[self.l, j, h].astype(f32)
                    dkv[j, k, h] = total.astype(bf16)
                self.out(m).start()

            each(go)

        def three(self):
            each(lambda m: self.out(m).wait())
            sents(self.s)

        def total(self, h):
            val = dkv[i, k, h].astype(f32) + dkr0[self.l, i, h].astype(f32)
            for m in range(7):
                val = val + dkr1[self.l, m, h].astype(f32)
            return val

    class Grads:
        def __init__(self, l, early):
            self.l, self.early = l, early
            self.own = 16 + y + 4 * (i // 4)
            self.s = []
            for lo, n in ((0, 16),) if early else ((16, 4), (20, 4)):
                there = rs0.at[l, pl.ds(lo, n)]
                self.s.append(move(land.at[l, 1 - k, pl.ds(lo, n)], there, there, sib))
            self.r1, self.r2, self.fin = (r1e, r2e, fine) if early else (r1l, r2l, finl)
            self.a, self.b, self.c, self.v, self.z = sems(12), sems(7), sems(7), sems(7), sems(1)
            own = self.fin.at[l, i, k]
            self.t = move(own, own, self.fin.at[l, i, 1 - k], sib)

        def out1(self, m):
            l = self.l
            if self.early:
                h, o = (m - 1) // 3, lax.rem(m - 1, 3)
                x_ = near(x, o + 1)
                src, to = land.at[l, k, pl.ds(8 * h, 8), pl.ds(2 * x_, 2)], {"dp": zl * 4 + x_}
                return rc(src, r1e.at[l, o, pl.ds(8 * h, 8)], self.a + m - 1, to)
            h, o = (m - 1) // 3, lax.rem(m - 1, 3)
            y_ = near(y, o + 1)
            to = {"ctx": ((i // 4) * 4 + y_) * 2 + k}
            return rc(land.at[l, k, 16 + 4 * h + y_], r1l.at[l, o, h], self.a + m - 1, to)

        def outz(self):
            if not self.early:
                src = land.at[self.l, k, 16 + y + 4 * (1 - i // 4)]
                return rc(src, rzl.at[self.l], self.z, {"ctx": ((1 - i // 4) * 4 + y) * 2 + k})
            src = land.at[self.l, k, pl.ds(0, 16), 2 * x + 1 - zl]
            return rc(src, rz.at[self.l], self.z, {"dp": 4 * (1 - zl) + x})

        def out2(self, m):
            l = self.l
            if self.early:
                src, to = land.at[l, k, pl.ds(2 * iplus(m), 2), mine], chip(m)
            else:
                src, to = land.at[l, k, self.own, slot(dplus(m))], shard(m)
            return rc(src, self.r2.at[l, m - 1], self.b + m - 1, to)

        def zero(self, part=0):
            starts(self.s[part])

        def one(self, part=0):
            recvs(self.s[part])
            l = self.l

            def go(u):
                total = land[l, k, u].astype(f32) + rs0[l, u].astype(f32)
                land[l, k, u] = total.astype(bf16)

            each(go, *((0, 16) if self.early else (16 + 4 * part, 20 + 4 * part)))

        def send(self, lo=1, hi=None):
            each(lambda m: self.out1(m).start(), lo, hi or 7)

        def two(self):
            each(lambda m: self.out1(m).wait(), 1, 7)
            l = self.l
            if self.early:
                def go(u):
                    total = land[l, k, u, pl.ds(2 * x, 2)].astype(f32)
                    for o in range(3):
                        total = total + r1e[l, o, u].astype(f32)
                    land[l, k, u, pl.ds(2 * x, 2)] = total.astype(bf16)

                each(go, 0, 16)
            else:
                def go(u):
                    for q in range(2):
                        total = land[l, k, 16 + y + 4 * q, u].astype(f32)
                        for m in range(3):
                            total = total + r1l[l, m, q, u].astype(f32)
                        land[l, k, 16 + y + 4 * q, u] = total.astype(bf16)

                each(go, 0, 8)
            self.outz().start()

        def pair(self):
            self.outz().wait()
            l = self.l

            def go(u):
                if self.early:
                    land[l, k, u, mine] = (land[l, k, u, mine].astype(f32) + rz[l, u].astype(f32)).astype(bf16)
                else:
                    total = land[l, k, self.own, u].astype(f32) + rzl[l, u].astype(f32)
                    land[l, k, self.own, u] = total.astype(bf16)

            each(go, 0, 16 if self.early else 8)
            each(lambda m: self.out2(m).start())

        def three(self):
            each(lambda m: self.out2(m).wait())
            l = self.l
            for u in range(2 if self.early else 1):
                total = (land[l, k, 2 * i + u, mine] if self.early else land[l, k, self.own, mine]).astype(f32)
                for m in range(7):
                    total = total + (self.r2[l, m, u] if self.early else self.r2[l, m]).astype(f32)
                self.fin[l, i, k, u] = total.astype(bf16)
            own = self.fin.at[l, i, k]
            each(lambda m: rc(own, own, self.c + m - 1, chip(m)).start())
            starts(self.t)

        def four(self):
            def go(m):
                ref = self.fin.at[self.l, iminus(m), k]
                rc(ref, ref, self.c + m - 1, chip(m)).wait_recv()
                rc(ref, ref, self.v + m - 1, sib).start()
            each(go)

        def five(self):
            l = self.l
            recvs(self.t)
            sents(self.t, *self.s)

            def go(m):
                got, gave = self.fin.at[l, iminus(m), 1 - k], self.fin.at[l, iminus(m), k]
                own = self.fin.at[l, i, k]
                rc(got, got, self.v + m - 1, sib).wait_recv()
                rc(gave, gave, self.v + m - 1, sib).wait_send()
                rc(own, own, self.c + m - 1, chip(m)).wait_send()
            each(go)

    weights = {
        (0, "A"): Weights(0, None, (20, 4)), (0, "O"): Weights(0, None, (18, 2)), (0, "F"): Weights(0, (0, 3), (12, 6)),
        (1, "A"): Weights(1, (18, 1), (22, 2)), (1, "F"): Weights(1, (0, 3), (12, 6)),
    }
    keys = [Keys(l) for l in range(LAYERS)]
    key_grads = [KeyGrads(l) for l in range(LAYERS)]
    grads = {(l, e): Grads(l, e) for l in range(LAYERS) for e in (True, False)}

    barrier = pltpu.get_barrier_semaphore()

    def hello(m):
        pl.semaphore_signal(barrier, inc=1, device_id=shard(m), device_id_type=MESH)
        pl.semaphore_signal(barrier, inc=1, device_id=chip(m), device_id_type=MESH)

    each(hello)
    pl.semaphore_signal(barrier, inc=1, device_id=sib, device_id_type=MESH)
    pack_attn(0)
    pl.semaphore_wait(barrier, 15)
    weights[0, "A"].one(0)
    pack_ffn(0)
    weights[0, "F"].one(1)
    pack_attn(1)
    pack_ffn(1)

    lane = lax.broadcasted_iota(jnp.int32, (128, 128), 1)
    low_half = lane < 64
    first_quarter = lax.rem(lane, 64) < 32
    place_own = pos[pl.ds(c, 1), :].astype(f32)
    angle = jnp.broadcast_to(place_own, (128, 128)).T * freq[...]
    cos_q = jnp.cos(angle)
    sin_q = jnp.sin(angle) * jnp.where(first_quarter, -1.0, 1.0)
    low = jnp.where(pos[:, 0:1] <= pos[pl.ds(c, 1), 0:1], 1.0, 0.0)
    for s in range(NC):
        mlow[64 * s:64 * s + 64, :] = jnp.broadcast_to(low[s:s + 1, :], (64, 128)).astype(bf16)
    row = lax.broadcasted_iota(jnp.int32, (D, PD), 0)
    col = lax.broadcasted_iota(jnp.int32, (D, PD), 1)
    shard_of = (row * 911) >> 16
    e1[...] = jnp.where(
        col == row - 72 * shard_of + R * ((shard_of & 3) * 2 + (shard_of >> 2)), 1.0, 0.0
    ).astype(bf16)
    row = lax.broadcasted_iota(jnp.int32, (PD, 128 * HEADS), 0)
    col = lax.broadcasted_iota(jnp.int32, (PD, 128 * HEADS), 1)
    at_slot = (row * 205) >> 14
    natural = row - R * at_slot + 72 * ((at_slot & 1) * 4 + (at_slot >> 1))
    hit = (row - R * at_slot < 72) & (col == 128 * (natural >> 6) + 64 + (natural & 63))
    e2[...] = jnp.where(hit, 1.0, 0.0).astype(bf16)
    cos_kv = jnp.where(low_half, cos_q, 1.0)
    sin_kv = jnp.where(low_half, sin_q, 0.0)

    def swap(x):
        return jnp.where(first_quarter, pltpu.roll(x, 96, axis=1), pltpu.roll(x, 32, axis=1))

    row = lax.broadcasted_iota(jnp.int32, (1024, 192), 0) - 64 * c
    col = lax.rem(lax.broadcasted_iota(jnp.int32, (1024, 192), 1), 64)
    bias[...] = jnp.where((row > col) & (row < 64), NEG, 0.0).astype(bf16)
    mk[...] = jnp.concatenate([mlow[...], mlow[:, 0:64]], axis=1).astype(f32)
    row = lax.broadcasted_iota(jnp.int32, (64, 192), 0)
    col = lax.rem(lax.broadcasted_iota(jnp.int32, (64, 192), 1), 64)
    tri = jnp.where(row > col, NEG, 0.0)
    zpad[...] = jnp.zeros((128, PD), bf16)

    def place(u):
        if isinstance(u, int) and u >= 36:
            return attn_place(u - 36)
        return lax.rem(u, 12) // 6, 6 * (u // 12) + lax.rem(u, 6)

    def unit(l, u):
        return land[(l, *place(u))].reshape(PD, 128)

    def pair(l, u):
        return jnp.concatenate([unit(l, u), unit(l, u + 1)], axis=1)

    def units(l, u, n):
        return jnp.concatenate([unit(l, u + j) for j in range(n)], axis=1)

    def norm_scale(h):
        return lax.rsqrt(jnp.mean(h * h, axis=-1, keepdims=True) + eps_norm)

    def spread(x):
        return nn(x.astype(bf16), e1[...]).astype(bf16)

    def unspread(x):
        hi = x.astype(bf16)
        lo = (x - hi.astype(f32)).astype(bf16)
        return nt(hi, e1[...]) + nt(lo, e1[...])

    def set_unit(l, u, val):
        land[(l, *place(u))] = val.reshape(8, R, 128)

    def load_gains(l):
        total = jnp.zeros((8, PD), f32)
        for s in range(ND):
            part = land[l, 0, 20, slot_of(s)].astype(f32)[72:80, :]
            wide = jnp.concatenate([part, jnp.zeros((8, PD - 128), f32)], axis=1)
            total = total + (pltpu.roll(wide, 72 * s, axis=1) if s else wide)
        gain[l] = total

    def down_pieces(l, f):
        def go(g):
            for k_ in range(2):
                for s in range(ND):
                    for lt in range(5):
                        f(
                            wd.at[12 * s + 6 * k_ + g, :, 128 * lt:128 * lt + 128],
                            land.at[l, k_, 12 + g, slot_of(s), 16 * lt:16 * lt + 16, :],
                        )
        each(go, 0, 6)

    def regroup_down(l):
        def go(rows, piece):
            rows[...] = piece[...]
        down_pieces(l, go)

    def scatter_down(l):
        def go(rows, piece):
            piece[...] = rows[...]
        down_pieces(l, go)

    def down(t):
        return wd[pl.ds(16 * t, 16)].reshape(256, PD)

    def tiles(l, h, j):
        tlo = kvl[l, pl.ds(2 * j, 2), :, h, 0].reshape(256, 128)
        thi = kvl[l, pl.ds(2 * j, 2), :, h, 1].reshape(256, 128)
        m = mlow[pl.ds(pl.multiple_of(256 * j, 256), 256), :]
        x2 = jnp.concatenate([tlo * m, thi * (1 - m)], axis=1)
        return tlo, x2, m

    def swiglu_parts(l, t, x):
        g = nn(x, pair(l, 2 * t))
        u = nn(x, pair(l, 12 + 2 * t))
        return g, u

    def forward(l, h):
        hs[l] = h
        if l == 0:
            weights[0, "A"].two(0)
        weights[l, "A"].five()
        load_gains(l)
        apad[l] = spread(h * norm_scale(h) * gain[l, 0:1, 0:D])
        a = apad[l]
        for s in range(KV_HEADS):
            kv = nn(a, unit(l, 45 + s))
            kv = kv * cos_kv + swap(kv) * sin_kv
            kvl[l, i, k, s] = kv.astype(bf16).reshape(2, 64, 128)
        keys[l].one()
        if l == 1:
            weights[1, "F"].two(1)
            weights[1, "F"].two(0)
        for t in range(5):
            q = nn(a, unit(l, 40 + t))
            q = (q * cos_q + swap(q) * sin_q) * HEAD_DIM ** (-0.5)
            for j in ((2 * t - 1, 2 * t) if t else (0,)):
                part = q if j % 2 else pltpu.roll(q, 64, axis=1)
                part = jnp.where(low_half, part, 0.0).astype(bf16)
                g = j % 3
                qc[l, j // 3, 64 * g:64 * g + 64, 0:128] = part[0:64]
                qc[l, j // 3, 64 * g:64 * g + 64, 128:256] = part[64:128]
        keys[l].two()
        if l == 0:
            weights[0, "F"].two(1)
            weights[0, "O"].one(0)
            weights[0, "F"].one(0)
        keys[l].three()

        def head(s):
            qcat = qc[l, s]
            qT = qcat.astype(f32).T.astype(bf16)
            qhT = qT[128:256]
            top_own = kvl[l, i, k, s, 1]
            se = nn(top_own, qhT) + tri

            def scores(j, carry):
                ml, mh = carry
                tlo, x2, _ = tiles(l, s, j)
                at = pl.ds(pl.multiple_of(256 * j, 256), 256)
                a1 = nn(tlo, qhT)
                a2 = nn(x2, qT) + bias[at, :].astype(f32)
                s1[at, 0:192] = a1
                s2[at, 0:192] = a2
                is_low = mk[at, :] > 0.5
                ml = jnp.maximum(ml, jnp.max(jnp.where(is_low, a2, NEG), axis=0, keepdims=True))
                mh = jnp.maximum(
                    mh, jnp.max(jnp.maximum(a1, jnp.where(is_low, NEG, a2)), axis=0, keepdims=True)
                )
                return ml, mh

            ml, mh = lax.fori_loop(
                0, 4, scores,
                (jnp.full((1, 192), NEG, f32), jnp.max(se, axis=0, keepdims=True)),
            )
            pe = jnp.exp(se - mh)
            acc1[...] = tn(top_own, pe.astype(bf16))
            acc2[...] = jnp.zeros((256, 192), f32)

            def weigh(j, carry):
                ll, lh = carry
                tlo, x2, _ = tiles(l, s, j)
                at = pl.ds(pl.multiple_of(256 * j, 256), 256)
                is_low = mk[at, :] > 0.5
                p1 = jnp.exp(s1[at, 0:192] - mh)
                p2 = jnp.exp(s2[at, 0:192] - jnp.where(is_low, ml, mh))
                ll = ll + jnp.sum(jnp.where(is_low, p2, 0.0), axis=0, keepdims=True)
                lh = lh + jnp.sum(p1 + jnp.where(is_low, 0.0, p2), axis=0, keepdims=True)
                acc1[...] += tn(tlo, p1.astype(bf16))
                acc2[...] += tn(x2, p2.astype(bf16))
                return ll, lh

            ll, lh = lax.fori_loop(
                0, 4, weigh, (jnp.zeros((1, 192), f32), jnp.sum(pe, axis=0, keepdims=True))
            )
            olow = acc2[64:128, :] / ll
            ohigh = (acc2[192:256, :] + acc1[64:128, :]) / lh
            oT[l, s, 0:64, :] = olow
            oT[l, s, 64:128, :] = ohigh
            lse[l, s, 0:1, :] = ml + jnp.log(ll)
            lse[l, s, 1:2, :] = mh + jnp.log(lh)
            zero = jnp.zeros((64, 192), f32)
            tl = jnp.concatenate([zero, olow], axis=0).T.astype(bf16)
            th = jnp.concatenate([zero, ohigh], axis=0).T.astype(bf16)
            for g in range(3):
                oz[3 * s + g, 0:64, :] = tl[64 * g:64 * g + 64]
                oz[3 * s + g, 64:128, :] = th[64 * g:64 * g + 64]

            if l == 0:
                @pl.when(s == 0)
                def _():
                    weights[1, "A"].one(1)
                    weights[1, "A"].one(0)

                @pl.when(s == 1)
                def _():
                    weights[0, "F"].three()
                    weights[0, "O"].two(0)
                    weights[1, "F"].one(1)
                    weights[1, "F"].one(0)
            else:
                @pl.when(s == 1)
                def _():
                    weights[1, "F"].three()

        each(head, 0, KV_HEADS)
        if l == 0:
            weights[0, "F"].two(0)
            weights[0, "F"].four()
            weights[0, "O"].five()
        mixp[l] = nt(jnp.concatenate([oz[j] for j in range(HEADS)], axis=1), e2[...]).astype(bf16)
        out = nn(mixp[l], units(l, 36, 5))
        h1 = h + out[:, 0:D]
        h1s[l] = h1
        bpad[l] = spread(h1 * norm_scale(h1) * gain[l, 1:2, 0:D])
        if l == 0:
            weights[1, "A"].two(1)
        else:
            weights[1, "F"].four()
        weights[l, "F"].five()
        regroup_down(l)

        def ffn(t, total):
            g, u = swiglu_parts(l, t, bpad[l])
            if l == LAYERS - 1:
                s1[pl.ds(pl.multiple_of(128 * t, 128), 128), :] = g
                s2[pl.ds(pl.multiple_of(128 * t, 128), 128), :] = u
            m = (g / (1.0 + jnp.exp(-g)) * u).astype(bf16)
            mid[l, t] = m
            if l == 0:
                @pl.when(t == 3)
                def _():
                    weights[1, "A"].three()

            return total + nn(m, down(t))

        total = lax.fori_loop(0, 6, ffn, jnp.zeros((128, PD), f32))
        if l == 0:
            weights[1, "A"].two(0)
            weights[1, "A"].four()
        return h1 + total[:, 0:D]

    def norm_back(h, g, dn, gain_row):
        r = norm_scale(h)
        xn = h * r
        cc = dn * gain_row
        return (
            g + r * (cc - xn * jnp.mean(cc * xn, axis=-1, keepdims=True)),
            jnp.sum(dn * xn, axis=0, keepdims=True),
        )

    def backward(l, g):
        zpad[:, 0:D] = g.astype(bf16)
        if l < LAYERS - 1:
            regroup_down(l)
        bT = bpad[l].T

        def ffn(t, total):
            dz = zpad[...]
            if l == LAYERS - 1:
                at = pl.ds(pl.multiple_of(128 * t, 128), 128)
                ga, u = s1[at, :], s2[at, :]
            else:
                ga, u = swiglu_parts(l, t, bpad[l])
            dm = nt(dz, down(t))
            sg = 1.0 / (1.0 + jnp.exp(-ga))
            silu = ga * sg
            dg = (dm * u * (sg * (1.0 + ga * (1.0 - sg)))).astype(bf16)
            du = (dm * silu).astype(bf16)
            total = total + nt(dg, pair(l, 2 * t)) + nt(du, pair(l, 12 + 2 * t))
            wd[pl.ds(16 * t, 16)] = tn(mid[l, t], dz).astype(bf16).reshape(16, 16, PD)
            gw = nn(bT, dg).astype(bf16)
            set_unit(l, 2 * t, gw[:, 0:128])
            set_unit(l, 2 * t + 1, gw[:, 128:256])
            gw = nn(bT, du).astype(bf16)
            set_unit(l, 12 + 2 * t, gw[:, 0:128])
            set_unit(l, 13 + 2 * t, gw[:, 128:256])
            return total

        total = lax.fori_loop(0, 6, ffn, jnp.zeros((128, PD), f32))
        scatter_down(l)
        grads[l, True].zero()
        if l < LAYERS - 1:
            grads[l + 1, False].one(1)
            grads[l + 1, False].send(4, 7)
        dh1, dgain_ffn = norm_back(h1s[l], g, unspread(total), gain[l, 1:2, 0:D])
        zpad[:, 0:D] = dh1.astype(bf16)
        do = nt(zpad[...], units(l, 36, 5)).astype(bf16)
        go = nn(mixp[l].T, zpad[...]).astype(bf16)
        for t in range(4):
            set_unit(l, 36 + t, go[:, 128 * t:128 * t + 128])
        go4[...] = go[:, 512:640]
        grads[l, False].zero(0)
        for j in range(HEADS):
            part = nn(do, e2[:, 128 * j:128 * j + 128]).astype(bf16)
            gidx = j % 3
            doc[j // 3, 64 * gidx:64 * gidx + 64, 0:128] = part[0:64]
            doc[j // 3, 64 * gidx:64 * gidx + 64, 128:256] = part[64:128]

        def head(s):
            qcat = qc[l, s]
            qh = qcat[:, 128:256]
            qT = qcat.astype(f32).T.astype(bf16)
            qhT = qT[128:256]
            docat = doc[s]
            doh = docat[:, 128:256]
            doT = docat.astype(f32).T
            doTb = doT.astype(bf16)
            dohT = doTb[128:256]
            dl = jnp.sum(oT[l, s, 0:64, :] * doT[64:128, :], axis=0, keepdims=True)
            dh = jnp.sum(oT[l, s, 64:128, :] * doT[192:256, :], axis=0, keepdims=True)
            lsl = lse[l, s, 0:1, :]
            lsh = lse[l, s, 1:2, :]
            own = kvl[l, i, k, s, 1]
            pe = jnp.exp(nn(own, qhT) + tri - lsh)
            dse = (pe * (nn(own, dohT) - dh)).astype(bf16)
            dxe = nn(dse, qh) + nn(pe.astype(bf16), doh)
            acc1[...] = tn(own, dse)
            acc2[...] = jnp.zeros((256, 192), f32)

            def chunk(j):
                tlo, x2, m = tiles(l, s, j)
                at = pl.ds(pl.multiple_of(256 * j, 256), 256)
                is_low = mk[at, :] > 0.5
                p1 = jnp.exp(nn(tlo, qhT) - lsh)
                p2 = jnp.exp(nn(x2, qT) + bias[at, :].astype(f32) - jnp.where(is_low, lsl, lsh))
                ds1 = (p1 * (nn(tlo, dohT) - dh)).astype(bf16)
                ds2 = (p2 * (nn(x2, doTb) - jnp.where(is_low, dl, dh))).astype(bf16)
                p1 = p1.astype(bf16)
                p2 = p2.astype(bf16)
                dx1 = nn(ds1, qh) + nn(p1, doh)
                dx2 = nn(ds2, qcat) + nn(p2, docat)
                mf = m.astype(f32)
                lo = dx1 + mf * dx2[:, 0:128]
                hi = (1.0 - mf) * dx2[:, 128:256]
                dkv[pl.ds(2 * j, 2), :, s, 0] = lo.astype(bf16).reshape(2, 2, 64, 128)
                dkv[pl.ds(2 * j, 2), :, s, 1] = hi.astype(bf16).reshape(2, 2, 64, 128)
                acc1[...] += tn(tlo, ds1)
                acc2[...] += tn(x2, ds2)

            each(chunk, 0, 4)
            dkv[i, k, s, 1] = dxe.astype(bf16)
            zero = jnp.zeros((64, 192), f32)
            tl = jnp.concatenate([acc2[0:64, :], zero], axis=0).T
            th = jnp.concatenate([acc2[128:192, :] + acc1[0:64, :], zero], axis=0).T
            scale = HEAD_DIM ** (-0.5)
            for gidx in range(3):
                dqz[3 * s + gidx, 0:64, :] = tl[64 * gidx:64 * gidx + 64] * scale
                dqz[3 * s + gidx, 64:128, :] = th[64 * gidx:64 * gidx + 64] * scale

            @pl.when(s == 1)
            def _():
                grads[l, False].one(0)
                if l < LAYERS - 1:
                    grads[l, False].send(1, 4)
                    grads[l + 1, True].two()
                else:
                    grads[l, True].one()

        if l < LAYERS - 1:
            grads[l, True].one()
            grads[l, True].send(1, 4)
        each(head, 0, KV_HEADS)
        kg = key_grads[l]
        kg.one()
        kg.two()
        if l < LAYERS - 1:
            grads[l, True].send(4, 7)
            grads[l + 1, False].two()
        else:
            grads[l, True].send()
            grads[l, False].send(1, 4)

        rot = []
        for j in range(HEADS):
            t = dqz[j]
            rot.append(t * cos_q - swap(t) * sin_q)
        dq = [pltpu.roll(rot[0], 64, axis=1).astype(bf16)]
        for t in range(1, 5):
            dq.append((rot[2 * t - 1] + pltpu.roll(rot[2 * t], 64, axis=1)).astype(bf16))
        dq = jnp.concatenate(dq, axis=1)
        aT = apad[l].T
        gq = nn(aT, dq).astype(bf16)
        kg.three()
        if l < LAYERS - 1:
            grads[l + 1, True].pair()
        dkv_in = []
        for s in range(KV_HEADS):
            t = kg.total(s).reshape(128, 128)
            dkv_in.append((t * cos_kv - swap(t) * sin_kv).astype(bf16))
        dkv_in = jnp.concatenate(dkv_in, axis=1)
        da = nt(dq, units(l, 40, 5)) + nt(dkv_in, units(l, 45, 3))
        set_unit(l, 40, gq[:, 0:128] + go4[...])
        for t in range(1, 5):
            set_unit(l, 40 + t, gq[:, 128 * t:128 * t + 128])
        gkv = nn(aT, dkv_in).astype(bf16)
        for t in range(3):
            set_unit(l, 45 + t, gkv[:, 128 * t:128 * t + 128])
        dh, dgain_attn = norm_back(hs[l], dh1, unspread(da), gain[l, 0:1, 0:D])
        rows = jnp.concatenate([dgain_attn, dgain_ffn, jnp.zeros((6, D), f32)], axis=0)
        rows = jnp.concatenate([rows, jnp.zeros((8, PD - D), f32)], axis=1)
        for s in range(ND):
            part = (pltpu.roll(rows, PD - 72 * s, axis=1) if s else rows)[:, 0:128]
            keep = land[l, 0, 20, slot_of(s)].astype(f32)[0:72, :]
            land[l, 0, 20, slot_of(s)] = jnp.concatenate([keep, part], axis=0).astype(bf16)
        grads[l, False].zero(1)
        return dh

    h = hidT[...].astype(f32).T
    h = forward(0, h)
    h = forward(1, h)
    hout[...] = h.astype(bf16)
    g = backward(1, goutT[...].astype(f32).T)
    g = backward(0, g)
    ghid[...] = g
    grads[0, False].one(1)
    grads[0, False].send(4, 7)
    grads[0, True].two()
    grads[1, False].pair()
    grads[1, True].three()
    grads[0, False].two()
    grads[0, True].pair()
    grads[1, False].three()
    grads[1, True].four()
    grads[1, True].five()
    grads[0, False].pair()
    grads[0, True].three()
    grads[1, False].four()
    grads[1, False].five()
    grads[0, False].three()
    grads[0, True].four()
    grads[0, True].five()
    oute[...] = fine[...]
    grads[0, False].four()
    grads[0, False].five()
    outl[...] = finl[...]


def unpack(h, gh, early, late, houtT, ghidT, gag, gq, gk, gv, go, gfg, ggate, gup, gdown):
    houtT[...] = h[...].astype(f32).T.astype(bf16)
    ghidT[...] = gh[...].T
    for l in range(LAYERS):
        attn = [None] * 12
        for cc in range(NC):
            i_, k_ = cc // 2, cc % 2
            for j in (2 * i_, 2 * i_ + 1, 16 + i_ % 4 + 4 * (i_ // 4)):
                val = (early[l, i_, k_, j - 2 * i_] if j < 16 else late[l, i_, k_, 0]).astype(f32)
                kind, t = j // 6, 6 * k_ + j % 6
                cols = slice(128 * t, 128 * t + 128)
                if kind == 0:
                    ggate[l, :, cols] = val[0:72]
                elif kind == 1:
                    gup[l, :, cols] = val[0:72]
                elif kind == 2:
                    at = slice(16 * t, 16 * t + 16)
                    for lt in range(4):
                        gdown[l, at, 128 * lt:128 * lt + 128] = val[16 * lt:16 * lt + 16]
                    gdown[l, at, 512:576] = val[64:80, 0:64]
                else:
                    t = 2 * k_ + j - 18 if j < 20 else 4 + 4 * k_ + j - 20
                    attn[t] = val[0:72]
                    if t == 4:
                        gag[l:l + 1, :] = val[72:73, 0:72]
                        gfg[l:l + 1, :] = val[73:74, 0:72]
        attn = jnp.concatenate(attn, axis=1)
        go[l] = attn[:, 0:D]
        gq[l] = attn[:, D:2 * D]
        kv = [attn[:, 2 * D + 64 * j:2 * D + 64 * j + 64] for j in range(2 * KV_HEADS)]
        gk[l] = jnp.concatenate(kv[0::2], axis=1)
        gv[l] = jnp.concatenate(kv[1::2], axis=1)


def body(
    hidden_in, positions, attn_gain, w_query, w_key, w_value, w_output, ffn_gain, w_gate, w_up, w_down, grad_out
):
    half = HEAD_DIM // 2
    freq = jnp.exp(-jnp.log(rope_base) * (2.0 * jnp.arange(half, dtype=f32) / HEAD_DIM))
    freq = jnp.tile(freq, 4).reshape(1, 128)
    outs = pl.pallas_call(
        kernel,
        out_shape=(
            jax.ShapeDtypeStruct((ROWS, D), bf16),
            jax.ShapeDtypeStruct((ROWS, D), f32),
            jax.ShapeDtypeStruct((LAYERS, NCHIP, 2, 2, R, 128), bf16),
            jax.ShapeDtypeStruct((LAYERS, NCHIP, 2, 1, R, 128), bf16),
        ),
        in_specs=[pl.BlockSpec(memory_space=pltpu.VMEM)] * 13,
        out_specs=tuple([pl.BlockSpec(memory_space=pltpu.VMEM)] * 4),
        scratch_shapes=[
            pltpu.VMEM((NC * 64, 128), bf16),
            pltpu.VMEM((D, PD), bf16),
            pltpu.VMEM((PD, 128 * HEADS), bf16),
            pltpu.VMEM((LAYERS, 8, 128), f32),
            pltpu.VMEM((72, FF), bf16),
            pltpu.VMEM((LAYERS, 2, 24, ND, R, 128), bf16),
            pltpu.VMEM((96, 16, PD), bf16),
            pltpu.VMEM((LAYERS, NCHIP, 2, KV_HEADS, 2, 64, 128), bf16),
            pltpu.VMEM((NCHIP, 2, KV_HEADS, 2, 64, 128), bf16),
            pltpu.VMEM((LAYERS, NCHIP, KV_HEADS, 2, 64, 128), bf16),
            pltpu.VMEM((LAYERS, 7, KV_HEADS, 2, 64, 128), bf16),
            pltpu.VMEM((LAYERS, 24, ND, R, 128), bf16),
            pltpu.VMEM((LAYERS, 3, 16, 2, R, 128), bf16),
            pltpu.VMEM((LAYERS, 16, R, 128), bf16),
            pltpu.VMEM((LAYERS, 7, 2, R, 128), bf16),
            pltpu.VMEM((LAYERS, 3, 2, ND, R, 128), bf16),
            pltpu.VMEM((LAYERS, ND, R, 128), bf16),
            pltpu.VMEM((LAYERS, 7, R, 128), bf16),
            pltpu.VMEM((LAYERS, NCHIP, 2, 2, R, 128), bf16),
            pltpu.VMEM((LAYERS, NCHIP, 2, 1, R, 128), bf16),
            pltpu.VMEM((LAYERS, 6, 128, 256), bf16),
            pltpu.VMEM((LAYERS, 128, D), f32),
            pltpu.VMEM((LAYERS, 128, D), f32),
            pltpu.VMEM((LAYERS, 128, PD), bf16),
            pltpu.VMEM((LAYERS, 128, PD), bf16),
            pltpu.VMEM((LAYERS, 128, PD), bf16),
            pltpu.VMEM((LAYERS, KV_HEADS, 192, 256), bf16),
            pltpu.VMEM((KV_HEADS, 192, 256), bf16),
            pltpu.VMEM((LAYERS, KV_HEADS, 128, 192), f32),
            pltpu.VMEM((LAYERS, KV_HEADS, 8, 192), f32),
            pltpu.VMEM((HEADS, 128, 128), bf16),
            pltpu.VMEM((HEADS, 128, 128), f32),
            pltpu.VMEM((1024, 256), f32),
            pltpu.VMEM((1024, 256), f32),
            pltpu.VMEM((1024, 192), bf16),
            pltpu.VMEM((1024, 192), f32),
            pltpu.VMEM((128, PD), bf16),
            pltpu.VMEM((LAYERS, 8, PD), f32),
            pltpu.VMEM((128, 192), f32),
            pltpu.VMEM((256, 192), f32),
            pltpu.VMEM((PD, 128), bf16),
            pltpu.SemaphoreType.DMA((320,)),
            pltpu.SemaphoreType.DMA((320,)),
        ],
        compiler_params=pltpu.CompilerParams(
            collective_id=0, has_side_effects=True, vmem_limit_bytes=127 * 512 * 1024
        ),
    )(
        hidden_in.T, grad_out.T, positions.reshape(NC, ROWS), freq, attn_gain, ffn_gain,
        w_gate, w_up, w_down, w_output, w_query, w_key, w_value,
    )
    shapes = (
        (D, ROWS), (D, ROWS), (LAYERS, 72), (LAYERS, 72, D), (LAYERS, 72, KV_HEADS * HEAD_DIM),
        (LAYERS, 72, KV_HEADS * HEAD_DIM), (LAYERS, 72, D), (LAYERS, 72), (LAYERS, 72, FF), (LAYERS, 72, FF),
        (LAYERS, 192, D),
    )
    houtT, ghidT, *rest = pl.pallas_call(
        unpack,
        out_shape=[jax.ShapeDtypeStruct(shape, f32 if n else bf16) for n, shape in enumerate(shapes)],
        in_specs=[pl.BlockSpec(memory_space=pltpu.VMEM)] * 4,
        out_specs=[pl.BlockSpec(memory_space=pltpu.VMEM)] * 11,
        compiler_params=pltpu.CompilerParams(vmem_limit_bytes=127 * 512 * 1024),
    )(*outs)
    return (houtT.T, ghidT.T, *rest)


def solution(mesh):
    placed = (
        P(("dp", "ctx"), None),
        P("dp"),
        P(None, "dp"),
        P(None, "dp", None),
        P(None, "dp", None),
        P(None, "dp", None),
        P(None, "dp", None),
        P(None, "dp"),
        P(None, "dp", None),
        P(None, "dp", None),
        P(None, "dp", None),
        P(("dp", "ctx"), None),
    )
    out = (
        P(("dp", "ctx"), None),
        P(("dp", "ctx"), None),
        P(None, "dp"),
        P(None, "dp", None),
        P(None, "dp", None),
        P(None, "dp", None),
        P(None, "dp", None),
        P(None, "dp"),
        P(None, "dp", None),
        P(None, "dp", None),
        P(None, "dp", None),
    )
    return jax.shard_map(body, mesh=mesh, in_specs=placed, out_specs=out, check_vma=False)
```

```python
import jax
import jax.numpy as jnp
from jax import lax
from jax.experimental import pallas as pl
from jax.experimental.pallas import tpu as pltpu
from jax.sharding import PartitionSpec as P

D = 576
HEADS = 9
KV_HEADS = 3
HEAD_DIM = 64
FF = 1536
LAYERS = 2
ROWS = 128
ND = 8
NC = 16
NCHIP = 8
R = 80
PD = 640
MESH = pl.DeviceIdType.MESH
bf16 = jnp.bfloat16
f32 = jnp.float32
NEG = -1e30
eps_norm = 1e-05
rope_base = 100000.0


def nn(a, b):
    return lax.dot_general(a, b, (((1,), (0,)), ((), ())), preferred_element_type=f32)


def nt(a, b):
    return lax.dot_general(a, b, (((1,), (1,)), ((), ())), preferred_element_type=f32)


def tn(a, b):
    return lax.dot_general(a, b, (((0,), (0,)), ((), ())), preferred_element_type=f32)


class Move:
    def __init__(self, make, src, dst, inc, s, dev):
        self.out = lambda: make(src, dst, s, dev)
        self.inc = lambda: make(inc, inc, s, dev)

    def start(self):
        self.out().start()

    def recv(self):
        self.inc().wait_recv()

    def sent(self):
        self.out().wait_send()


def slot_of(shard):
    return (shard % 4) * 2 + shard // 4


def attn_place(t):
    return (t // 2, 18 + t % 2) if t < 4 else ((t - 4) // 4, 20 + (t - 4) % 4)


def kernel(
    hidT, goutT, pos, freq, again, fgain, wgate, wup, wdown, wo, wq, wk, wv,
    hout, ghid, oute, outl,
    mlow, e1, e2, gains, wattn,
    land, wd, kvl, dkv, dkr0, dkr1,
    rs0, r1e, rz, r2e, r1l, rzl, r2l, fine, finl,
    mid, hs, h1s, apad, bpad, mixp, qc, doc, oT, lse, oz, dqz,
    s1, s2, bias, mk, zpad, gain, acc1, acc2, go4,
    send, recv,
):
    d = lax.axis_index("dp")
    c = lax.axis_index("ctx")
    k, y = lax.rem(c, 2), lax.rem(c // 2, 4)
    x, zl = lax.rem(d, 4), d // 4
    mine = 2 * x + zl
    i = c // 2
    sib = {"ctx": i * 2 + 1 - k}
    count = [0]

    def dplus(m):
        return lax.rem(d + m, ND)

    def dminus(m):
        return lax.rem(d - m + ND, ND)

    def iplus(m):
        return lax.rem(i + m, NCHIP)

    def iminus(m):
        return lax.rem(i - m + NCHIP, NCHIP)

    def shard(m):
        return {"dp": dplus(m)}

    def slot(j):
        return lax.rem(j, 4) * 2 + j // 4

    def chip(m):
        return {"ctx": iplus(m) * 2 + k}

    def near(at, o):
        return lax.rem(at + o + 4, 4)

    def X(o):
        return {"dp": zl * 4 + near(x, o)}

    def Y(o):
        return {"ctx": ((i // 4) * 4 + near(y, o)) * 2 + k}

    def rc(src, dst, s, to):
        return pltpu.make_async_remote_copy(
            src_ref=src, dst_ref=dst, send_sem=send.at[s], recv_sem=recv.at[s],
            device_id=to, device_id_type=MESH,
        )

    def sems(n):
        count[0] += n
        return count[0] - n

    def move(src, dst, inc, to, s=None):
        return Move(rc, src, dst, inc, sems(1) if s is None else s, to)

    def starts(*moves):
        for m in moves:
            m.start()

    def recvs(*moves):
        for m in moves:
            m.recv()

    def sents(*moves):
        for m in moves:
            m.sent()

    def each(f, lo=1, hi=8):
        def step(m, carry):
            f(m)
            return carry
        lax.fori_loop(lo, hi, step, 0)

    def put(l, j, val, last=None, k=k):
        last = jnp.zeros((8, 128), f32) if last is None else last
        land[l, k, j, mine] = jnp.concatenate([val.astype(f32), last], axis=0).astype(bf16)

    def column(t):
        return pl.ds(pl.multiple_of(128 * t, 128), 128)

    def pack_attn(l):
        key, value = wk[l].astype(f32), wv[l].astype(f32)
        parts = [wo[l].astype(f32), wq[l].astype(f32)]
        for h in range(KV_HEADS):
            parts += [key[:, 64 * h:64 * h + 64], value[:, 64 * h:64 * h + 64]]
        wattn[...] = jnp.concatenate(parts, axis=1).astype(bf16)
        gains[l] = jnp.zeros((8, 128), f32)
        gains[l, 0:1, 0:72] = again[l:l + 1, :].astype(f32)
        gains[l, 1:2, 0:72] = fgain[l:l + 1, :].astype(f32)
        if l == 0:
            for t in range(12):
                k_, j = attn_place(t)
                put(l, j, wattn[:, 128 * t:128 * t + 128], gains[l], k_)
        else:
            put(l, 18 + y, wattn[:, column(jnp.where(y < 2, 2 * k + y, 2 + 4 * k + y))], gains[l])
            put(l, 22, wattn[:, column(6 + 4 * k)])
            put(l, 23, wattn[:, column(7 + 4 * k)])

    def pack_ffn(l):
        @pl.when(y < 2)
        def _():
            for r in range(3):
                put(l, 3 * y + r, wgate[l, :, column(6 * k + 3 * y + r)])

        @pl.when(y >= 2)
        def _():
            for r in range(3):
                put(l, 3 * y + r, wup[l, :, column(6 * k + 3 * (y - 2) + r)])

        for g in range(6):
            val = wdown[l, pl.ds(pl.multiple_of(16 * (6 * k + g), 16), 16), :]
            val = jnp.concatenate([val.astype(f32), jnp.zeros((16, 64), f32)], axis=1).astype(bf16)
            for lt in range(5):
                land[l, k, 12 + g, mine, 16 * lt:16 * lt + 16, :] = val[:, 128 * lt:128 * lt + 128]

    class Weights:
        def __init__(self, l, shared, direct):
            self.shared = shared is not None
            self.relays = (l, direct[0]) != (0, 20)
            db, nd = direct

            def straight(slot):
                return land.at[l, k, pl.ds(db, nd), slot]

            self.parts = [(straight, sems(7))]
            here, there = land.at[l, k, pl.ds(db, nd)], land.at[l, 1 - k, pl.ds(db, nd)]
            self.u = []
            if not self.shared:
                self.v = None
                self.base = sems(7)
                self.slot = lambda k_, slot: land.at[l, k_, pl.ds(db, nd), slot]
                return
            sb, ns = shared
            self.parts.append((lambda slot: land.at[l, k, pl.ds(sb + ns * y, ns), slot], sems(7)))
            self.v = [move(here, here, there, sib)]

            def block(y_, k_=k, half=None):
                ref = land.at[l, k_, pl.ds(sb + ns * y_, ns)]
                return ref if half is None else ref.at[:, pl.ds(4 * half, 4)]

            yp, ym, y2 = near(y, 1), near(y, -1), near(y, 2)
            self.u = [
                move(block(y), block(y), block(ym), Y(1)), move(block(y), block(y), block(yp), Y(-1)),
                move(block(ym, half=0), block(ym, half=0), block(y2, half=0), Y(1)),
                move(block(yp, half=1), block(yp, half=1), block(y2, half=1), Y(-1)),
            ]
            self.v += [move(block(y_), block(y_), block(y_, 1 - k), sib) for y_ in (y, ym, yp, y2)]

        def sends(self, part):
            ref, s = self.parts[part]
            if not self.relays:
                return [(rc(ref(mine), ref(mine), s + m - 1, shard(m)), slot(dminus(m)), s + m - 1, m - 1) for m in range(1, 8)]
            other = 2 * x + 1 - zl
            out = [
                (rc(ref(mine), ref(mine), s + o - 1, X(o)), 2 * near(x, -o) + zl, s + o - 1, o - 1) for o in (1, 2, 3)
            ]
            out.append((rc(ref(mine), ref(mine), s + 3, {"dp": (1 - zl) * 4 + x}), other, s + 3, 3))
            return out + [
                (rc(ref(other), ref(other), s + 3 + o, X(o)), 2 * near(x, -o) + 1 - zl, s + 3 + o, 3 + o)
                for o in (1, 2, 3)
            ]

        def one(self, part):
            for copy, *_ in self.sends(part)[:4 if self.relays else 7]:
                copy.start()

        def got(self, part, item):
            _, at, s, b = item
            ref = self.parts[part][0](at)
            rc(ref, ref, s, sib).wait_recv()
            if not self.shared:
                rc(ref, ref, self.base + b, sib).start()

        def relay(self, part):
            sends = self.sends(part)
            self.got(part, sends[3])
            for copy, *_ in sends[4:]:
                copy.start()

        def two(self, part):
            for n, item in enumerate(self.sends(part)):
                if not (self.relays and n == 3):
                    self.got(part, item)
            if part:
                starts(self.u[0], self.u[1], self.v[1])
            elif self.shared:
                starts(self.v[0])

        def three(self):
            recvs(self.u[0])
            starts(self.u[2], self.v[2])
            recvs(self.u[1])
            starts(self.u[3], self.v[3])

        def four(self):
            recvs(self.u[2], self.u[3])
            starts(self.v[4])

        def five(self):
            if self.shared:
                recvs(*self.v)
                sents(*self.u)
                sents(*self.v)

            for part in range(len(self.parts)):
                for copy, at, _, b in self.sends(part):
                    copy.wait_send()
                    if not self.shared:
                        got, gave = self.slot(1 - k, at), self.slot(k, at)
                        rc(got, got, self.base + b, sib).wait_recv()
                        rc(gave, gave, self.base + b, sib).wait_send()

    class Keys:
        def __init__(self, l):
            self.l, self.a, self.b, self.s = l, sems(21), sems(21), sems(3)

        def own(self, h):
            ref = kvl.at[self.l, i, k, h]
            return rc(ref, ref, self.s + h, sib)

        def out(self, h, m):
            ref = kvl.at[self.l, i, k, h]
            return rc(ref, ref, self.a + 7 * h + m - 1, chip(m))

        def passed(self, h, m, k_):
            ref = kvl.at[self.l, iminus(m), k_, h]
            return rc(ref, ref, self.b + 7 * h + m - 1, sib)

        def one(self, h):
            each(lambda m: self.out(h, m).start())
            self.own(h).start()

        def two(self, h):
            def go(m):
                ref = kvl.at[self.l, iminus(m), k, h]
                rc(ref, ref, self.a + 7 * h + m - 1, chip(m)).wait_recv()
                self.passed(h, m, k).start()
            each(go)

        def three(self, h):
            ref = kvl.at[self.l, i, 1 - k, h]
            rc(ref, ref, self.s + h, sib).wait_recv()
            self.own(h).wait_send()

            def go(m):
                self.passed(h, m, 1 - k).wait_recv()
                self.passed(h, m, k).wait_send()
                self.out(h, m).wait_send()
            each(go)

    class KeyGrads:
        def __init__(self, l):
            self.l, self.s, self.a = l, sems(3), sems(21)

        def pair(self, h):
            return rc(dkv.at[:, 1 - k, h], dkr0.at[self.l, :, h], self.s + h, sib)

        def out(self, h, m):
            return rc(dkv.at[iplus(m), k, h], dkr1.at[self.l, m - 1, h], self.a + 7 * h + m - 1, chip(m))

        def one(self, h):
            self.pair(h).start()

        def two(self, h):
            self.pair(h).wait()

            def go(m):
                j = iplus(m)
                total = dkv[j, k, h].astype(f32) + dkr0[self.l, j, h].astype(f32)
                dkv[j, k, h] = total.astype(bf16)
                self.out(h, m).start()

            each(go)

        def three(self, h):
            each(lambda m: self.out(h, m).wait())

        def total(self, h):
            val = dkv[i, k, h].astype(f32) + dkr0[self.l, i, h].astype(f32)
            for m in range(7):
                val = val + dkr1[self.l, m, h].astype(f32)
            return val

    class Grads:
        def __init__(self, l, early):
            self.l, self.early = l, early
            self.own = 16 + y + 4 * (i // 4)
            self.s = []
            for lo, n in ((0, 16),) if early else ((16, 4), (20, 4)):
                there = rs0.at[l, pl.ds(lo, n)]
                self.s.append(move(land.at[l, 1 - k, pl.ds(lo, n)], there, there, sib))
            self.r1, self.r2, self.fin = (r1e, r2e, fine) if early else (r1l, r2l, finl)
            self.a, self.b, self.c, self.v, self.z = sems(12), sems(7), sems(7), sems(7), sems(1)
            own = self.fin.at[l, i, k]
            self.t = move(own, own, self.fin.at[l, i, 1 - k], sib)

        def out1(self, m):
            l = self.l
            if self.early:
                h, o = (m - 1) // 3, lax.rem(m - 1, 3)
                x_ = near(x, o + 1)
                src, to = land.at[l, k, pl.ds(8 * h, 8), pl.ds(2 * x_, 2)], {"dp": zl * 4 + x_}
                return rc(src, r1e.at[l, o, pl.ds(8 * h, 8)], self.a + m - 1, to)
            h, o = (m - 1) // 3, lax.rem(m - 1, 3)
            y_ = near(y, o + 1)
            to = {"ctx": ((i // 4) * 4 + y_) * 2 + k}
            return rc(land.at[l, k, 16 + 4 * h + y_], r1l.at[l, o, h], self.a + m - 1, to)

        def outz(self):
            if not self.early:
                src = land.at[self.l, k, 16 + y + 4 * (1 - i // 4)]
                return rc(src, rzl.at[self.l], self.z, {"ctx": ((1 - i // 4) * 4 + y) * 2 + k})
            src = land.at[self.l, k, pl.ds(0, 16), 2 * x + 1 - zl]
            return rc(src, rz.at[self.l], self.z, {"dp": 4 * (1 - zl) + x})

        def out2(self, m):
            l = self.l
            if self.early:
                src, to = land.at[l, k, pl.ds(2 * iplus(m), 2), mine], chip(m)
            else:
                src, to = land.at[l, k, self.own, slot(dplus(m))], shard(m)
            return rc(src, self.r2.at[l, m - 1], self.b + m - 1, to)

        def zero(self, part=0):
            starts(self.s[part])

        def one(self, part=0):
            recvs(self.s[part])
            l = self.l

            def go(u):
                total = land[l, k, u].astype(f32) + rs0[l, u].astype(f32)
                land[l, k, u] = total.astype(bf16)

            each(go, *((0, 16) if self.early else (16 + 4 * part, 20 + 4 * part)))

        def send(self, lo=1, hi=None):
            each(lambda m: self.out1(m).start(), lo, hi or 7)

        def two(self):
            each(lambda m: self.out1(m).wait(), 1, 7)
            l = self.l
            if self.early:
                def go(u):
                    total = land[l, k, u, pl.ds(2 * x, 2)].astype(f32)
                    for o in range(3):
                        total = total + r1e[l, o, u].astype(f32)
                    land[l, k, u, pl.ds(2 * x, 2)] = total.astype(bf16)

                each(go, 0, 16)
            else:
                def go(u):
                    for q in range(2):
                        total = land[l, k, 16 + y + 4 * q, u].astype(f32)
                        for m in range(3):
                            total = total + r1l[l, m, q, u].astype(f32)
                        land[l, k, 16 + y + 4 * q, u] = total.astype(bf16)

                each(go, 0, 8)
            self.outz().start()

        def pair(self):
            self.outz().wait()
            l = self.l

            def go(u):
                if self.early:
                    land[l, k, u, mine] = (land[l, k, u, mine].astype(f32) + rz[l, u].astype(f32)).astype(bf16)
                else:
                    total = land[l, k, self.own, u].astype(f32) + rzl[l, u].astype(f32)
                    land[l, k, self.own, u] = total.astype(bf16)

            each(go, 0, 16 if self.early else 8)
            each(lambda m: self.out2(m).start())

        def three(self):
            each(lambda m: self.out2(m).wait())
            l = self.l
            for u in range(2 if self.early else 1):
                total = (land[l, k, 2 * i + u, mine] if self.early else land[l, k, self.own, mine]).astype(f32)
                for m in range(7):
                    total = total + (self.r2[l, m, u] if self.early else self.r2[l, m]).astype(f32)
                self.fin[l, i, k, u] = total.astype(bf16)
            own = self.fin.at[l, i, k]
            each(lambda m: rc(own, own, self.c + m - 1, chip(m)).start())
            starts(self.t)

        def four(self):
            def go(m):
                ref = self.fin.at[self.l, iminus(m), k]
                rc(ref, ref, self.c + m - 1, chip(m)).wait_recv()
                rc(ref, ref, self.v + m - 1, sib).start()
            each(go)

        def five(self):
            l = self.l
            recvs(self.t)
            sents(self.t, *self.s)

            def go(m):
                got, gave = self.fin.at[l, iminus(m), 1 - k], self.fin.at[l, iminus(m), k]
                own = self.fin.at[l, i, k]
                rc(got, got, self.v + m - 1, sib).wait_recv()
                rc(gave, gave, self.v + m - 1, sib).wait_send()
                rc(own, own, self.c + m - 1, chip(m)).wait_send()
            each(go)

    weights = {
        (0, "A"): Weights(0, None, (20, 4)), (0, "O"): Weights(0, None, (18, 2)), (0, "F"): Weights(0, (0, 3), (12, 6)),
        (1, "A"): Weights(1, (18, 1), (22, 2)), (1, "F"): Weights(1, (0, 3), (12, 6)),
    }
    keys = [Keys(l) for l in range(LAYERS)]
    key_grads = [KeyGrads(l) for l in range(LAYERS)]
    grads = {(l, e): Grads(l, e) for l in range(LAYERS) for e in (True, False)}

    barrier = pltpu.get_barrier_semaphore()

    def hello(m):
        pl.semaphore_signal(barrier, inc=1, device_id=shard(m), device_id_type=MESH)
        pl.semaphore_signal(barrier, inc=1, device_id=chip(m), device_id_type=MESH)

    each(hello)
    pl.semaphore_signal(barrier, inc=1, device_id=sib, device_id_type=MESH)
    pack_attn(0)
    pl.semaphore_wait(barrier, 15)
    weights[0, "A"].one(0)
    pack_ffn(0)
    weights[0, "F"].one(1)
    pack_attn(1)
    pack_ffn(1)

    lane = lax.broadcasted_iota(jnp.int32, (128, 128), 1)
    low_half = lane < 64
    first_quarter = lax.rem(lane, 64) < 32
    place_own = pos[pl.ds(c, 1), :].astype(f32)
    angle = jnp.broadcast_to(place_own, (128, 128)).T * freq[...]
    cos_q = jnp.cos(angle)
    sin_q = jnp.sin(angle) * jnp.where(first_quarter, -1.0, 1.0)
    low = jnp.where(pos[:, 0:1] <= pos[pl.ds(c, 1), 0:1], 1.0, 0.0)
    for s in range(NC):
        mlow[64 * s:64 * s + 64, :] = jnp.broadcast_to(low[s:s + 1, :], (64, 128)).astype(bf16)
    row = lax.broadcasted_iota(jnp.int32, (D, PD), 0)
    col = lax.broadcasted_iota(jnp.int32, (D, PD), 1)
    shard_of = (row * 911) >> 16
    e1[...] = jnp.where(
        col == row - 72 * shard_of + R * ((shard_of & 3) * 2 + (shard_of >> 2)), 1.0, 0.0
    ).astype(bf16)
    row = lax.broadcasted_iota(jnp.int32, (PD, 128 * HEADS), 0)
    col = lax.broadcasted_iota(jnp.int32, (PD, 128 * HEADS), 1)
    at_slot = (row * 205) >> 14
    natural = row - R * at_slot + 72 * ((at_slot & 1) * 4 + (at_slot >> 1))
    hit = (row - R * at_slot < 72) & (col == 128 * (natural >> 6) + 64 + (natural & 63))
    e2[...] = jnp.where(hit, 1.0, 0.0).astype(bf16)
    cos_kv = jnp.where(low_half, cos_q, 1.0)
    sin_kv = jnp.where(low_half, sin_q, 0.0)

    def swap(x):
        return jnp.where(first_quarter, pltpu.roll(x, 96, axis=1), pltpu.roll(x, 32, axis=1))

    row = lax.broadcasted_iota(jnp.int32, (1024, 192), 0) - 64 * c
    col = lax.rem(lax.broadcasted_iota(jnp.int32, (1024, 192), 1), 64)
    bias[...] = jnp.where((row > col) & (row < 64), NEG, 0.0).astype(bf16)
    mk[...] = jnp.concatenate([mlow[...], mlow[:, 0:64]], axis=1).astype(f32)
    row = lax.broadcasted_iota(jnp.int32, (64, 192), 0)
    col = lax.rem(lax.broadcasted_iota(jnp.int32, (64, 192), 1), 64)
    tri = jnp.where(row > col, NEG, 0.0)
    zpad[...] = jnp.zeros((128, PD), bf16)

    def place(u):
        if isinstance(u, int) and u >= 36:
            return attn_place(u - 36)
        return lax.rem(u, 12) // 6, 6 * (u // 12) + lax.rem(u, 6)

    def unit(l, u):
        return land[(l, *place(u))].reshape(PD, 128)

    def pair(l, u):
        return jnp.concatenate([unit(l, u), unit(l, u + 1)], axis=1)

    def units(l, u, n):
        return jnp.concatenate([unit(l, u + j) for j in range(n)], axis=1)

    def norm_scale(h):
        return lax.rsqrt(jnp.mean(h * h, axis=-1, keepdims=True) + eps_norm)

    def spread(x):
        return nn(x.astype(bf16), e1[...]).astype(bf16)

    def unspread(x):
        hi = x.astype(bf16)
        lo = (x - hi.astype(f32)).astype(bf16)
        return nt(hi, e1[...]) + nt(lo, e1[...])

    def set_unit(l, u, val):
        land[(l, *place(u))] = val.reshape(8, R, 128)

    def load_gains(l):
        total = jnp.zeros((8, PD), f32)
        for s in range(ND):
            part = land[l, 0, 20, slot_of(s)].astype(f32)[72:80, :]
            wide = jnp.concatenate([part, jnp.zeros((8, PD - 128), f32)], axis=1)
            total = total + (pltpu.roll(wide, 72 * s, axis=1) if s else wide)
        gain[l] = total

    def down_pieces(l, f):
        def go(g):
            for k_ in range(2):
                for s in range(ND):
                    for lt in range(5):
                        f(
                            wd.at[12 * s + 6 * k_ + g, :, 128 * lt:128 * lt + 128],
                            land.at[l, k_, 12 + g, slot_of(s), 16 * lt:16 * lt + 16, :],
                        )
        each(go, 0, 6)

    def regroup_down(l):
        def go(rows, piece):
            rows[...] = piece[...]
        down_pieces(l, go)

    def scatter_down(l):
        def go(rows, piece):
            piece[...] = rows[...]
        down_pieces(l, go)

    def down(t):
        return wd[pl.ds(16 * t, 16)].reshape(256, PD)

    def tiles(l, h, j):
        tlo = kvl[l, pl.ds(2 * j, 2), :, h, 0].reshape(256, 128)
        thi = kvl[l, pl.ds(2 * j, 2), :, h, 1].reshape(256, 128)
        m = mlow[pl.ds(pl.multiple_of(256 * j, 256), 256), :]
        x2 = jnp.concatenate([tlo * m, thi * (1 - m)], axis=1)
        return tlo, x2, m

    def swiglu_parts(l, t, x):
        g = nn(x, pair(l, 2 * t))
        u = nn(x, pair(l, 12 + 2 * t))
        return g, u

    def forward(l, h):
        hs[l] = h
        if l == 0:
            weights[0, "A"].two(0)
        weights[l, "A"].five()
        if l == 0:
            weights[0, "F"].relay(1)
        load_gains(l)
        apad[l] = spread(h * norm_scale(h) * gain[l, 0:1, 0:D])
        a = apad[l]
        for s in range(KV_HEADS):
            kv = nn(a, unit(l, 45 + s))
            kv = kv * cos_kv + swap(kv) * sin_kv
            kvl[l, i, k, s] = kv.astype(bf16).reshape(2, 64, 128)
            keys[l].one(s)
        if l == 0:
            weights[0, "O"].one(0)
            weights[0, "F"].one(0)
        else:
            weights[1, "F"].two(1)
        for t in range(5):
            q = nn(a, unit(l, 40 + t))
            q = (q * cos_q + swap(q) * sin_q) * HEAD_DIM ** (-0.5)
            for j in ((2 * t - 1, 2 * t) if t else (0,)):
                part = q if j % 2 else pltpu.roll(q, 64, axis=1)
                part = jnp.where(low_half, part, 0.0).astype(bf16)
                g = j % 3
                qc[l, j // 3, 64 * g:64 * g + 64, 0:128] = part[0:64]
                qc[l, j // 3, 64 * g:64 * g + 64, 128:256] = part[64:128]
        keys[l].two(0)
        if l == 0:
            weights[0, "F"].two(1)

        def head(s):
            keys[l].three(s)

            @pl.when(s < KV_HEADS - 1)
            def _():
                keys[l].two(s + 1)

            qcat = qc[l, s]
            qT = qcat.astype(f32).T.astype(bf16)
            qhT = qT[128:256]
            top_own = kvl[l, i, k, s, 1]
            se = nn(top_own, qhT) + tri

            def scores(j, carry):
                ml, mh = carry
                tlo, x2, _ = tiles(l, s, j)
                at = pl.ds(pl.multiple_of(256 * j, 256), 256)
                a1 = nn(tlo, qhT)
                a2 = nn(x2, qT) + bias[at, :].astype(f32)
                s1[at, 0:192] = a1
                s2[at, 0:192] = a2
                is_low = mk[at, :] > 0.5
                ml = jnp.maximum(ml, jnp.max(jnp.where(is_low, a2, NEG), axis=0, keepdims=True))
                mh = jnp.maximum(
                    mh, jnp.max(jnp.maximum(a1, jnp.where(is_low, NEG, a2)), axis=0, keepdims=True)
                )
                return ml, mh

            ml, mh = lax.fori_loop(
                0, 4, scores,
                (jnp.full((1, 192), NEG, f32), jnp.max(se, axis=0, keepdims=True)),
            )
            pe = jnp.exp(se - mh)
            acc1[...] = tn(top_own, pe.astype(bf16))
            acc2[...] = jnp.zeros((256, 192), f32)

            def weigh(j, carry):
                ll, lh = carry
                tlo, x2, _ = tiles(l, s, j)
                at = pl.ds(pl.multiple_of(256 * j, 256), 256)
                is_low = mk[at, :] > 0.5
                p1 = jnp.exp(s1[at, 0:192] - mh)
                p2 = jnp.exp(s2[at, 0:192] - jnp.where(is_low, ml, mh))
                ll = ll + jnp.sum(jnp.where(is_low, p2, 0.0), axis=0, keepdims=True)
                lh = lh + jnp.sum(p1 + jnp.where(is_low, 0.0, p2), axis=0, keepdims=True)
                acc1[...] += tn(tlo, p1.astype(bf16))
                acc2[...] += tn(x2, p2.astype(bf16))
                return ll, lh

            ll, lh = lax.fori_loop(
                0, 4, weigh, (jnp.zeros((1, 192), f32), jnp.sum(pe, axis=0, keepdims=True))
            )
            olow = acc2[64:128, :] / ll
            ohigh = (acc2[192:256, :] + acc1[64:128, :]) / lh
            oT[l, s, 0:64, :] = olow
            oT[l, s, 64:128, :] = ohigh
            lse[l, s, 0:1, :] = ml + jnp.log(ll)
            lse[l, s, 1:2, :] = mh + jnp.log(lh)
            zero = jnp.zeros((64, 192), f32)
            tl = jnp.concatenate([zero, olow], axis=0).T.astype(bf16)
            th = jnp.concatenate([zero, ohigh], axis=0).T.astype(bf16)
            for g in range(3):
                oz[3 * s + g, 0:64, :] = tl[64 * g:64 * g + 64]
                oz[3 * s + g, 64:128, :] = th[64 * g:64 * g + 64]

            if l == 0:
                @pl.when(s == 0)
                def _():
                    weights[0, "O"].relay(0)
                    weights[0, "F"].relay(0)
                    weights[1, "A"].one(1)
                    weights[1, "A"].one(0)

                @pl.when(s == 1)
                def _():
                    weights[1, "A"].relay(1)
                    weights[1, "A"].relay(0)
                    weights[1, "F"].one(1)
                    weights[1, "F"].one(0)
            else:
                @pl.when(s == 1)
                def _():
                    weights[1, "F"].two(0)
                    weights[1, "F"].three()

        each(head, 0, KV_HEADS)
        if l == 0:
            weights[0, "F"].three()
            weights[0, "O"].two(0)
            weights[0, "F"].two(0)
            weights[0, "F"].four()
            weights[0, "O"].five()
        mixp[l] = nt(jnp.concatenate([oz[j] for j in range(HEADS)], axis=1), e2[...]).astype(bf16)
        out = nn(mixp[l], units(l, 36, 5))
        h1 = h + out[:, 0:D]
        h1s[l] = h1
        bpad[l] = spread(h1 * norm_scale(h1) * gain[l, 1:2, 0:D])
        if l == 0:
            weights[1, "A"].two(1)
            weights[1, "F"].relay(1)
            weights[1, "F"].relay(0)
        else:
            weights[1, "F"].four()
        weights[l, "F"].five()
        regroup_down(l)

        def ffn(t, total):
            g, u = swiglu_parts(l, t, bpad[l])
            if l == LAYERS - 1:
                s1[pl.ds(pl.multiple_of(128 * t, 128), 128), :] = g
                s2[pl.ds(pl.multiple_of(128 * t, 128), 128), :] = u
            m = (g / (1.0 + jnp.exp(-g)) * u).astype(bf16)
            mid[l, t] = m
            if l == 0:
                @pl.when(t == 3)
                def _():
                    weights[1, "A"].three()

            return total + nn(m, down(t))

        total = lax.fori_loop(0, 6, ffn, jnp.zeros((128, PD), f32))
        if l == 0:
            weights[1, "A"].two(0)
            weights[1, "A"].four()
        return h1 + total[:, 0:D]

    def norm_back(h, g, dn, gain_row):
        r = norm_scale(h)
        xn = h * r
        cc = dn * gain_row
        return (
            g + r * (cc - xn * jnp.mean(cc * xn, axis=-1, keepdims=True)),
            jnp.sum(dn * xn, axis=0, keepdims=True),
        )

    def backward(l, g):
        zpad[:, 0:D] = g.astype(bf16)
        if l < LAYERS - 1:
            regroup_down(l)
        bT = bpad[l].T

        def ffn(t, total):
            dz = zpad[...]
            if l == LAYERS - 1:
                at = pl.ds(pl.multiple_of(128 * t, 128), 128)
                ga, u = s1[at, :], s2[at, :]
            else:
                ga, u = swiglu_parts(l, t, bpad[l])
            dm = nt(dz, down(t))
            sg = 1.0 / (1.0 + jnp.exp(-ga))
            silu = ga * sg
            dg = (dm * u * (sg * (1.0 + ga * (1.0 - sg)))).astype(bf16)
            du = (dm * silu).astype(bf16)
            total = total + nt(dg, pair(l, 2 * t)) + nt(du, pair(l, 12 + 2 * t))
            wd[pl.ds(16 * t, 16)] = tn(mid[l, t], dz).astype(bf16).reshape(16, 16, PD)
            gw = nn(bT, dg).astype(bf16)
            set_unit(l, 2 * t, gw[:, 0:128])
            set_unit(l, 2 * t + 1, gw[:, 128:256])
            gw = nn(bT, du).astype(bf16)
            set_unit(l, 12 + 2 * t, gw[:, 0:128])
            set_unit(l, 13 + 2 * t, gw[:, 128:256])
            return total

        total = lax.fori_loop(0, 6, ffn, jnp.zeros((128, PD), f32))
        scatter_down(l)
        grads[l, True].zero()
        if l < LAYERS - 1:
            grads[l + 1, False].one(1)
            grads[l + 1, False].send(4, 7)
        dh1, dgain_ffn = norm_back(h1s[l], g, unspread(total), gain[l, 1:2, 0:D])
        zpad[:, 0:D] = dh1.astype(bf16)
        do = nt(zpad[...], units(l, 36, 5)).astype(bf16)
        go = nn(mixp[l].T, zpad[...]).astype(bf16)
        for t in range(4):
            set_unit(l, 36 + t, go[:, 128 * t:128 * t + 128])
        go4[...] = go[:, 512:640]
        grads[l, False].zero(0)
        for j in range(HEADS):
            part = nn(do, e2[:, 128 * j:128 * j + 128]).astype(bf16)
            gidx = j % 3
            doc[j // 3, 64 * gidx:64 * gidx + 64, 0:128] = part[0:64]
            doc[j // 3, 64 * gidx:64 * gidx + 64, 128:256] = part[64:128]

        def head(s):
            qcat = qc[l, s]
            qh = qcat[:, 128:256]
            qT = qcat.astype(f32).T.astype(bf16)
            qhT = qT[128:256]
            docat = doc[s]
            doh = docat[:, 128:256]
            doT = docat.astype(f32).T
            doTb = doT.astype(bf16)
            dohT = doTb[128:256]
            dl = jnp.sum(oT[l, s, 0:64, :] * doT[64:128, :], axis=0, keepdims=True)
            dh = jnp.sum(oT[l, s, 64:128, :] * doT[192:256, :], axis=0, keepdims=True)
            lsl = lse[l, s, 0:1, :]
            lsh = lse[l, s, 1:2, :]
            own = kvl[l, i, k, s, 1]
            pe = jnp.exp(nn(own, qhT) + tri - lsh)
            dse = (pe * (nn(own, dohT) - dh)).astype(bf16)
            dxe = nn(dse, qh) + nn(pe.astype(bf16), doh)
            acc1[...] = tn(own, dse)
            acc2[...] = jnp.zeros((256, 192), f32)

            def chunk(j):
                tlo, x2, m = tiles(l, s, j)
                at = pl.ds(pl.multiple_of(256 * j, 256), 256)
                is_low = mk[at, :] > 0.5
                p1 = jnp.exp(nn(tlo, qhT) - lsh)
                p2 = jnp.exp(nn(x2, qT) + bias[at, :].astype(f32) - jnp.where(is_low, lsl, lsh))
                ds1 = (p1 * (nn(tlo, dohT) - dh)).astype(bf16)
                ds2 = (p2 * (nn(x2, doTb) - jnp.where(is_low, dl, dh))).astype(bf16)
                p1 = p1.astype(bf16)
                p2 = p2.astype(bf16)
                dx1 = nn(ds1, qh) + nn(p1, doh)
                dx2 = nn(ds2, qcat) + nn(p2, docat)
                mf = m.astype(f32)
                lo = dx1 + mf * dx2[:, 0:128]
                hi = (1.0 - mf) * dx2[:, 128:256]
                dkv[pl.ds(2 * j, 2), :, s, 0] = lo.astype(bf16).reshape(2, 2, 64, 128)
                dkv[pl.ds(2 * j, 2), :, s, 1] = hi.astype(bf16).reshape(2, 2, 64, 128)
                acc1[...] += tn(tlo, ds1)
                acc2[...] += tn(x2, ds2)

            each(chunk, 0, 4)
            dkv[i, k, s, 1] = dxe.astype(bf16)
            zero = jnp.zeros((64, 192), f32)
            tl = jnp.concatenate([acc2[0:64, :], zero], axis=0).T
            th = jnp.concatenate([acc2[128:192, :] + acc1[0:64, :], zero], axis=0).T
            scale = HEAD_DIM ** (-0.5)
            for gidx in range(3):
                dqz[3 * s + gidx, 0:64, :] = tl[64 * gidx:64 * gidx + 64] * scale
                dqz[3 * s + gidx, 64:128, :] = th[64 * gidx:64 * gidx + 64] * scale

            kg.one(s)

            @pl.when(s == 0)
            def _():
                grads[l, True].one()
                grads[l, True].send()
                if l < LAYERS - 1:
                    grads[l + 1, True].two()

            @pl.when(s == 1)
            def _():
                kg.two(0)
                grads[l, False].one(0)

            @pl.when(s == 2)
            def _():
                kg.two(1)

        kg = key_grads[l]
        each(head, 0, KV_HEADS)
        kg.two(2)
        grads[l, False].send(1, 4)
        if l < LAYERS - 1:
            grads[l + 1, False].two()

        rot = []
        for j in range(HEADS):
            t = dqz[j]
            rot.append(t * cos_q - swap(t) * sin_q)
        dq = [pltpu.roll(rot[0], 64, axis=1).astype(bf16)]
        for t in range(1, 5):
            dq.append((rot[2 * t - 1] + pltpu.roll(rot[2 * t], 64, axis=1)).astype(bf16))
        dq = jnp.concatenate(dq, axis=1)
        aT = apad[l].T
        gq = nn(aT, dq).astype(bf16)
        for s in range(KV_HEADS):
            kg.three(s)
        if l < LAYERS - 1:
            grads[l + 1, True].pair()
        dkv_in = []
        for s in range(KV_HEADS):
            t = kg.total(s).reshape(128, 128)
            dkv_in.append((t * cos_kv - swap(t) * sin_kv).astype(bf16))
        dkv_in = jnp.concatenate(dkv_in, axis=1)
        da = nt(dq, units(l, 40, 5)) + nt(dkv_in, units(l, 45, 3))
        set_unit(l, 40, gq[:, 0:128] + go4[...])
        for t in range(1, 5):
            set_unit(l, 40 + t, gq[:, 128 * t:128 * t + 128])
        gkv = nn(aT, dkv_in).astype(bf16)
        for t in range(3):
            set_unit(l, 45 + t, gkv[:, 128 * t:128 * t + 128])
        dh, dgain_attn = norm_back(hs[l], dh1, unspread(da), gain[l, 0:1, 0:D])
        rows = jnp.concatenate([dgain_attn, dgain_ffn, jnp.zeros((6, D), f32)], axis=0)
        rows = jnp.concatenate([rows, jnp.zeros((8, PD - D), f32)], axis=1)
        for s in range(ND):
            part = (pltpu.roll(rows, PD - 72 * s, axis=1) if s else rows)[:, 0:128]
            keep = land[l, 0, 20, slot_of(s)].astype(f32)[0:72, :]
            land[l, 0, 20, slot_of(s)] = jnp.concatenate([keep, part], axis=0).astype(bf16)
        grads[l, False].zero(1)
        return dh

    h = hidT[...].astype(f32).T
    h = forward(0, h)
    h = forward(1, h)
    hout[...] = h.astype(bf16)
    g = backward(1, goutT[...].astype(f32).T)
    g = backward(0, g)
    ghid[...] = g
    grads[0, False].one(1)
    grads[0, False].send(4, 7)
    grads[1, False].pair()
    grads[1, True].three()
    grads[0, True].two()
    grads[0, False].two()
    grads[1, False].three()
    grads[1, True].four()
    grads[0, True].pair()
    grads[0, False].pair()
    grads[1, True].five()
    grads[1, False].four()
    grads[0, True].three()
    grads[0, False].three()
    grads[1, False].five()
    grads[0, True].four()
    grads[0, False].four()
    grads[0, True].five()
    grads[0, False].five()
    oute[...] = fine[...]
    outl[...] = finl[...]


def unpack(h, gh, early, late, houtT, ghidT, gag, gq, gk, gv, go, gfg, ggate, gup, gdown):
    houtT[...] = h[...].astype(f32).T.astype(bf16)
    ghidT[...] = gh[...].T
    for l in range(LAYERS):
        attn = [None] * 12
        for cc in range(NC):
            i_, k_ = cc // 2, cc % 2
            for j in (2 * i_, 2 * i_ + 1, 16 + i_ % 4 + 4 * (i_ // 4)):
                val = (early[l, i_, k_, j - 2 * i_] if j < 16 else late[l, i_, k_, 0]).astype(f32)
                kind, t = j // 6, 6 * k_ + j % 6
                cols = slice(128 * t, 128 * t + 128)
                if kind == 0:
                    ggate[l, :, cols] = val[0:72]
                elif kind == 1:
                    gup[l, :, cols] = val[0:72]
                elif kind == 2:
                    at = slice(16 * t, 16 * t + 16)
                    for lt in range(4):
                        gdown[l, at, 128 * lt:128 * lt + 128] = val[16 * lt:16 * lt + 16]
                    gdown[l, at, 512:576] = val[64:80, 0:64]
                else:
                    t = 2 * k_ + j - 18 if j < 20 else 4 + 4 * k_ + j - 20
                    attn[t] = val[0:72]
                    if t == 4:
                        gag[l:l + 1, :] = val[72:73, 0:72]
                        gfg[l:l + 1, :] = val[73:74, 0:72]
        attn = jnp.concatenate(attn, axis=1)
        go[l] = attn[:, 0:D]
        gq[l] = attn[:, D:2 * D]
        kv = [attn[:, 2 * D + 64 * j:2 * D + 64 * j + 64] for j in range(2 * KV_HEADS)]
        gk[l] = jnp.concatenate(kv[0::2], axis=1)
        gv[l] = jnp.concatenate(kv[1::2], axis=1)


def body(
    hidden_in, positions, attn_gain, w_query, w_key, w_value, w_output, ffn_gain, w_gate, w_up, w_down, grad_out
):
    half = HEAD_DIM // 2
    freq = jnp.exp(-jnp.log(rope_base) * (2.0 * jnp.arange(half, dtype=f32) / HEAD_DIM))
    freq = jnp.tile(freq, 4).reshape(1, 128)
    outs = pl.pallas_call(
        kernel,
        out_shape=(
            jax.ShapeDtypeStruct((ROWS, D), bf16),
            jax.ShapeDtypeStruct((ROWS, D), f32),
            jax.ShapeDtypeStruct((LAYERS, NCHIP, 2, 2, R, 128), bf16),
            jax.ShapeDtypeStruct((LAYERS, NCHIP, 2, 1, R, 128), bf16),
        ),
        in_specs=[pl.BlockSpec(memory_space=pltpu.VMEM)] * 13,
        out_specs=tuple([pl.BlockSpec(memory_space=pltpu.VMEM)] * 4),
        scratch_shapes=[
            pltpu.VMEM((NC * 64, 128), bf16),
            pltpu.VMEM((D, PD), bf16),
            pltpu.VMEM((PD, 128 * HEADS), bf16),
            pltpu.VMEM((LAYERS, 8, 128), f32),
            pltpu.VMEM((72, FF), bf16),
            pltpu.VMEM((LAYERS, 2, 24, ND, R, 128), bf16),
            pltpu.VMEM((96, 16, PD), bf16),
            pltpu.VMEM((LAYERS, NCHIP, 2, KV_HEADS, 2, 64, 128), bf16),
            pltpu.VMEM((NCHIP, 2, KV_HEADS, 2, 64, 128), bf16),
            pltpu.VMEM((LAYERS, NCHIP, KV_HEADS, 2, 64, 128), bf16),
            pltpu.VMEM((LAYERS, 7, KV_HEADS, 2, 64, 128), bf16),
            pltpu.VMEM((LAYERS, 24, ND, R, 128), bf16),
            pltpu.VMEM((LAYERS, 3, 16, 2, R, 128), bf16),
            pltpu.VMEM((LAYERS, 16, R, 128), bf16),
            pltpu.VMEM((LAYERS, 7, 2, R, 128), bf16),
            pltpu.VMEM((LAYERS, 3, 2, ND, R, 128), bf16),
            pltpu.VMEM((LAYERS, ND, R, 128), bf16),
            pltpu.VMEM((LAYERS, 7, R, 128), bf16),
            pltpu.VMEM((LAYERS, NCHIP, 2, 2, R, 128), bf16),
            pltpu.VMEM((LAYERS, NCHIP, 2, 1, R, 128), bf16),
            pltpu.VMEM((LAYERS, 6, 128, 256), bf16),
            pltpu.VMEM((LAYERS, 128, D), f32),
            pltpu.VMEM((LAYERS, 128, D), f32),
            pltpu.VMEM((LAYERS, 128, PD), bf16),
            pltpu.VMEM((LAYERS, 128, PD), bf16),
            pltpu.VMEM((LAYERS, 128, PD), bf16),
            pltpu.VMEM((LAYERS, KV_HEADS, 192, 256), bf16),
            pltpu.VMEM((KV_HEADS, 192, 256), bf16),
            pltpu.VMEM((LAYERS, KV_HEADS, 128, 192), f32),
            pltpu.VMEM((LAYERS, KV_HEADS, 8, 192), f32),
            pltpu.VMEM((HEADS, 128, 128), bf16),
            pltpu.VMEM((HEADS, 128, 128), f32),
            pltpu.VMEM((1024, 256), f32),
            pltpu.VMEM((1024, 256), f32),
            pltpu.VMEM((1024, 192), bf16),
            pltpu.VMEM((1024, 192), f32),
            pltpu.VMEM((128, PD), bf16),
            pltpu.VMEM((LAYERS, 8, PD), f32),
            pltpu.VMEM((128, 192), f32),
            pltpu.VMEM((256, 192), f32),
            pltpu.VMEM((PD, 128), bf16),
            pltpu.SemaphoreType.DMA((416,)),
            pltpu.SemaphoreType.DMA((416,)),
        ],
        compiler_params=pltpu.CompilerParams(
            collective_id=0, has_side_effects=True, vmem_limit_bytes=127 * 512 * 1024
        ),
    )(
        hidden_in.T, grad_out.T, positions.reshape(NC, ROWS), freq, attn_gain, ffn_gain,
        w_gate, w_up, w_down, w_output, w_query, w_key, w_value,
    )
    shapes = (
        (D, ROWS), (D, ROWS), (LAYERS, 72), (LAYERS, 72, D), (LAYERS, 72, KV_HEADS * HEAD_DIM),
        (LAYERS, 72, KV_HEADS * HEAD_DIM), (LAYERS, 72, D), (LAYERS, 72), (LAYERS, 72, FF), (LAYERS, 72, FF),
        (LAYERS, 192, D),
    )
    houtT, ghidT, *rest = pl.pallas_call(
        unpack,
        out_shape=[jax.ShapeDtypeStruct(shape, f32 if n else bf16) for n, shape in enumerate(shapes)],
        in_specs=[pl.BlockSpec(memory_space=pltpu.VMEM)] * 4,
        out_specs=[pl.BlockSpec(memory_space=pltpu.VMEM)] * 11,
        compiler_params=pltpu.CompilerParams(vmem_limit_bytes=127 * 512 * 1024),
    )(*outs)
    return (houtT.T, ghidT.T, *rest)


def solution(mesh):
    placed = (
        P(("dp", "ctx"), None),
        P("dp"),
        P(None, "dp"),
        P(None, "dp", None),
        P(None, "dp", None),
        P(None, "dp", None),
        P(None, "dp", None),
        P(None, "dp"),
        P(None, "dp", None),
        P(None, "dp", None),
        P(None, "dp", None),
        P(("dp", "ctx"), None),
    )
    out = (
        P(("dp", "ctx"), None),
        P(("dp", "ctx"), None),
        P(None, "dp"),
        P(None, "dp", None),
        P(None, "dp", None),
        P(None, "dp", None),
        P(None, "dp", None),
        P(None, "dp"),
        P(None, "dp", None),
        P(None, "dp", None),
        P(None, "dp", None),
    )
    return jax.shard_map(body, mesh=mesh, in_specs=placed, out_specs=out, check_vma=False)
```

```python
import jax
import jax.numpy as jnp
from jax import lax
from jax.experimental import pallas as pl
from jax.experimental.pallas import tpu as pltpu
from jax.sharding import PartitionSpec as P

D = 576
HEADS = 9
KV_HEADS = 3
HEAD_DIM = 64
FF = 1536
LAYERS = 2
ROWS = 128
ND = 8
NC = 16
NCHIP = 8
R = 80
PD = 640
MESH = pl.DeviceIdType.MESH
bf16 = jnp.bfloat16
f32 = jnp.float32
NEG = -1e30
eps_norm = 1e-05
rope_base = 100000.0


def nn(a, b):
    return lax.dot_general(a, b, (((1,), (0,)), ((), ())), preferred_element_type=f32)


def nt(a, b):
    return lax.dot_general(a, b, (((1,), (1,)), ((), ())), preferred_element_type=f32)


def tn(a, b):
    return lax.dot_general(a, b, (((0,), (0,)), ((), ())), preferred_element_type=f32)


class Move:
    def __init__(self, make, src, dst, inc, s, dev):
        self.out = lambda: make(src, dst, s, dev)
        self.inc = lambda: make(inc, inc, s, dev)

    def start(self):
        self.out().start()

    def recv(self):
        self.inc().wait_recv()

    def sent(self):
        self.out().wait_send()


def slot_of(shard):
    return (shard % 4) * 2 + shard // 4


def attn_place(t):
    return (t // 2, 18 + t % 2) if t < 4 else ((t - 4) // 4, 20 + (t - 4) % 4)


def kernel(
    hidT, goutT, pos, freq, again, fgain, wgate, wup, wdown, wo, wq, wk, wv,
    hout, ghid, oute, outl,
    mlow, e1, e2, gains, wattn,
    land, wd, kvl, dkv, dkr0, dkr1,
    rs0, r1e, rz, r2e, r1l, rzl, r2l, fine, finl,
    mid, hs, h1s, apad, bpad, mixp, qc, doc, oT, lse, oz, dqz,
    s1, s2, bias, mk, zpad, gain, acc1, acc2, go4,
    hv, gv, send, recv, leave,
):
    d = lax.axis_index("dp")
    c = lax.axis_index("ctx")
    k, y = lax.rem(c, 2), lax.rem(c // 2, 4)
    x, zl = lax.rem(d, 4), d // 4
    mine = 2 * x + zl
    i = c // 2
    sib = {"ctx": i * 2 + 1 - k}
    count = [0]

    def dplus(m):
        return lax.rem(d + m, ND)

    def dminus(m):
        return lax.rem(d - m + ND, ND)

    def iplus(m):
        return lax.rem(i + m, NCHIP)

    def iminus(m):
        return lax.rem(i - m + NCHIP, NCHIP)

    def shard(m):
        return {"dp": dplus(m)}

    def slot(j):
        return lax.rem(j, 4) * 2 + j // 4

    def chip(m):
        return {"ctx": iplus(m) * 2 + k}

    def near(at, o):
        return lax.rem(at + o + 4, 4)

    def X(o):
        return {"dp": zl * 4 + near(x, o)}

    def Y(o):
        return {"ctx": ((i // 4) * 4 + near(y, o)) * 2 + k}

    def rc(src, dst, s, to):
        return pltpu.make_async_remote_copy(
            src_ref=src, dst_ref=dst, send_sem=send.at[s], recv_sem=recv.at[s],
            device_id=to, device_id_type=MESH,
        )

    def sems(n):
        count[0] += n
        return count[0] - n

    def move(src, dst, inc, to, s=None):
        return Move(rc, src, dst, inc, sems(1) if s is None else s, to)

    def starts(*moves):
        for m in moves:
            m.start()

    def recvs(*moves):
        for m in moves:
            m.recv()

    def sents(*moves):
        for m in moves:
            m.sent()

    def each(f, lo=1, hi=8):
        def step(m, carry):
            f(m)
            return carry
        lax.fori_loop(lo, hi, step, 0)

    def put(l, j, val, last=None, k=k):
        last = jnp.zeros((8, 128), f32) if last is None else last
        land[l, k, j, mine] = jnp.concatenate([val.astype(f32), last], axis=0).astype(bf16)

    def column(t):
        return pl.ds(pl.multiple_of(128 * t, 128), 128)

    def pack_attn(l):
        key, value = wk[l].astype(f32), wv[l].astype(f32)
        parts = [wo[l].astype(f32), wq[l].astype(f32)]
        for h in range(KV_HEADS):
            parts += [key[:, 64 * h:64 * h + 64], value[:, 64 * h:64 * h + 64]]
        wattn[...] = jnp.concatenate(parts, axis=1).astype(bf16)
        gains[l] = jnp.zeros((8, 128), f32)
        gains[l, 0:1, 0:72] = again[l:l + 1, :].astype(f32)
        gains[l, 1:2, 0:72] = fgain[l:l + 1, :].astype(f32)
        if l == 0:
            for t in range(12):
                k_, j = attn_place(t)
                put(l, j, wattn[:, 128 * t:128 * t + 128], gains[l], k_)
        else:
            put(l, 18 + y, wattn[:, column(jnp.where(y < 2, 2 * k + y, 2 + 4 * k + y))], gains[l])
            put(l, 22, wattn[:, column(6 + 4 * k)])
            put(l, 23, wattn[:, column(7 + 4 * k)])

    def pack_ffn(l):
        @pl.when(y < 3)
        def _():
            for r in range(2):
                put(l, 2 * y + r, wgate[l, :, column(6 * k + 2 * y + r)])

        @pl.when(y == 3)
        def _():
            for r in range(2):
                put(l, 6 + r, wup[l, :, column(6 * k + r)])

        for r in range(2, 6):
            put(l, 6 + r, wup[l, :, column(6 * k + r)])
        for g in range(6):
            val = wdown[l, pl.ds(pl.multiple_of(16 * (6 * k + g), 16), 16), :]
            val = jnp.concatenate([val.astype(f32), jnp.zeros((16, 64), f32)], axis=1).astype(bf16)
            for lt in range(5):
                land[l, k, 12 + g, mine, 16 * lt:16 * lt + 16, :] = val[:, 128 * lt:128 * lt + 128]

    class Weights:
        def __init__(self, l, shared, direct):
            self.shared = shared is not None
            self.relays = (l, direct[0]) != (0, 20)
            db, nd = direct

            def straight(slot):
                return land.at[l, k, pl.ds(db, nd), slot]

            self.parts = [(straight, sems(7))]
            here, there = land.at[l, k, pl.ds(db, nd)], land.at[l, 1 - k, pl.ds(db, nd)]
            self.u = []
            if not self.shared:
                self.v = None
                self.base = sems(7)
                self.slot = lambda k_, slot: land.at[l, k_, pl.ds(db, nd), slot]
                return
            sb, ns = shared
            self.parts.append((lambda slot: land.at[l, k, pl.ds(sb + ns * y, ns), slot], sems(7)))
            self.v = [move(here, here, there, sib)]

            def block(y_, k_=k, half=None):
                ref = land.at[l, k_, pl.ds(sb + ns * y_, ns)]
                return ref if half is None else ref.at[:, pl.ds(4 * half, 4)]

            yp, ym, y2 = near(y, 1), near(y, -1), near(y, 2)
            self.u = [
                move(block(y), block(y), block(ym), Y(1)), move(block(y), block(y), block(yp), Y(-1)),
                move(block(ym, half=0), block(ym, half=0), block(y2, half=0), Y(1)),
                move(block(yp, half=1), block(yp, half=1), block(y2, half=1), Y(-1)),
            ]
            self.v += [move(block(y_), block(y_), block(y_, 1 - k), sib) for y_ in (y, ym, yp, y2)]

        def sends(self, part):
            ref, s = self.parts[part]
            if not self.relays:
                return [(rc(ref(mine), ref(mine), s + m - 1, shard(m)), slot(dminus(m)), s + m - 1, m - 1) for m in range(1, 8)]
            other = 2 * x + 1 - zl
            out = [
                (rc(ref(mine), ref(mine), s + o - 1, X(o)), 2 * near(x, -o) + zl, s + o - 1, o - 1) for o in (1, 2, 3)
            ]
            out.append((rc(ref(mine), ref(mine), s + 3, {"dp": (1 - zl) * 4 + x}), other, s + 3, 3))
            return out + [
                (rc(ref(other), ref(other), s + 3 + o, X(o)), 2 * near(x, -o) + 1 - zl, s + 3 + o, 3 + o)
                for o in (1, 2, 3)
            ]

        def one(self, part):
            sends = self.sends(part)
            for copy, *_ in [sends[3], *sends[:3]] if self.relays else sends:
                copy.start()

        def got(self, part, item):
            _, at, s, b = item
            ref = self.parts[part][0](at)
            rc(ref, ref, s, sib).wait_recv()
            if not self.shared:
                rc(ref, ref, self.base + b, sib).start()

        def relay(self, part):
            sends = self.sends(part)
            self.got(part, sends[3])
            for copy, *_ in sends[4:]:
                copy.start()

        def two(self, part):
            for n, item in enumerate(self.sends(part)):
                if not (self.relays and n == 3):
                    self.got(part, item)
            if part:
                starts(self.u[0], self.u[1], self.v[1])
            elif self.shared:
                starts(self.v[0])

        def three(self):
            recvs(self.u[0])
            starts(self.u[2], self.v[2])
            recvs(self.u[1])
            starts(self.u[3], self.v[3])

        def four(self):
            recvs(self.u[2], self.u[3])
            starts(self.v[4])

        def five(self):
            if self.shared:
                recvs(*self.v)
                sents(*self.u)
                sents(*self.v)

            for part in range(len(self.parts)):
                for copy, at, _, b in self.sends(part):
                    copy.wait_send()
                    if not self.shared:
                        got, gave = self.slot(1 - k, at), self.slot(k, at)
                        rc(got, got, self.base + b, sib).wait_recv()
                        rc(gave, gave, self.base + b, sib).wait_send()

    class Keys:
        def __init__(self, l):
            self.l, self.a, self.b, self.s = l, sems(21), sems(21), sems(3)

        def own(self, h):
            ref = kvl.at[self.l, i, k, h]
            return rc(ref, ref, self.s + h, sib)

        def out(self, h, m):
            ref = kvl.at[self.l, i, k, h]
            return rc(ref, ref, self.a + 7 * h + m - 1, chip(m))

        def passed(self, h, m, k_):
            ref = kvl.at[self.l, iminus(m), k_, h]
            return rc(ref, ref, self.b + 7 * h + m - 1, sib)

        def one(self, h):
            each(lambda m: self.out(h, m).start())
            self.own(h).start()

        def two(self, h):
            def go(m):
                ref = kvl.at[self.l, iminus(m), k, h]
                rc(ref, ref, self.a + 7 * h + m - 1, chip(m)).wait_recv()
                self.passed(h, m, k).start()
            each(go)

        def three(self, h):
            ref = kvl.at[self.l, i, 1 - k, h]
            rc(ref, ref, self.s + h, sib).wait_recv()
            self.own(h).wait_send()

            def go(m):
                self.passed(h, m, 1 - k).wait_recv()
                self.passed(h, m, k).wait_send()
                self.out(h, m).wait_send()
            each(go)

    class KeyGrads:
        def __init__(self, l):
            self.l, self.s, self.a = l, sems(3), sems(21)

        def pair(self, h):
            return rc(dkv.at[:, 1 - k, h], dkr0.at[self.l, :, h], self.s + h, sib)

        def out(self, h, m):
            return rc(dkv.at[iplus(m), k, h], dkr1.at[self.l, m - 1, h], self.a + 7 * h + m - 1, chip(m))

        def one(self, h):
            self.pair(h).start()

        def two(self, h):
            self.pair(h).wait()

            def go(m):
                j = iplus(m)
                total = dkv[j, k, h].astype(f32) + dkr0[self.l, j, h].astype(f32)
                dkv[j, k, h] = total.astype(bf16)
                self.out(h, m).start()

            each(go)

        def three(self, h):
            each(lambda m: self.out(h, m).wait())

        def total(self, h):
            val = dkv[i, k, h].astype(f32) + dkr0[self.l, i, h].astype(f32)
            for m in range(7):
                val = val + dkr1[self.l, m, h].astype(f32)
            return val

    class Grads:
        def __init__(self, l, early):
            self.l, self.early = l, early
            self.own = 16 + y + 4 * (i // 4)
            self.s = []
            for lo, n in ((0, 16),) if early else ((16, 4), (20, 4)):
                there = rs0.at[l, pl.ds(lo, n)]
                self.s.append(move(land.at[l, 1 - k, pl.ds(lo, n)], there, there, sib))
            self.r1, self.r2, self.fin = (r1e, r2e, fine) if early else (r1l, r2l, finl)
            self.a, self.b, self.c, self.v, self.z = sems(12), sems(7), sems(7), sems(7), sems(1)
            own = self.fin.at[l, i, k]
            self.t = move(own, own, self.fin.at[l, i, 1 - k], sib)

        def out1(self, m):
            l = self.l
            if self.early:
                h, o = (m - 1) // 3, lax.rem(m - 1, 3)
                x_ = near(x, o + 1)
                src, to = land.at[l, k, pl.ds(8 * h, 8), pl.ds(2 * x_, 2)], {"dp": zl * 4 + x_}
                return rc(src, r1e.at[l, o, pl.ds(8 * h, 8)], self.a + m - 1, to)
            h, o = (m - 1) // 3, lax.rem(m - 1, 3)
            y_ = near(y, o + 1)
            to = {"ctx": ((i // 4) * 4 + y_) * 2 + k}
            return rc(land.at[l, k, 16 + 4 * h + y_], r1l.at[l, o, h], self.a + m - 1, to)

        def outz(self):
            if not self.early:
                src = land.at[self.l, k, 16 + y + 4 * (1 - i // 4)]
                return rc(src, rzl.at[self.l], self.z, {"ctx": ((1 - i // 4) * 4 + y) * 2 + k})
            src = land.at[self.l, k, pl.ds(0, 16), 2 * x + 1 - zl]
            return rc(src, rz.at[self.l], self.z, {"dp": 4 * (1 - zl) + x})

        def out2(self, m):
            l = self.l
            if self.early:
                src, to = land.at[l, k, pl.ds(2 * iplus(m), 2), mine], chip(m)
            else:
                src, to = land.at[l, k, self.own, slot(dplus(m))], shard(m)
            return rc(src, self.r2.at[l, m - 1], self.b + m - 1, to)

        def zero(self, part=0):
            starts(self.s[part])

        def one(self, part=0):
            recvs(self.s[part])
            l = self.l

            def go(u):
                total = land[l, k, u].astype(f32) + rs0[l, u].astype(f32)
                land[l, k, u] = total.astype(bf16)

            each(go, *((0, 16) if self.early else (16 + 4 * part, 20 + 4 * part)))

        def send(self, lo=1, hi=None):
            each(lambda m: self.out1(m).start(), lo, hi or 7)

        def two(self):
            each(lambda m: self.out1(m).wait(), 1, 7)
            l = self.l
            if self.early:
                def go(u):
                    total = land[l, k, u, pl.ds(2 * x, 2)].astype(f32)
                    for o in range(3):
                        total = total + r1e[l, o, u].astype(f32)
                    land[l, k, u, pl.ds(2 * x, 2)] = total.astype(bf16)

                each(go, 0, 16)
            else:
                def go(u):
                    for q in range(2):
                        total = land[l, k, 16 + y + 4 * q, u].astype(f32)
                        for m in range(3):
                            total = total + r1l[l, m, q, u].astype(f32)
                        land[l, k, 16 + y + 4 * q, u] = total.astype(bf16)

                each(go, 0, 8)
            self.outz().start()

        def pair(self):
            self.outz().wait()
            l = self.l

            def go(u):
                if self.early:
                    land[l, k, u, mine] = (land[l, k, u, mine].astype(f32) + rz[l, u].astype(f32)).astype(bf16)
                else:
                    total = land[l, k, self.own, u].astype(f32) + rzl[l, u].astype(f32)
                    land[l, k, self.own, u] = total.astype(bf16)

            each(go, 0, 16 if self.early else 8)
            each(lambda m: self.out2(m).start())

        def three(self):
            each(lambda m: self.out2(m).wait())
            l = self.l
            for u in range(2 if self.early else 1):
                total = (land[l, k, 2 * i + u, mine] if self.early else land[l, k, self.own, mine]).astype(f32)
                for m in range(7):
                    total = total + (self.r2[l, m, u] if self.early else self.r2[l, m]).astype(f32)
                self.fin[l, i, k, u] = total.astype(bf16)
            own = self.fin.at[l, i, k]
            each(lambda m: rc(own, own, self.c + m - 1, chip(m)).start())
            starts(self.t)

        def four(self):
            def go(m):
                ref = self.fin.at[self.l, iminus(m), k]
                rc(ref, ref, self.c + m - 1, chip(m)).wait_recv()
                rc(ref, ref, self.v + m - 1, sib).start()
            each(go)

        def five(self):
            l = self.l
            recvs(self.t)
            sents(self.t, *self.s)

            def go(m):
                got, gave = self.fin.at[l, iminus(m), 1 - k], self.fin.at[l, iminus(m), k]
                own = self.fin.at[l, i, k]
                rc(got, got, self.v + m - 1, sib).wait_recv()
                rc(gave, gave, self.v + m - 1, sib).wait_send()
                rc(own, own, self.c + m - 1, chip(m)).wait_send()
            each(go)

    weights = {
        (0, "A"): Weights(0, None, (20, 4)), (0, "O"): Weights(0, None, (18, 2)), (0, "F"): Weights(0, (0, 2), (8, 10)),
        (1, "A"): Weights(1, (18, 1), (22, 2)), (1, "F"): Weights(1, (0, 2), (8, 10)),
    }
    keys = [Keys(l) for l in range(LAYERS)]
    key_grads = [KeyGrads(l) for l in range(LAYERS)]
    grads = {(l, e): Grads(l, e) for l in range(LAYERS) for e in (True, False)}

    barrier = pltpu.get_barrier_semaphore()

    def hello(m):
        pl.semaphore_signal(barrier, inc=1, device_id=shard(m), device_id_type=MESH)
        pl.semaphore_signal(barrier, inc=1, device_id=chip(m), device_id_type=MESH)

    each(hello)
    pl.semaphore_signal(barrier, inc=1, device_id=sib, device_id_type=MESH)
    pack_attn(0)
    pl.semaphore_wait(barrier, 15)
    weights[0, "A"].one(0)
    pack_ffn(0)
    weights[0, "F"].one(1)
    pack_attn(1)
    pack_ffn(1)

    lane = lax.broadcasted_iota(jnp.int32, (128, 128), 1)
    low_half = lane < 64
    first_quarter = lax.rem(lane, 64) < 32
    place_own = pos[pl.ds(c, 1), :].astype(f32)
    angle = jnp.broadcast_to(place_own, (128, 128)).T * freq[...]
    cos_q = jnp.cos(angle)
    sin_q = jnp.sin(angle) * jnp.where(first_quarter, -1.0, 1.0)
    low = jnp.where(pos[:, 0:1] <= pos[pl.ds(c, 1), 0:1], 1.0, 0.0)
    for s in range(NC):
        mlow[64 * s:64 * s + 64, :] = jnp.broadcast_to(low[s:s + 1, :], (64, 128)).astype(bf16)
    row = lax.broadcasted_iota(jnp.int32, (D, PD), 0)
    col = lax.broadcasted_iota(jnp.int32, (D, PD), 1)
    shard_of = (row * 911) >> 16
    e1[...] = jnp.where(
        col == row - 72 * shard_of + R * ((shard_of & 3) * 2 + (shard_of >> 2)), 1.0, 0.0
    ).astype(bf16)
    row = lax.broadcasted_iota(jnp.int32, (PD, 128 * HEADS), 0)
    col = lax.broadcasted_iota(jnp.int32, (PD, 128 * HEADS), 1)
    at_slot = (row * 205) >> 14
    natural = row - R * at_slot + 72 * ((at_slot & 1) * 4 + (at_slot >> 1))
    hit = (row - R * at_slot < 72) & (col == 128 * (natural >> 6) + 64 + (natural & 63))
    e2[...] = jnp.where(hit, 1.0, 0.0).astype(bf16)
    cos_kv = jnp.where(low_half, cos_q, 1.0)
    sin_kv = jnp.where(low_half, sin_q, 0.0)

    def swap(x):
        return jnp.where(first_quarter, pltpu.roll(x, 96, axis=1), pltpu.roll(x, 32, axis=1))

    row = lax.broadcasted_iota(jnp.int32, (1024, 192), 0) - 64 * c
    col = lax.rem(lax.broadcasted_iota(jnp.int32, (1024, 192), 1), 64)
    bias[...] = jnp.where((row > col) & (row < 64), NEG, 0.0).astype(bf16)
    mk[...] = jnp.concatenate([mlow[...], mlow[:, 0:64]], axis=1).astype(f32)
    row = lax.broadcasted_iota(jnp.int32, (64, 192), 0)
    col = lax.rem(lax.broadcasted_iota(jnp.int32, (64, 192), 1), 64)
    tri = jnp.where(row > col, NEG, 0.0)
    zpad[...] = jnp.zeros((128, PD), bf16)

    def place(u):
        if isinstance(u, int) and u >= 36:
            return attn_place(u - 36)
        return lax.rem(u, 12) // 6, 6 * (u // 12) + lax.rem(u, 6)

    def unit(l, u):
        return land[(l, *place(u))].reshape(PD, 128)

    def pair(l, u):
        return jnp.concatenate([unit(l, u), unit(l, u + 1)], axis=1)

    def units(l, u, n):
        return jnp.concatenate([unit(l, u + j) for j in range(n)], axis=1)

    def norm_scale(h):
        return lax.rsqrt(jnp.mean(h * h, axis=-1, keepdims=True) + eps_norm)

    def spread(x):
        return nn(x.astype(bf16), e1[...]).astype(bf16)

    def unspread(x):
        hi = x.astype(bf16)
        lo = (x - hi.astype(f32)).astype(bf16)
        return nt(hi, e1[...]) + nt(lo, e1[...])

    def set_unit(l, u, val):
        land[(l, *place(u))] = val.reshape(8, R, 128)

    def load_gains(l):
        total = jnp.zeros((8, PD), f32)
        for s in range(ND):
            part = land[l, 0, 20, slot_of(s)].astype(f32)[72:80, :]
            wide = jnp.concatenate([part, jnp.zeros((8, PD - 128), f32)], axis=1)
            total = total + (pltpu.roll(wide, 72 * s, axis=1) if s else wide)
        gain[l] = total

    def down_pieces(l, f):
        def go(g):
            for k_ in range(2):
                for s in range(ND):
                    for lt in range(5):
                        f(
                            wd.at[12 * s + 6 * k_ + g, :, 128 * lt:128 * lt + 128],
                            land.at[l, k_, 12 + g, slot_of(s), 16 * lt:16 * lt + 16, :],
                        )
        each(go, 0, 6)

    def regroup_down(l):
        def go(rows, piece):
            rows[...] = piece[...]
        down_pieces(l, go)

    def scatter_down(l):
        def go(rows, piece):
            piece[...] = rows[...]
        down_pieces(l, go)

    def down(t):
        return wd[pl.ds(16 * t, 16)].reshape(256, PD)

    def tiles(l, h, j):
        tlo = kvl[l, pl.ds(2 * j, 2), :, h, 0].reshape(256, 128)
        thi = kvl[l, pl.ds(2 * j, 2), :, h, 1].reshape(256, 128)
        m = mlow[pl.ds(pl.multiple_of(256 * j, 256), 256), :]
        x2 = jnp.concatenate([tlo * m, thi * (1 - m)], axis=1)
        return tlo, x2, m

    def swiglu_parts(l, t, x):
        g = nn(x, pair(l, 2 * t))
        u = nn(x, pair(l, 12 + 2 * t))
        return g, u

    def forward(l, h):
        hs[l] = h
        if l == 0:
            weights[0, "A"].two(0)
        weights[l, "A"].five()
        if l == 0:
            weights[0, "F"].relay(1)
        load_gains(l)
        apad[l] = spread(h * norm_scale(h) * gain[l, 0:1, 0:D])
        a = apad[l]
        for s in range(KV_HEADS):
            kv = nn(a, unit(l, 45 + s))
            kv = kv * cos_kv + swap(kv) * sin_kv
            kvl[l, i, k, s] = kv.astype(bf16).reshape(2, 64, 128)
            keys[l].one(s)
        if l == 0:
            weights[0, "O"].one(0)
            weights[0, "F"].one(0)
        else:
            weights[1, "F"].two(1)
        for t in range(5):
            q = nn(a, unit(l, 40 + t))
            q = (q * cos_q + swap(q) * sin_q) * HEAD_DIM ** (-0.5)
            for j in ((2 * t - 1, 2 * t) if t else (0,)):
                part = q if j % 2 else pltpu.roll(q, 64, axis=1)
                part = jnp.where(low_half, part, 0.0).astype(bf16)
                g = j % 3
                qc[l, j // 3, 64 * g:64 * g + 64, 0:128] = part[0:64]
                qc[l, j // 3, 64 * g:64 * g + 64, 128:256] = part[64:128]
        keys[l].two(0)
        if l == 0:
            weights[0, "F"].two(1)

        def head(s):
            keys[l].three(s)

            @pl.when(s < KV_HEADS - 1)
            def _():
                keys[l].two(s + 1)

            qcat = qc[l, s]
            qT = qcat.astype(f32).T.astype(bf16)
            qhT = qT[128:256]
            top_own = kvl[l, i, k, s, 1]
            se = nn(top_own, qhT) + tri

            def scores(j, carry):
                ml, mh = carry
                tlo, x2, _ = tiles(l, s, j)
                at = pl.ds(pl.multiple_of(256 * j, 256), 256)
                a1 = nn(tlo, qhT)
                a2 = nn(x2, qT) + bias[at, :].astype(f32)
                s1[at, 0:192] = a1
                s2[at, 0:192] = a2
                is_low = mk[at, :] > 0.5
                ml = jnp.maximum(ml, jnp.max(jnp.where(is_low, a2, NEG), axis=0, keepdims=True))
                mh = jnp.maximum(
                    mh, jnp.max(jnp.maximum(a1, jnp.where(is_low, NEG, a2)), axis=0, keepdims=True)
                )
                return ml, mh

            ml, mh = lax.fori_loop(
                0, 4, scores,
                (jnp.full((1, 192), NEG, f32), jnp.max(se, axis=0, keepdims=True)),
            )
            pe = jnp.exp(se - mh)
            acc1[...] = tn(top_own, pe.astype(bf16))
            acc2[...] = jnp.zeros((256, 192), f32)

            def weigh(j, carry):
                ll, lh = carry
                tlo, x2, _ = tiles(l, s, j)
                at = pl.ds(pl.multiple_of(256 * j, 256), 256)
                is_low = mk[at, :] > 0.5
                p1 = jnp.exp(s1[at, 0:192] - mh)
                p2 = jnp.exp(s2[at, 0:192] - jnp.where(is_low, ml, mh))
                ll = ll + jnp.sum(jnp.where(is_low, p2, 0.0), axis=0, keepdims=True)
                lh = lh + jnp.sum(p1 + jnp.where(is_low, 0.0, p2), axis=0, keepdims=True)
                acc1[...] += tn(tlo, p1.astype(bf16))
                acc2[...] += tn(x2, p2.astype(bf16))
                return ll, lh

            ll, lh = lax.fori_loop(
                0, 4, weigh, (jnp.zeros((1, 192), f32), jnp.sum(pe, axis=0, keepdims=True))
            )
            olow = acc2[64:128, :] / ll
            ohigh = (acc2[192:256, :] + acc1[64:128, :]) / lh
            oT[l, s, 0:64, :] = olow
            oT[l, s, 64:128, :] = ohigh
            lse[l, s, 0:1, :] = ml + jnp.log(ll)
            lse[l, s, 1:2, :] = mh + jnp.log(lh)
            zero = jnp.zeros((64, 192), f32)
            tl = jnp.concatenate([zero, olow], axis=0).T.astype(bf16)
            th = jnp.concatenate([zero, ohigh], axis=0).T.astype(bf16)
            for g in range(3):
                oz[3 * s + g, 0:64, :] = tl[64 * g:64 * g + 64]
                oz[3 * s + g, 64:128, :] = th[64 * g:64 * g + 64]

            if l == 0:
                @pl.when(s == 0)
                def _():
                    weights[0, "O"].relay(0)
                    weights[0, "F"].relay(0)
                    weights[1, "A"].one(1)
                    weights[1, "A"].one(0)

                @pl.when(s == 1)
                def _():
                    weights[1, "A"].relay(1)
                    weights[1, "A"].relay(0)
                    weights[1, "F"].one(1)
                    weights[1, "F"].one(0)
            else:
                @pl.when(s == 1)
                def _():
                    weights[1, "F"].two(0)
                    weights[1, "F"].three()

        each(head, 0, KV_HEADS)
        if l == 0:
            weights[0, "F"].three()
            weights[0, "O"].two(0)
            weights[0, "F"].two(0)
            weights[0, "F"].four()
            weights[0, "O"].five()
        mixp[l] = nt(jnp.concatenate([oz[j] for j in range(HEADS)], axis=1), e2[...]).astype(bf16)
        out = nn(mixp[l], units(l, 36, 5))
        h1 = h + out[:, 0:D]
        h1s[l] = h1
        bpad[l] = spread(h1 * norm_scale(h1) * gain[l, 1:2, 0:D])
        if l == 0:
            weights[1, "A"].two(1)
            weights[1, "F"].relay(1)
            weights[1, "F"].relay(0)
        else:
            weights[1, "F"].four()
        weights[l, "F"].five()
        regroup_down(l)

        def ffn(t, total):
            g, u = swiglu_parts(l, t, bpad[l])
            if l == LAYERS - 1:
                s1[pl.ds(pl.multiple_of(128 * t, 128), 128), :] = g
                s2[pl.ds(pl.multiple_of(128 * t, 128), 128), :] = u
            m = (g / (1.0 + jnp.exp(-g)) * u).astype(bf16)
            mid[l, t] = m
            if l == 0:
                @pl.when(t == 3)
                def _():
                    weights[1, "A"].three()

            return total + nn(m, down(t))

        total = lax.fori_loop(0, 6, ffn, jnp.zeros((128, PD), f32))
        if l == 0:
            weights[1, "A"].two(0)
            weights[1, "A"].four()
        return h1 + total[:, 0:D]

    def norm_back(h, g, dn, gain_row):
        r = norm_scale(h)
        xn = h * r
        cc = dn * gain_row
        return (
            g + r * (cc - xn * jnp.mean(cc * xn, axis=-1, keepdims=True)),
            jnp.sum(dn * xn, axis=0, keepdims=True),
        )

    def backward(l, g):
        zpad[:, 0:D] = g.astype(bf16)
        if l < LAYERS - 1:
            regroup_down(l)
        bT = bpad[l].T

        def ffn(t, total):
            dz = zpad[...]
            if l == LAYERS - 1:
                at = pl.ds(pl.multiple_of(128 * t, 128), 128)
                ga, u = s1[at, :], s2[at, :]
            else:
                ga, u = swiglu_parts(l, t, bpad[l])
            dm = nt(dz, down(t))
            sg = 1.0 / (1.0 + jnp.exp(-ga))
            silu = ga * sg
            dg = (dm * u * (sg * (1.0 + ga * (1.0 - sg)))).astype(bf16)
            du = (dm * silu).astype(bf16)
            total = total + nt(dg, pair(l, 2 * t)) + nt(du, pair(l, 12 + 2 * t))
            wd[pl.ds(16 * t, 16)] = tn(mid[l, t], dz).astype(bf16).reshape(16, 16, PD)
            gw = nn(bT, dg).astype(bf16)
            set_unit(l, 2 * t, gw[:, 0:128])
            set_unit(l, 2 * t + 1, gw[:, 128:256])
            gw = nn(bT, du).astype(bf16)
            set_unit(l, 12 + 2 * t, gw[:, 0:128])
            set_unit(l, 13 + 2 * t, gw[:, 128:256])
            return total

        total = lax.fori_loop(0, 6, ffn, jnp.zeros((128, PD), f32))
        scatter_down(l)
        grads[l, True].zero()
        if l < LAYERS - 1:
            grads[l + 1, False].one(1)
            grads[l + 1, False].send(4, 7)
        dh1, dgain_ffn = norm_back(h1s[l], g, unspread(total), gain[l, 1:2, 0:D])
        zpad[:, 0:D] = dh1.astype(bf16)
        do = nt(zpad[...], units(l, 36, 5)).astype(bf16)
        go = nn(mixp[l].T, zpad[...]).astype(bf16)
        for t in range(4):
            set_unit(l, 36 + t, go[:, 128 * t:128 * t + 128])
        go4[...] = go[:, 512:640]
        grads[l, False].zero(0)
        for j in range(HEADS):
            part = nn(do, e2[:, 128 * j:128 * j + 128]).astype(bf16)
            gidx = j % 3
            doc[j // 3, 64 * gidx:64 * gidx + 64, 0:128] = part[0:64]
            doc[j // 3, 64 * gidx:64 * gidx + 64, 128:256] = part[64:128]

        def head(s):
            qcat = qc[l, s]
            qh = qcat[:, 128:256]
            qT = qcat.astype(f32).T.astype(bf16)
            qhT = qT[128:256]
            docat = doc[s]
            doh = docat[:, 128:256]
            doT = docat.astype(f32).T
            doTb = doT.astype(bf16)
            dohT = doTb[128:256]
            dl = jnp.sum(oT[l, s, 0:64, :] * doT[64:128, :], axis=0, keepdims=True)
            dh = jnp.sum(oT[l, s, 64:128, :] * doT[192:256, :], axis=0, keepdims=True)
            lsl = lse[l, s, 0:1, :]
            lsh = lse[l, s, 1:2, :]
            own = kvl[l, i, k, s, 1]
            pe = jnp.exp(nn(own, qhT) + tri - lsh)
            dse = (pe * (nn(own, dohT) - dh)).astype(bf16)
            dxe = nn(dse, qh) + nn(pe.astype(bf16), doh)
            acc1[...] = tn(own, dse)
            acc2[...] = jnp.zeros((256, 192), f32)

            def chunk(j):
                tlo, x2, m = tiles(l, s, j)
                at = pl.ds(pl.multiple_of(256 * j, 256), 256)
                is_low = mk[at, :] > 0.5
                p1 = jnp.exp(nn(tlo, qhT) - lsh)
                p2 = jnp.exp(nn(x2, qT) + bias[at, :].astype(f32) - jnp.where(is_low, lsl, lsh))
                ds1 = (p1 * (nn(tlo, dohT) - dh)).astype(bf16)
                ds2 = (p2 * (nn(x2, doTb) - jnp.where(is_low, dl, dh))).astype(bf16)
                p1 = p1.astype(bf16)
                p2 = p2.astype(bf16)
                dx1 = nn(ds1, qh) + nn(p1, doh)
                dx2 = nn(ds2, qcat) + nn(p2, docat)
                mf = m.astype(f32)
                lo = dx1 + mf * dx2[:, 0:128]
                hi = (1.0 - mf) * dx2[:, 128:256]
                dkv[pl.ds(2 * j, 2), :, s, 0] = lo.astype(bf16).reshape(2, 2, 64, 128)
                dkv[pl.ds(2 * j, 2), :, s, 1] = hi.astype(bf16).reshape(2, 2, 64, 128)
                acc1[...] += tn(tlo, ds1)
                acc2[...] += tn(x2, ds2)

            each(chunk, 0, 4)
            dkv[i, k, s, 1] = dxe.astype(bf16)
            zero = jnp.zeros((64, 192), f32)
            tl = jnp.concatenate([acc2[0:64, :], zero], axis=0).T
            th = jnp.concatenate([acc2[128:192, :] + acc1[0:64, :], zero], axis=0).T
            scale = HEAD_DIM ** (-0.5)
            for gidx in range(3):
                dqz[3 * s + gidx, 0:64, :] = tl[64 * gidx:64 * gidx + 64] * scale
                dqz[3 * s + gidx, 64:128, :] = th[64 * gidx:64 * gidx + 64] * scale

            kg.one(s)

            @pl.when(s == 0)
            def _():
                grads[l, True].one()
                grads[l, True].send()
                if l < LAYERS - 1:
                    grads[l + 1, True].two()

            @pl.when(s == 1)
            def _():
                kg.two(0)
                grads[l, False].one(0)

            @pl.when(s == 2)
            def _():
                kg.two(1)

        kg = key_grads[l]
        each(head, 0, KV_HEADS)
        kg.two(2)
        grads[l, False].send(1, 4)
        if l < LAYERS - 1:
            grads[l + 1, False].two()

        rot = []
        for j in range(HEADS):
            t = dqz[j]
            rot.append(t * cos_q - swap(t) * sin_q)
        dq = [pltpu.roll(rot[0], 64, axis=1).astype(bf16)]
        for t in range(1, 5):
            dq.append((rot[2 * t - 1] + pltpu.roll(rot[2 * t], 64, axis=1)).astype(bf16))
        dq = jnp.concatenate(dq, axis=1)
        aT = apad[l].T
        gq = nn(aT, dq).astype(bf16)
        for s in range(KV_HEADS):
            kg.three(s)
        if l < LAYERS - 1:
            grads[l + 1, True].pair()
        dkv_in = []
        for s in range(KV_HEADS):
            t = kg.total(s).reshape(128, 128)
            dkv_in.append((t * cos_kv - swap(t) * sin_kv).astype(bf16))
        dkv_in = jnp.concatenate(dkv_in, axis=1)
        da = nt(dq, units(l, 40, 5)) + nt(dkv_in, units(l, 45, 3))
        set_unit(l, 40, gq[:, 0:128] + go4[...])
        for t in range(1, 5):
            set_unit(l, 40 + t, gq[:, 128 * t:128 * t + 128])
        gkv = nn(aT, dkv_in).astype(bf16)
        for t in range(3):
            set_unit(l, 45 + t, gkv[:, 128 * t:128 * t + 128])
        dh, dgain_attn = norm_back(hs[l], dh1, unspread(da), gain[l, 0:1, 0:D])
        rows = jnp.concatenate([dgain_attn, dgain_ffn, jnp.zeros((6, D), f32)], axis=0)
        rows = jnp.concatenate([rows, jnp.zeros((8, PD - D), f32)], axis=1)
        for s in range(ND):
            part = (pltpu.roll(rows, PD - 72 * s, axis=1) if s else rows)[:, 0:128]
            keep = land[l, 0, 20, slot_of(s)].astype(f32)[0:72, :]
            land[l, 0, 20, slot_of(s)] = jnp.concatenate([keep, part], axis=0).astype(bf16)
        grads[l, False].zero(1)
        return dh

    h = hidT[...].astype(f32).T
    h = forward(0, h)
    h = forward(1, h)
    hv[...] = h.astype(bf16)
    outputs = [
        pltpu.make_async_copy(src, dst, leave.at[n])
        for n, (src, dst) in enumerate(((hv, hout), (gv, ghid), (fine, oute), (finl, outl)))
    ]
    outputs[0].start()
    g = backward(1, goutT[...].astype(f32).T)
    g = backward(0, g)
    gv[...] = g
    outputs[1].start()
    grads[0, False].one(1)
    grads[0, False].send(4, 7)
    grads[1, False].pair()
    grads[1, True].three()
    grads[0, True].two()
    grads[0, False].two()
    grads[1, False].three()
    grads[1, True].four()
    grads[0, True].pair()
    grads[0, False].pair()
    grads[1, True].five()
    grads[1, False].four()
    grads[0, True].three()
    grads[0, False].three()
    grads[1, False].five()
    grads[0, True].four()
    grads[0, False].four()
    grads[0, True].five()
    outputs[2].start()
    grads[0, False].five()
    outputs[3].start()
    for copy in outputs:
        copy.wait()


def unpack(h, gh, early, late, houtT, ghidT, gag, gq, gk, gv, go, gfg, ggate, gup, gdown):
    houtT[...] = h[...].astype(f32).T.astype(bf16)
    ghidT[...] = gh[...].T
    for l in range(LAYERS):
        attn = [None] * 12
        for cc in range(NC):
            i_, k_ = cc // 2, cc % 2
            for j in (2 * i_, 2 * i_ + 1, 16 + i_ % 4 + 4 * (i_ // 4)):
                val = (early[l, i_, k_, j - 2 * i_] if j < 16 else late[l, i_, k_, 0]).astype(f32)
                kind, t = j // 6, 6 * k_ + j % 6
                cols = slice(128 * t, 128 * t + 128)
                if kind == 0:
                    ggate[l, :, cols] = val[0:72]
                elif kind == 1:
                    gup[l, :, cols] = val[0:72]
                elif kind == 2:
                    at = slice(16 * t, 16 * t + 16)
                    for lt in range(4):
                        gdown[l, at, 128 * lt:128 * lt + 128] = val[16 * lt:16 * lt + 16]
                    gdown[l, at, 512:576] = val[64:80, 0:64]
                else:
                    t = 2 * k_ + j - 18 if j < 20 else 4 + 4 * k_ + j - 20
                    attn[t] = val[0:72]
                    if t == 4:
                        gag[l:l + 1, :] = val[72:73, 0:72]
                        gfg[l:l + 1, :] = val[73:74, 0:72]
        attn = jnp.concatenate(attn, axis=1)
        go[l] = attn[:, 0:D]
        gq[l] = attn[:, D:2 * D]
        kv = [attn[:, 2 * D + 64 * j:2 * D + 64 * j + 64] for j in range(2 * KV_HEADS)]
        gk[l] = jnp.concatenate(kv[0::2], axis=1)
        gv[l] = jnp.concatenate(kv[1::2], axis=1)


def body(
    hidden_in, positions, attn_gain, w_query, w_key, w_value, w_output, ffn_gain, w_gate, w_up, w_down, grad_out
):
    half = HEAD_DIM // 2
    freq = jnp.exp(-jnp.log(rope_base) * (2.0 * jnp.arange(half, dtype=f32) / HEAD_DIM))
    freq = jnp.tile(freq, 4).reshape(1, 128)
    outs = pl.pallas_call(
        kernel,
        out_shape=(
            jax.ShapeDtypeStruct((ROWS, D), bf16),
            jax.ShapeDtypeStruct((ROWS, D), f32),
            jax.ShapeDtypeStruct((LAYERS, NCHIP, 2, 2, R, 128), bf16),
            jax.ShapeDtypeStruct((LAYERS, NCHIP, 2, 1, R, 128), bf16),
        ),
        in_specs=[pl.BlockSpec(memory_space=pltpu.VMEM)] * 13,
        out_specs=tuple([pl.BlockSpec(memory_space=pl.ANY)] * 4),
        scratch_shapes=[
            pltpu.VMEM((NC * 64, 128), bf16),
            pltpu.VMEM((D, PD), bf16),
            pltpu.VMEM((PD, 128 * HEADS), bf16),
            pltpu.VMEM((LAYERS, 8, 128), f32),
            pltpu.VMEM((72, FF), bf16),
            pltpu.VMEM((LAYERS, 2, 24, ND, R, 128), bf16),
            pltpu.VMEM((96, 16, PD), bf16),
            pltpu.VMEM((LAYERS, NCHIP, 2, KV_HEADS, 2, 64, 128), bf16),
            pltpu.VMEM((NCHIP, 2, KV_HEADS, 2, 64, 128), bf16),
            pltpu.VMEM((LAYERS, NCHIP, KV_HEADS, 2, 64, 128), bf16),
            pltpu.VMEM((LAYERS, 7, KV_HEADS, 2, 64, 128), bf16),
            pltpu.VMEM((LAYERS, 24, ND, R, 128), bf16),
            pltpu.VMEM((LAYERS, 3, 16, 2, R, 128), bf16),
            pltpu.VMEM((LAYERS, 16, R, 128), bf16),
            pltpu.VMEM((LAYERS, 7, 2, R, 128), bf16),
            pltpu.VMEM((LAYERS, 3, 2, ND, R, 128), bf16),
            pltpu.VMEM((LAYERS, ND, R, 128), bf16),
            pltpu.VMEM((LAYERS, 7, R, 128), bf16),
            pltpu.VMEM((LAYERS, NCHIP, 2, 2, R, 128), bf16),
            pltpu.VMEM((LAYERS, NCHIP, 2, 1, R, 128), bf16),
            pltpu.VMEM((LAYERS, 6, 128, 256), bf16),
            pltpu.VMEM((LAYERS, 128, D), f32),
            pltpu.VMEM((LAYERS, 128, D), f32),
            pltpu.VMEM((LAYERS, 128, PD), bf16),
            pltpu.VMEM((LAYERS, 128, PD), bf16),
            pltpu.VMEM((LAYERS, 128, PD), bf16),
            pltpu.VMEM((LAYERS, KV_HEADS, 192, 256), bf16),
            pltpu.VMEM((KV_HEADS, 192, 256), bf16),
            pltpu.VMEM((LAYERS, KV_HEADS, 128, 192), f32),
            pltpu.VMEM((LAYERS, KV_HEADS, 8, 192), f32),
            pltpu.VMEM((HEADS, 128, 128), bf16),
            pltpu.VMEM((HEADS, 128, 128), f32),
            pltpu.VMEM((1024, 256), f32),
            pltpu.VMEM((1024, 256), f32),
            pltpu.VMEM((1024, 192), bf16),
            pltpu.VMEM((1024, 192), f32),
            pltpu.VMEM((128, PD), bf16),
            pltpu.VMEM((LAYERS, 8, PD), f32),
            pltpu.VMEM((128, 192), f32),
            pltpu.VMEM((256, 192), f32),
            pltpu.VMEM((PD, 128), bf16),
            pltpu.VMEM((ROWS, D), bf16),
            pltpu.VMEM((ROWS, D), f32),
            pltpu.SemaphoreType.DMA((381,)),
            pltpu.SemaphoreType.DMA((381,)),
            pltpu.SemaphoreType.DMA((4,)),
        ],
        compiler_params=pltpu.CompilerParams(
            collective_id=0, has_side_effects=True, vmem_limit_bytes=127 * 512 * 1024
        ),
    )(
        hidden_in.T, grad_out.T, positions.reshape(NC, ROWS), freq, attn_gain, ffn_gain,
        w_gate, w_up, w_down, w_output, w_query, w_key, w_value,
    )
    shapes = (
        (D, ROWS), (D, ROWS), (LAYERS, 72), (LAYERS, 72, D), (LAYERS, 72, KV_HEADS * HEAD_DIM),
        (LAYERS, 72, KV_HEADS * HEAD_DIM), (LAYERS, 72, D), (LAYERS, 72), (LAYERS, 72, FF), (LAYERS, 72, FF),
        (LAYERS, 192, D),
    )
    houtT, ghidT, *rest = pl.pallas_call(
        unpack,
        out_shape=[jax.ShapeDtypeStruct(shape, f32 if n else bf16) for n, shape in enumerate(shapes)],
        in_specs=[pl.BlockSpec(memory_space=pltpu.VMEM)] * 4,
        out_specs=[pl.BlockSpec(memory_space=pltpu.VMEM)] * 11,
        compiler_params=pltpu.CompilerParams(vmem_limit_bytes=127 * 512 * 1024),
    )(*outs)
    return (houtT.T, ghidT.T, *rest)


def solution(mesh):
    placed = (
        P(("dp", "ctx"), None),
        P("dp"),
        P(None, "dp"),
        P(None, "dp", None),
        P(None, "dp", None),
        P(None, "dp", None),
        P(None, "dp", None),
        P(None, "dp"),
        P(None, "dp", None),
        P(None, "dp", None),
        P(None, "dp", None),
        P(("dp", "ctx"), None),
    )
    out = (
        P(("dp", "ctx"), None),
        P(("dp", "ctx"), None),
        P(None, "dp"),
        P(None, "dp", None),
        P(None, "dp", None),
        P(None, "dp", None),
        P(None, "dp", None),
        P(None, "dp"),
        P(None, "dp", None),
        P(None, "dp", None),
        P(None, "dp", None),
    )
    return jax.shard_map(body, mesh=mesh, in_specs=placed, out_specs=out, check_vma=False)
```

```python
import jax
import jax.numpy as jnp
from jax import lax
from jax.experimental import pallas as pl
from jax.experimental.pallas import tpu as pltpu
from jax.sharding import PartitionSpec as P

D = 576
HEADS = 9
KV_HEADS = 3
HEAD_DIM = 64
FF = 1536
LAYERS = 2
ROWS = 128
ND = 8
NC = 16
NCHIP = 8
R = 80
PD = 640
MESH = pl.DeviceIdType.MESH
bf16 = jnp.bfloat16
f32 = jnp.float32
NEG = -1e30
eps_norm = 1e-05
rope_base = 100000.0


def nn(a, b):
    return lax.dot_general(a, b, (((1,), (0,)), ((), ())), preferred_element_type=f32)


def nt(a, b):
    return lax.dot_general(a, b, (((1,), (1,)), ((), ())), preferred_element_type=f32)


def tn(a, b):
    return lax.dot_general(a, b, (((0,), (0,)), ((), ())), preferred_element_type=f32)


class Move:
    def __init__(self, make, src, dst, inc, s, dev):
        self.out = lambda: make(src, dst, s, dev)
        self.inc = lambda: make(inc, inc, s, dev)

    def start(self):
        self.out().start()

    def recv(self):
        self.inc().wait_recv()

    def sent(self):
        self.out().wait_send()


def slot_of(shard):
    return (shard % 4) * 2 + shard // 4


def attn_place(t):
    return (t // 2, 18 + t % 2) if t < 4 else ((t - 4) // 4, 20 + (t - 4) % 4)


def kernel(
    hidT, goutT, pos, freq, again, fgain, wgate, wup, wdown, wo, wq, wk, wv,
    hout, ghid, oute, outl,
    mlow, e1, e2, gains, wattn,
    land, wd, kvl, dkv, dkr0, dkr1,
    rs0, r1e, rz, r2e, r1l, rzl, r2l, fine, finl,
    mid, hs, h1s, apad, bpad, mixp, qc, doc, oT, lse, oz, dqz,
    s1, s2, bias, mk, zpad, gain, acc1, acc2, go4,
    hv, gv, send, recv, leave,
):
    d = lax.axis_index("dp")
    c = lax.axis_index("ctx")
    k, y = lax.rem(c, 2), lax.rem(c // 2, 4)
    x, zl = lax.rem(d, 4), d // 4
    mine = 2 * x + zl
    i = c // 2
    sib = {"ctx": i * 2 + 1 - k}
    count = [0]

    def dplus(m):
        return lax.rem(d + m, ND)

    def dminus(m):
        return lax.rem(d - m + ND, ND)

    def iplus(m):
        return lax.rem(i + m, NCHIP)

    def iminus(m):
        return lax.rem(i - m + NCHIP, NCHIP)

    def shard(m):
        return {"dp": dplus(m)}

    def slot(j):
        return lax.rem(j, 4) * 2 + j // 4

    def chip(m):
        return {"ctx": iplus(m) * 2 + k}

    def near(at, o):
        return lax.rem(at + o + 4, 4)

    def X(o):
        return {"dp": zl * 4 + near(x, o)}

    def Y(o):
        return {"ctx": ((i // 4) * 4 + near(y, o)) * 2 + k}

    def rc(src, dst, s, to):
        return pltpu.make_async_remote_copy(
            src_ref=src, dst_ref=dst, send_sem=send.at[s], recv_sem=recv.at[s],
            device_id=to, device_id_type=MESH,
        )

    def sems(n):
        count[0] += n
        return count[0] - n

    def move(src, dst, inc, to, s=None):
        return Move(rc, src, dst, inc, sems(1) if s is None else s, to)

    def starts(*moves):
        for m in moves:
            m.start()

    def recvs(*moves):
        for m in moves:
            m.recv()

    def sents(*moves):
        for m in moves:
            m.sent()

    def each(f, lo=1, hi=8):
        def step(m, carry):
            f(m)
            return carry
        lax.fori_loop(lo, hi, step, 0)

    def put(l, j, val, last=None, k=k):
        last = jnp.zeros((8, 128), f32) if last is None else last
        land[l, k, j, mine] = jnp.concatenate([val.astype(f32), last], axis=0).astype(bf16)

    def column(t):
        return pl.ds(pl.multiple_of(128 * t, 128), 128)

    def pack_attn(l):
        key, value = wk[l].astype(f32), wv[l].astype(f32)
        parts = [wo[l].astype(f32), wq[l].astype(f32)]
        for h in range(KV_HEADS):
            parts += [key[:, 64 * h:64 * h + 64], value[:, 64 * h:64 * h + 64]]
        wattn[...] = jnp.concatenate(parts, axis=1).astype(bf16)
        gains[l] = jnp.zeros((8, 128), f32)
        gains[l, 0:1, 0:72] = again[l:l + 1, :].astype(f32)
        gains[l, 1:2, 0:72] = fgain[l:l + 1, :].astype(f32)
        if l == 0:
            for t in range(12):
                k_, j = attn_place(t)
                put(l, j, wattn[:, 128 * t:128 * t + 128], gains[l], k_)
        else:
            put(l, 18 + y, wattn[:, column(jnp.where(y < 2, 2 * k + y, 2 + 4 * k + y))], gains[l])
            put(l, 22, wattn[:, column(6 + 4 * k)])
            put(l, 23, wattn[:, column(7 + 4 * k)])

    def pack_ffn(l):
        @pl.when(y < 3)
        def _():
            for r in range(2):
                put(l, 2 * y + r, wgate[l, :, column(6 * k + 2 * y + r)])

        @pl.when(y == 3)
        def _():
            for r in range(2):
                put(l, 6 + r, wup[l, :, column(6 * k + r)])

        for r in range(2, 6):
            put(l, 6 + r, wup[l, :, column(6 * k + r)])
        for g in range(6):
            val = wdown[l, pl.ds(pl.multiple_of(16 * (6 * k + g), 16), 16), :]
            val = jnp.concatenate([val.astype(f32), jnp.zeros((16, 64), f32)], axis=1).astype(bf16)
            for lt in range(5):
                land[l, k, 12 + g, mine, 16 * lt:16 * lt + 16, :] = val[:, 128 * lt:128 * lt + 128]

    class Weights:
        def __init__(self, l, shared, direct):
            self.shared = shared is not None
            self.relays = (l, direct[0]) != (0, 20)
            db, nd = direct

            def straight(slot):
                return land.at[l, k, pl.ds(db, nd), slot]

            self.parts = [(straight, sems(7))]
            here, there = land.at[l, k, pl.ds(db, nd)], land.at[l, 1 - k, pl.ds(db, nd)]
            self.u = []
            if not self.shared:
                self.v = None
                self.base = sems(7)
                self.slot = lambda k_, slot: land.at[l, k_, pl.ds(db, nd), slot]
                return
            sb, ns = shared
            self.parts.append((lambda slot: land.at[l, k, pl.ds(sb + ns * y, ns), slot], sems(7)))
            self.v = [move(here, here, there, sib)]

            def block(y_, k_=k, half=None):
                ref = land.at[l, k_, pl.ds(sb + ns * y_, ns)]
                return ref if half is None else ref.at[:, pl.ds(4 * half, 4)]

            yp, ym, y2 = near(y, 1), near(y, -1), near(y, 2)
            self.u = [
                move(block(y), block(y), block(ym), Y(1)), move(block(y), block(y), block(yp), Y(-1)),
                move(block(ym, half=0), block(ym, half=0), block(y2, half=0), Y(1)),
                move(block(yp, half=1), block(yp, half=1), block(y2, half=1), Y(-1)),
            ]
            self.v += [move(block(y_), block(y_), block(y_, 1 - k), sib) for y_ in (y, ym, yp, y2)]

        def sends(self, part):
            ref, s = self.parts[part]
            if not self.relays:
                return [(rc(ref(mine), ref(mine), s + m - 1, shard(m)), slot(dminus(m)), s + m - 1, m - 1) for m in range(1, 8)]
            other = 2 * x + 1 - zl
            out = [
                (rc(ref(mine), ref(mine), s + o - 1, X(o)), 2 * near(x, -o) + zl, s + o - 1, o - 1) for o in (1, 2, 3)
            ]
            out.append((rc(ref(mine), ref(mine), s + 3, {"dp": (1 - zl) * 4 + x}), other, s + 3, 3))
            return out + [
                (rc(ref(other), ref(other), s + 3 + o, X(o)), 2 * near(x, -o) + 1 - zl, s + 3 + o, 3 + o)
                for o in (1, 2, 3)
            ]

        def one(self, part):
            sends = self.sends(part)
            for copy, *_ in [sends[3], *sends[:3]] if self.relays else sends:
                copy.start()

        def got(self, part, item):
            _, at, s, b = item
            ref = self.parts[part][0](at)
            rc(ref, ref, s, sib).wait_recv()
            if not self.shared:
                rc(ref, ref, self.base + b, sib).start()

        def relay(self, part):
            sends = self.sends(part)
            self.got(part, sends[3])
            for copy, *_ in sends[4:]:
                copy.start()

        def two(self, part):
            for n, item in enumerate(self.sends(part)):
                if not (self.relays and n == 3):
                    self.got(part, item)
            if part:
                starts(self.u[0], self.u[1], self.v[1])
            elif self.shared:
                starts(self.v[0])

        def three(self):
            recvs(self.u[0])
            starts(self.u[2], self.v[2])
            recvs(self.u[1])
            starts(self.u[3], self.v[3])

        def four(self):
            recvs(self.u[2], self.u[3])
            starts(self.v[4])

        def five(self):
            if self.shared:
                recvs(*self.v)
                sents(*self.u)
                sents(*self.v)

            for part in range(len(self.parts)):
                for copy, at, _, b in self.sends(part):
                    copy.wait_send()
                    if not self.shared:
                        got, gave = self.slot(1 - k, at), self.slot(k, at)
                        rc(got, got, self.base + b, sib).wait_recv()
                        rc(gave, gave, self.base + b, sib).wait_send()

    class Keys:
        def __init__(self, l):
            self.l, self.a, self.b, self.s = l, sems(21), sems(21), sems(3)

        def own(self, h):
            ref = kvl.at[self.l, i, k, h]
            return rc(ref, ref, self.s + h, sib)

        def out(self, h, m):
            ref = kvl.at[self.l, i, k, h]
            return rc(ref, ref, self.a + 7 * h + m - 1, chip(m))

        def passed(self, h, m, k_):
            ref = kvl.at[self.l, iminus(m), k_, h]
            return rc(ref, ref, self.b + 7 * h + m - 1, sib)

        def one(self, h):
            each(lambda m: self.out(h, m).start())
            self.own(h).start()

        def two(self, h):
            def go(m):
                ref = kvl.at[self.l, iminus(m), k, h]
                rc(ref, ref, self.a + 7 * h + m - 1, chip(m)).wait_recv()
                self.passed(h, m, k).start()
            each(go)

        def three(self, h):
            ref = kvl.at[self.l, i, 1 - k, h]
            rc(ref, ref, self.s + h, sib).wait_recv()
            self.own(h).wait_send()

            def go(m):
                self.passed(h, m, 1 - k).wait_recv()
                self.passed(h, m, k).wait_send()
                self.out(h, m).wait_send()
            each(go)

    class KeyGrads:
        def __init__(self, l):
            self.l, self.s, self.a = l, sems(3), sems(21)

        def pair(self, h):
            return rc(dkv.at[:, 1 - k, h], dkr0.at[self.l, :, h], self.s + h, sib)

        def out(self, h, m):
            return rc(dkv.at[iplus(m), k, h], dkr1.at[self.l, m - 1, h], self.a + 7 * h + m - 1, chip(m))

        def one(self, h):
            self.pair(h).start()

        def two(self, h):
            self.pair(h).wait()

            def go(m):
                j = iplus(m)
                total = dkv[j, k, h].astype(f32) + dkr0[self.l, j, h].astype(f32)
                dkv[j, k, h] = total.astype(bf16)
                self.out(h, m).start()

            each(go)

        def three(self, h):
            each(lambda m: self.out(h, m).wait())

        def total(self, h):
            val = dkv[i, k, h].astype(f32) + dkr0[self.l, i, h].astype(f32)
            for m in range(7):
                val = val + dkr1[self.l, m, h].astype(f32)
            return val

    class Grads:
        def __init__(self, l, early):
            self.l, self.early = l, early
            self.own = 16 + y + 4 * (i // 4)
            self.s = []
            for lo, n in ((0, 16),) if early else ((16, 4), (20, 4)):
                there = rs0.at[l, pl.ds(lo, n)]
                self.s.append(move(land.at[l, 1 - k, pl.ds(lo, n)], there, there, sib))
            self.r1, self.r2, self.fin = (r1e, r2e, fine) if early else (r1l, r2l, finl)
            self.a, self.b, self.c, self.v, self.z = sems(6), sems(7), sems(7), sems(7), sems(2 if early else 1)
            own = self.fin.at[l, i, k]
            self.t = move(own, own, self.fin.at[l, i, 1 - k], sib)

        def out1(self, m):
            l = self.l
            if self.early:
                h, o = (m - 1) // 3, lax.rem(m - 1, 3)
                x_ = near(x, o + 1)
                src, to = land.at[l, k, pl.ds(8 * h, 8), pl.ds(2 * x_, 2)], {"dp": zl * 4 + x_}
                return rc(src, r1e.at[l, o, pl.ds(8 * h, 8)], self.a + m - 1, to)
            h, o = (m - 1) // 3, lax.rem(m - 1, 3)
            y_ = near(y, o + 1)
            to = {"ctx": ((i // 4) * 4 + y_) * 2 + k}
            return rc(land.at[l, k, 16 + 4 * h + y_], r1l.at[l, o, h], self.a + m - 1, to)

        def outz(self, h=0):
            if not self.early:
                src = land.at[self.l, k, 16 + y + 4 * (1 - i // 4)]
                return rc(src, rzl.at[self.l], self.z, {"ctx": ((1 - i // 4) * 4 + y) * 2 + k})
            src = land.at[self.l, k, pl.ds(8 * h, 8), 2 * x + 1 - zl]
            return rc(src, rz.at[self.l, pl.ds(8 * h, 8)], self.z + h, {"dp": 4 * (1 - zl) + x})

        def out2(self, m):
            l = self.l
            if self.early:
                src, to = land.at[l, k, pl.ds(2 * iplus(m), 2), mine], chip(m)
            else:
                src, to = land.at[l, k, self.own, slot(dplus(m))], shard(m)
            return rc(src, self.r2.at[l, m - 1], self.b + m - 1, to)

        def zero(self, part=0):
            starts(self.s[part])

        def one(self, part=0):
            recvs(self.s[part])
            l = self.l

            def go(u):
                total = land[l, k, u].astype(f32) + rs0[l, u].astype(f32)
                land[l, k, u] = total.astype(bf16)

            each(go, *((0, 16) if self.early else (16 + 4 * part, 20 + 4 * part)))

        def send(self, lo=1, hi=None):
            each(lambda m: self.out1(m).start(), lo, hi or 7)

        def two(self, halves=(0, 1)):
            l = self.l
            if self.early:
                def go(u):
                    total = land[l, k, u, pl.ds(2 * x, 2)].astype(f32)
                    for o in range(3):
                        total = total + r1e[l, o, u].astype(f32)
                    land[l, k, u, pl.ds(2 * x, 2)] = total.astype(bf16)

                for h in halves:
                    each(lambda m: self.out1(m).wait(), 1 + 3 * h, 4 + 3 * h)
                    each(go, 8 * h, 8 * h + 8)
                    self.outz(h).start()
            else:
                each(lambda m: self.out1(m).wait(), 1, 7)

                def go(u):
                    for q in range(2):
                        total = land[l, k, 16 + y + 4 * q, u].astype(f32)
                        for m in range(3):
                            total = total + r1l[l, m, q, u].astype(f32)
                        land[l, k, 16 + y + 4 * q, u] = total.astype(bf16)

                each(go, 0, 8)
                self.outz().start()

        def pair(self):
            for h in range(2 if self.early else 1):
                self.outz(h).wait()
            l = self.l

            def go(u):
                if self.early:
                    land[l, k, u, mine] = (land[l, k, u, mine].astype(f32) + rz[l, u].astype(f32)).astype(bf16)
                else:
                    total = land[l, k, self.own, u].astype(f32) + rzl[l, u].astype(f32)
                    land[l, k, self.own, u] = total.astype(bf16)

            each(go, 0, 16 if self.early else 8)
            each(lambda m: self.out2(m).start())

        def three(self):
            each(lambda m: self.out2(m).wait())
            l = self.l
            for u in range(2 if self.early else 1):
                total = (land[l, k, 2 * i + u, mine] if self.early else land[l, k, self.own, mine]).astype(f32)
                for m in range(7):
                    total = total + (self.r2[l, m, u] if self.early else self.r2[l, m]).astype(f32)
                self.fin[l, i, k, u] = total.astype(bf16)
            own = self.fin.at[l, i, k]
            each(lambda m: rc(own, own, self.c + m - 1, chip(m)).start())
            starts(self.t)

        def four(self):
            def go(m):
                ref = self.fin.at[self.l, iminus(m), k]
                rc(ref, ref, self.c + m - 1, chip(m)).wait_recv()
                rc(ref, ref, self.v + m - 1, sib).start()
            each(go)

        def five(self):
            l = self.l
            recvs(self.t)
            sents(self.t, *self.s)

            def go(m):
                got, gave = self.fin.at[l, iminus(m), 1 - k], self.fin.at[l, iminus(m), k]
                own = self.fin.at[l, i, k]
                rc(got, got, self.v + m - 1, sib).wait_recv()
                rc(gave, gave, self.v + m - 1, sib).wait_send()
                rc(own, own, self.c + m - 1, chip(m)).wait_send()
            each(go)

    weights = {
        (0, "A"): Weights(0, None, (20, 4)), (0, "O"): Weights(0, None, (18, 2)), (0, "F"): Weights(0, (0, 2), (8, 10)),
        (1, "A"): Weights(1, (18, 1), (22, 2)), (1, "F"): Weights(1, (0, 2), (8, 10)),
    }
    keys = [Keys(l) for l in range(LAYERS)]
    key_grads = [KeyGrads(l) for l in range(LAYERS)]
    grads = {(l, e): Grads(l, e) for l in range(LAYERS) for e in (True, False)}

    barrier = pltpu.get_barrier_semaphore()

    def hello(m):
        pl.semaphore_signal(barrier, inc=1, device_id=shard(m), device_id_type=MESH)
        pl.semaphore_signal(barrier, inc=1, device_id=chip(m), device_id_type=MESH)

    each(hello)
    pl.semaphore_signal(barrier, inc=1, device_id=sib, device_id_type=MESH)
    pack_attn(0)
    pl.semaphore_wait(barrier, 15)
    weights[0, "A"].one(0)
    pack_ffn(0)
    weights[0, "F"].one(1)
    pack_attn(1)
    pack_ffn(1)

    lane = lax.broadcasted_iota(jnp.int32, (128, 128), 1)
    low_half = lane < 64
    first_quarter = lax.rem(lane, 64) < 32
    place_own = pos[pl.ds(c, 1), :].astype(f32)
    angle = jnp.broadcast_to(place_own, (128, 128)).T * freq[...]
    cos_q = jnp.cos(angle)
    sin_q = jnp.sin(angle) * jnp.where(first_quarter, -1.0, 1.0)
    low = jnp.where(pos[:, 0:1] <= pos[pl.ds(c, 1), 0:1], 1.0, 0.0)
    for s in range(NC):
        mlow[64 * s:64 * s + 64, :] = jnp.broadcast_to(low[s:s + 1, :], (64, 128)).astype(bf16)
    row = lax.broadcasted_iota(jnp.int32, (D, PD), 0)
    col = lax.broadcasted_iota(jnp.int32, (D, PD), 1)
    shard_of = (row * 911) >> 16
    e1[...] = jnp.where(
        col == row - 72 * shard_of + R * ((shard_of & 3) * 2 + (shard_of >> 2)), 1.0, 0.0
    ).astype(bf16)
    row = lax.broadcasted_iota(jnp.int32, (PD, 128 * HEADS), 0)
    col = lax.broadcasted_iota(jnp.int32, (PD, 128 * HEADS), 1)
    at_slot = (row * 205) >> 14
    natural = row - R * at_slot + 72 * ((at_slot & 1) * 4 + (at_slot >> 1))
    hit = (row - R * at_slot < 72) & (col == 128 * (natural >> 6) + 64 + (natural & 63))
    e2[...] = jnp.where(hit, 1.0, 0.0).astype(bf16)
    cos_kv = jnp.where(low_half, cos_q, 1.0)
    sin_kv = jnp.where(low_half, sin_q, 0.0)

    def swap(x):
        return jnp.where(first_quarter, pltpu.roll(x, 96, axis=1), pltpu.roll(x, 32, axis=1))

    row = lax.broadcasted_iota(jnp.int32, (1024, 192), 0) - 64 * c
    col = lax.rem(lax.broadcasted_iota(jnp.int32, (1024, 192), 1), 64)
    bias[...] = jnp.where((row > col) & (row < 64), NEG, 0.0).astype(bf16)
    mk[...] = jnp.concatenate([mlow[...], mlow[:, 0:64]], axis=1).astype(f32)
    row = lax.broadcasted_iota(jnp.int32, (64, 192), 0)
    col = lax.rem(lax.broadcasted_iota(jnp.int32, (64, 192), 1), 64)
    tri = jnp.where(row > col, NEG, 0.0)
    zpad[...] = jnp.zeros((128, PD), bf16)

    def place(u):
        if isinstance(u, int) and u >= 36:
            return attn_place(u - 36)
        return lax.rem(u, 12) // 6, 6 * (u // 12) + lax.rem(u, 6)

    def unit(l, u):
        return land[(l, *place(u))].reshape(PD, 128)

    def pair(l, u):
        return jnp.concatenate([unit(l, u), unit(l, u + 1)], axis=1)

    def units(l, u, n):
        return jnp.concatenate([unit(l, u + j) for j in range(n)], axis=1)

    def norm_scale(h):
        return lax.rsqrt(jnp.mean(h * h, axis=-1, keepdims=True) + eps_norm)

    def spread(x):
        return nn(x.astype(bf16), e1[...]).astype(bf16)

    def unspread(x):
        hi = x.astype(bf16)
        lo = (x - hi.astype(f32)).astype(bf16)
        return nt(hi, e1[...]) + nt(lo, e1[...])

    def set_unit(l, u, val):
        land[(l, *place(u))] = val.reshape(8, R, 128)

    def load_gains(l):
        total = jnp.zeros((8, PD), f32)
        for s in range(ND):
            part = land[l, 0, 20, slot_of(s)].astype(f32)[72:80, :]
            wide = jnp.concatenate([part, jnp.zeros((8, PD - 128), f32)], axis=1)
            total = total + (pltpu.roll(wide, 72 * s, axis=1) if s else wide)
        gain[l] = total

    def down_pieces(l, f):
        def go(g):
            for k_ in range(2):
                for s in range(ND):
                    for lt in range(5):
                        f(
                            wd.at[12 * s + 6 * k_ + g, :, 128 * lt:128 * lt + 128],
                            land.at[l, k_, 12 + g, slot_of(s), 16 * lt:16 * lt + 16, :],
                        )
        each(go, 0, 6)

    def regroup_down(l):
        def go(rows, piece):
            rows[...] = piece[...]
        down_pieces(l, go)

    def scatter_down(l):
        def go(rows, piece):
            piece[...] = rows[...]
        down_pieces(l, go)

    def down(t):
        return wd[pl.ds(16 * t, 16)].reshape(256, PD)

    def tiles(l, h, j):
        tlo = kvl[l, pl.ds(2 * j, 2), :, h, 0].reshape(256, 128)
        thi = kvl[l, pl.ds(2 * j, 2), :, h, 1].reshape(256, 128)
        m = mlow[pl.ds(pl.multiple_of(256 * j, 256), 256), :]
        x2 = jnp.concatenate([tlo * m, thi * (1 - m)], axis=1)
        return tlo, x2, m

    def swiglu_parts(l, t, x):
        g = nn(x, pair(l, 2 * t))
        u = nn(x, pair(l, 12 + 2 * t))
        return g, u

    def forward(l, h):
        hs[l] = h
        if l == 0:
            weights[0, "A"].two(0)
        weights[l, "A"].five()
        if l == 0:
            weights[0, "F"].relay(1)
        load_gains(l)
        apad[l] = spread(h * norm_scale(h) * gain[l, 0:1, 0:D])
        a = apad[l]
        for s in range(KV_HEADS):
            kv = nn(a, unit(l, 45 + s))
            kv = kv * cos_kv + swap(kv) * sin_kv
            kvl[l, i, k, s] = kv.astype(bf16).reshape(2, 64, 128)
            keys[l].one(s)
        if l == 0:
            weights[0, "O"].one(0)
            weights[0, "F"].one(0)
        else:
            weights[1, "F"].two(1)
        for t in range(5):
            q = nn(a, unit(l, 40 + t))
            q = (q * cos_q + swap(q) * sin_q) * HEAD_DIM ** (-0.5)
            for j in ((2 * t - 1, 2 * t) if t else (0,)):
                part = q if j % 2 else pltpu.roll(q, 64, axis=1)
                part = jnp.where(low_half, part, 0.0).astype(bf16)
                g = j % 3
                qc[l, j // 3, 64 * g:64 * g + 64, 0:128] = part[0:64]
                qc[l, j // 3, 64 * g:64 * g + 64, 128:256] = part[64:128]
        keys[l].two(0)
        if l == 0:
            weights[0, "F"].two(1)

        def head(s):
            keys[l].three(s)

            @pl.when(s < KV_HEADS - 1)
            def _():
                keys[l].two(s + 1)

            qcat = qc[l, s]
            qT = qcat.astype(f32).T.astype(bf16)
            qhT = qT[128:256]
            top_own = kvl[l, i, k, s, 1]
            se = nn(top_own, qhT) + tri

            def scores(j, carry):
                ml, mh = carry
                tlo, x2, _ = tiles(l, s, j)
                at = pl.ds(pl.multiple_of(256 * j, 256), 256)
                a1 = nn(tlo, qhT)
                a2 = nn(x2, qT) + bias[at, :].astype(f32)
                s1[at, 0:192] = a1
                s2[at, 0:192] = a2
                is_low = mk[at, :] > 0.5
                ml = jnp.maximum(ml, jnp.max(jnp.where(is_low, a2, NEG), axis=0, keepdims=True))
                mh = jnp.maximum(
                    mh, jnp.max(jnp.maximum(a1, jnp.where(is_low, NEG, a2)), axis=0, keepdims=True)
                )
                return ml, mh

            ml, mh = lax.fori_loop(
                0, 4, scores,
                (jnp.full((1, 192), NEG, f32), jnp.max(se, axis=0, keepdims=True)),
            )
            pe = jnp.exp(se - mh)
            acc1[...] = tn(top_own, pe.astype(bf16))
            acc2[...] = jnp.zeros((256, 192), f32)

            def weigh(j, carry):
                ll, lh = carry
                tlo, x2, _ = tiles(l, s, j)
                at = pl.ds(pl.multiple_of(256 * j, 256), 256)
                is_low = mk[at, :] > 0.5
                p1 = jnp.exp(s1[at, 0:192] - mh)
                p2 = jnp.exp(s2[at, 0:192] - jnp.where(is_low, ml, mh))
                ll = ll + jnp.sum(jnp.where(is_low, p2, 0.0), axis=0, keepdims=True)
                lh = lh + jnp.sum(p1 + jnp.where(is_low, 0.0, p2), axis=0, keepdims=True)
                acc1[...] += tn(tlo, p1.astype(bf16))
                acc2[...] += tn(x2, p2.astype(bf16))
                return ll, lh

            ll, lh = lax.fori_loop(
                0, 4, weigh, (jnp.zeros((1, 192), f32), jnp.sum(pe, axis=0, keepdims=True))
            )
            olow = acc2[64:128, :] / ll
            ohigh = (acc2[192:256, :] + acc1[64:128, :]) / lh
            oT[l, s, 0:64, :] = olow
            oT[l, s, 64:128, :] = ohigh
            lse[l, s, 0:1, :] = ml + jnp.log(ll)
            lse[l, s, 1:2, :] = mh + jnp.log(lh)
            zero = jnp.zeros((64, 192), f32)
            tl = jnp.concatenate([zero, olow], axis=0).T.astype(bf16)
            th = jnp.concatenate([zero, ohigh], axis=0).T.astype(bf16)
            for g in range(3):
                oz[3 * s + g, 0:64, :] = tl[64 * g:64 * g + 64]
                oz[3 * s + g, 64:128, :] = th[64 * g:64 * g + 64]

            if l == 0:
                @pl.when(s == 0)
                def _():
                    weights[0, "O"].relay(0)
                    weights[0, "F"].relay(0)
                    weights[1, "A"].one(1)
                    weights[1, "A"].one(0)

                @pl.when(s == 1)
                def _():
                    weights[1, "A"].relay(1)
                    weights[1, "A"].relay(0)
                    weights[1, "F"].one(1)
                    weights[1, "F"].one(0)
            else:
                @pl.when(s == 1)
                def _():
                    weights[1, "F"].two(0)
                    weights[1, "F"].three()

        each(head, 0, KV_HEADS)
        if l == 0:
            weights[0, "F"].three()
            weights[0, "O"].two(0)
            weights[0, "F"].two(0)
            weights[0, "F"].four()
            weights[0, "O"].five()
        mixp[l] = nt(jnp.concatenate([oz[j] for j in range(HEADS)], axis=1), e2[...]).astype(bf16)
        out = nn(mixp[l], units(l, 36, 5))
        h1 = h + out[:, 0:D]
        h1s[l] = h1
        bpad[l] = spread(h1 * norm_scale(h1) * gain[l, 1:2, 0:D])
        if l == 0:
            weights[1, "A"].two(1)
            weights[1, "F"].relay(1)
            weights[1, "F"].relay(0)
        else:
            weights[1, "F"].four()
        weights[l, "F"].five()
        regroup_down(l)

        def ffn(t, total):
            g, u = swiglu_parts(l, t, bpad[l])
            if l == LAYERS - 1:
                s1[pl.ds(pl.multiple_of(128 * t, 128), 128), :] = g
                s2[pl.ds(pl.multiple_of(128 * t, 128), 128), :] = u
            m = (g / (1.0 + jnp.exp(-g)) * u).astype(bf16)
            mid[l, t] = m
            if l == 0:
                @pl.when(t == 3)
                def _():
                    weights[1, "A"].three()

            return total + nn(m, down(t))

        total = lax.fori_loop(0, 6, ffn, jnp.zeros((128, PD), f32))
        if l == 0:
            weights[1, "A"].two(0)
            weights[1, "A"].four()
        return h1 + total[:, 0:D]

    def norm_back(h, g, dn, gain_row):
        r = norm_scale(h)
        xn = h * r
        cc = dn * gain_row
        return (
            g + r * (cc - xn * jnp.mean(cc * xn, axis=-1, keepdims=True)),
            jnp.sum(dn * xn, axis=0, keepdims=True),
        )

    def backward(l, g):
        zpad[:, 0:D] = g.astype(bf16)
        if l < LAYERS - 1:
            regroup_down(l)
        bT = bpad[l].T

        def ffn(t, total):
            dz = zpad[...]
            if l == LAYERS - 1:
                at = pl.ds(pl.multiple_of(128 * t, 128), 128)
                ga, u = s1[at, :], s2[at, :]
            else:
                ga, u = swiglu_parts(l, t, bpad[l])
            dm = nt(dz, down(t))
            sg = 1.0 / (1.0 + jnp.exp(-ga))
            silu = ga * sg
            dg = (dm * u * (sg * (1.0 + ga * (1.0 - sg)))).astype(bf16)
            du = (dm * silu).astype(bf16)
            total = total + nt(dg, pair(l, 2 * t)) + nt(du, pair(l, 12 + 2 * t))
            wd[pl.ds(16 * t, 16)] = tn(mid[l, t], dz).astype(bf16).reshape(16, 16, PD)
            gw = nn(bT, dg).astype(bf16)
            set_unit(l, 2 * t, gw[:, 0:128])
            set_unit(l, 2 * t + 1, gw[:, 128:256])
            gw = nn(bT, du).astype(bf16)
            set_unit(l, 12 + 2 * t, gw[:, 0:128])
            set_unit(l, 13 + 2 * t, gw[:, 128:256])
            return total

        total = lax.fori_loop(0, 6, ffn, jnp.zeros((128, PD), f32))
        scatter_down(l)
        grads[l, True].zero()
        if l < LAYERS - 1:
            grads[l + 1, False].one(1)
            grads[l + 1, False].send(4, 7)
        dh1, dgain_ffn = norm_back(h1s[l], g, unspread(total), gain[l, 1:2, 0:D])
        zpad[:, 0:D] = dh1.astype(bf16)
        do = nt(zpad[...], units(l, 36, 5)).astype(bf16)
        go = nn(mixp[l].T, zpad[...]).astype(bf16)
        for t in range(4):
            set_unit(l, 36 + t, go[:, 128 * t:128 * t + 128])
        go4[...] = go[:, 512:640]
        grads[l, False].zero(0)
        for j in range(HEADS):
            part = nn(do, e2[:, 128 * j:128 * j + 128]).astype(bf16)
            gidx = j % 3
            doc[j // 3, 64 * gidx:64 * gidx + 64, 0:128] = part[0:64]
            doc[j // 3, 64 * gidx:64 * gidx + 64, 128:256] = part[64:128]

        def head(s):
            qcat = qc[l, s]
            qh = qcat[:, 128:256]
            qT = qcat.astype(f32).T.astype(bf16)
            qhT = qT[128:256]
            docat = doc[s]
            doh = docat[:, 128:256]
            doT = docat.astype(f32).T
            doTb = doT.astype(bf16)
            dohT = doTb[128:256]
            dl = jnp.sum(oT[l, s, 0:64, :] * doT[64:128, :], axis=0, keepdims=True)
            dh = jnp.sum(oT[l, s, 64:128, :] * doT[192:256, :], axis=0, keepdims=True)
            lsl = lse[l, s, 0:1, :]
            lsh = lse[l, s, 1:2, :]
            own = kvl[l, i, k, s, 1]
            pe = jnp.exp(nn(own, qhT) + tri - lsh)
            dse = (pe * (nn(own, dohT) - dh)).astype(bf16)
            dxe = nn(dse, qh) + nn(pe.astype(bf16), doh)
            acc1[...] = tn(own, dse)
            acc2[...] = jnp.zeros((256, 192), f32)

            def chunk(j):
                tlo, x2, m = tiles(l, s, j)
                at = pl.ds(pl.multiple_of(256 * j, 256), 256)
                is_low = mk[at, :] > 0.5
                p1 = jnp.exp(nn(tlo, qhT) - lsh)
                p2 = jnp.exp(nn(x2, qT) + bias[at, :].astype(f32) - jnp.where(is_low, lsl, lsh))
                ds1 = (p1 * (nn(tlo, dohT) - dh)).astype(bf16)
                ds2 = (p2 * (nn(x2, doTb) - jnp.where(is_low, dl, dh))).astype(bf16)
                p1 = p1.astype(bf16)
                p2 = p2.astype(bf16)
                dx1 = nn(ds1, qh) + nn(p1, doh)
                dx2 = nn(ds2, qcat) + nn(p2, docat)
                mf = m.astype(f32)
                lo = dx1 + mf * dx2[:, 0:128]
                hi = (1.0 - mf) * dx2[:, 128:256]
                dkv[pl.ds(2 * j, 2), :, s, 0] = lo.astype(bf16).reshape(2, 2, 64, 128)
                dkv[pl.ds(2 * j, 2), :, s, 1] = hi.astype(bf16).reshape(2, 2, 64, 128)
                acc1[...] += tn(tlo, ds1)
                acc2[...] += tn(x2, ds2)

            each(chunk, 0, 4)
            dkv[i, k, s, 1] = dxe.astype(bf16)
            zero = jnp.zeros((64, 192), f32)
            tl = jnp.concatenate([acc2[0:64, :], zero], axis=0).T
            th = jnp.concatenate([acc2[128:192, :] + acc1[0:64, :], zero], axis=0).T
            scale = HEAD_DIM ** (-0.5)
            for gidx in range(3):
                dqz[3 * s + gidx, 0:64, :] = tl[64 * gidx:64 * gidx + 64] * scale
                dqz[3 * s + gidx, 64:128, :] = th[64 * gidx:64 * gidx + 64] * scale

            kg.one(s)

            @pl.when(s == 0)
            def _():
                grads[l, True].one()
                grads[l, True].send(1, 4)
                if l < LAYERS - 1:
                    grads[l + 1, True].two()
                else:
                    grads[l, True].send(4, 7)

            @pl.when(s == 1)
            def _():
                kg.two(0)
                grads[l, False].one(0)

            @pl.when(s == 2)
            def _():
                kg.two(1)
                if l < LAYERS - 1:
                    grads[l, True].send(4, 7)

        kg = key_grads[l]
        each(head, 0, KV_HEADS)
        kg.two(2)
        grads[l, False].send(1, 4)
        if l < LAYERS - 1:
            grads[l + 1, False].two()

        rot = []
        for j in range(HEADS):
            t = dqz[j]
            rot.append(t * cos_q - swap(t) * sin_q)
        dq = [pltpu.roll(rot[0], 64, axis=1).astype(bf16)]
        for t in range(1, 5):
            dq.append((rot[2 * t - 1] + pltpu.roll(rot[2 * t], 64, axis=1)).astype(bf16))
        dq = jnp.concatenate(dq, axis=1)
        aT = apad[l].T
        gq = nn(aT, dq).astype(bf16)
        for s in range(KV_HEADS):
            kg.three(s)
        if l < LAYERS - 1:
            grads[l, True].two((0,))
            grads[l + 1, True].pair()
        dkv_in = []
        for s in range(KV_HEADS):
            t = kg.total(s).reshape(128, 128)
            dkv_in.append((t * cos_kv - swap(t) * sin_kv).astype(bf16))
        dkv_in = jnp.concatenate(dkv_in, axis=1)
        da = nt(dq, units(l, 40, 5)) + nt(dkv_in, units(l, 45, 3))
        set_unit(l, 40, gq[:, 0:128] + go4[...])
        for t in range(1, 5):
            set_unit(l, 40 + t, gq[:, 128 * t:128 * t + 128])
        gkv = nn(aT, dkv_in).astype(bf16)
        for t in range(3):
            set_unit(l, 45 + t, gkv[:, 128 * t:128 * t + 128])
        dh, dgain_attn = norm_back(hs[l], dh1, unspread(da), gain[l, 0:1, 0:D])
        rows = jnp.concatenate([dgain_attn, dgain_ffn, jnp.zeros((6, D), f32)], axis=0)
        rows = jnp.concatenate([rows, jnp.zeros((8, PD - D), f32)], axis=1)
        for s in range(ND):
            part = (pltpu.roll(rows, PD - 72 * s, axis=1) if s else rows)[:, 0:128]
            keep = land[l, 0, 20, slot_of(s)].astype(f32)[0:72, :]
            land[l, 0, 20, slot_of(s)] = jnp.concatenate([keep, part], axis=0).astype(bf16)
        grads[l, False].zero(1)
        return dh

    h = hidT[...].astype(f32).T
    h = forward(0, h)
    h = forward(1, h)
    hv[...] = h.astype(bf16)
    outputs = [
        pltpu.make_async_copy(src, dst, leave.at[n])
        for n, (src, dst) in enumerate(((hv, hout), (gv, ghid), (fine, oute), (finl, outl)))
    ]
    outputs[0].start()
    g = backward(1, goutT[...].astype(f32).T)
    g = backward(0, g)
    gv[...] = g
    outputs[1].start()
    grads[0, False].one(1)
    grads[0, False].send(4, 7)
    grads[1, False].pair()
    grads[1, True].three()
    grads[0, True].two((1,))
    grads[0, False].two()
    grads[1, False].three()
    grads[1, True].four()
    grads[0, True].pair()
    grads[0, False].pair()
    grads[1, True].five()
    grads[1, False].four()
    grads[0, True].three()
    grads[0, False].three()
    grads[1, False].five()
    grads[0, True].four()
    grads[0, False].four()
    grads[0, True].five()
    outputs[2].start()
    grads[0, False].five()
    outputs[3].start()
    for copy in outputs:
        copy.wait()


def unpack(h, gh, early, late, houtT, ghidT, gag, gq, gk, gv, go, gfg, ggate, gup, gdown):
    houtT[...] = h[...].astype(f32).T.astype(bf16)
    ghidT[...] = gh[...].T
    for l in range(LAYERS):
        attn = [None] * 12
        for cc in range(NC):
            i_, k_ = cc // 2, cc % 2
            for j in (2 * i_, 2 * i_ + 1, 16 + i_ % 4 + 4 * (i_ // 4)):
                val = (early[l, i_, k_, j - 2 * i_] if j < 16 else late[l, i_, k_, 0]).astype(f32)
                kind, t = j // 6, 6 * k_ + j % 6
                cols = slice(128 * t, 128 * t + 128)
                if kind == 0:
                    ggate[l, :, cols] = val[0:72]
                elif kind == 1:
                    gup[l, :, cols] = val[0:72]
                elif kind == 2:
                    at = slice(16 * t, 16 * t + 16)
                    for lt in range(4):
                        gdown[l, at, 128 * lt:128 * lt + 128] = val[16 * lt:16 * lt + 16]
                    gdown[l, at, 512:576] = val[64:80, 0:64]
                else:
                    t = 2 * k_ + j - 18 if j < 20 else 4 + 4 * k_ + j - 20
                    attn[t] = val[0:72]
                    if t == 4:
                        gag[l:l + 1, :] = val[72:73, 0:72]
                        gfg[l:l + 1, :] = val[73:74, 0:72]
        attn = jnp.concatenate(attn, axis=1)
        go[l] = attn[:, 0:D]
        gq[l] = attn[:, D:2 * D]
        kv = [attn[:, 2 * D + 64 * j:2 * D + 64 * j + 64] for j in range(2 * KV_HEADS)]
        gk[l] = jnp.concatenate(kv[0::2], axis=1)
        gv[l] = jnp.concatenate(kv[1::2], axis=1)


def body(
    hidden_in, positions, attn_gain, w_query, w_key, w_value, w_output, ffn_gain, w_gate, w_up, w_down, grad_out
):
    half = HEAD_DIM // 2
    freq = jnp.exp(-jnp.log(rope_base) * (2.0 * jnp.arange(half, dtype=f32) / HEAD_DIM))
    freq = jnp.tile(freq, 4).reshape(1, 128)
    outs = pl.pallas_call(
        kernel,
        out_shape=(
            jax.ShapeDtypeStruct((ROWS, D), bf16),
            jax.ShapeDtypeStruct((ROWS, D), f32),
            jax.ShapeDtypeStruct((LAYERS, NCHIP, 2, 2, R, 128), bf16),
            jax.ShapeDtypeStruct((LAYERS, NCHIP, 2, 1, R, 128), bf16),
        ),
        in_specs=[pl.BlockSpec(memory_space=pltpu.VMEM)] * 13,
        out_specs=tuple([pl.BlockSpec(memory_space=pl.ANY)] * 4),
        scratch_shapes=[
            pltpu.VMEM((NC * 64, 128), bf16),
            pltpu.VMEM((D, PD), bf16),
            pltpu.VMEM((PD, 128 * HEADS), bf16),
            pltpu.VMEM((LAYERS, 8, 128), f32),
            pltpu.VMEM((72, FF), bf16),
            pltpu.VMEM((LAYERS, 2, 24, ND, R, 128), bf16),
            pltpu.VMEM((96, 16, PD), bf16),
            pltpu.VMEM((LAYERS, NCHIP, 2, KV_HEADS, 2, 64, 128), bf16),
            pltpu.VMEM((NCHIP, 2, KV_HEADS, 2, 64, 128), bf16),
            pltpu.VMEM((LAYERS, NCHIP, KV_HEADS, 2, 64, 128), bf16),
            pltpu.VMEM((LAYERS, 7, KV_HEADS, 2, 64, 128), bf16),
            pltpu.VMEM((LAYERS, 24, ND, R, 128), bf16),
            pltpu.VMEM((LAYERS, 3, 16, 2, R, 128), bf16),
            pltpu.VMEM((LAYERS, 16, R, 128), bf16),
            pltpu.VMEM((LAYERS, 7, 2, R, 128), bf16),
            pltpu.VMEM((LAYERS, 3, 2, ND, R, 128), bf16),
            pltpu.VMEM((LAYERS, ND, R, 128), bf16),
            pltpu.VMEM((LAYERS, 7, R, 128), bf16),
            pltpu.VMEM((LAYERS, NCHIP, 2, 2, R, 128), bf16),
            pltpu.VMEM((LAYERS, NCHIP, 2, 1, R, 128), bf16),
            pltpu.VMEM((LAYERS, 6, 128, 256), bf16),
            pltpu.VMEM((LAYERS, 128, D), f32),
            pltpu.VMEM((LAYERS, 128, D), f32),
            pltpu.VMEM((LAYERS, 128, PD), bf16),
            pltpu.VMEM((LAYERS, 128, PD), bf16),
            pltpu.VMEM((LAYERS, 128, PD), bf16),
            pltpu.VMEM((LAYERS, KV_HEADS, 192, 256), bf16),
            pltpu.VMEM((KV_HEADS, 192, 256), bf16),
            pltpu.VMEM((LAYERS, KV_HEADS, 128, 192), f32),
            pltpu.VMEM((LAYERS, KV_HEADS, 8, 192), f32),
            pltpu.VMEM((HEADS, 128, 128), bf16),
            pltpu.VMEM((HEADS, 128, 128), f32),
            pltpu.VMEM((1024, 256), f32),
            pltpu.VMEM((1024, 256), f32),
            pltpu.VMEM((1024, 192), bf16),
            pltpu.VMEM((1024, 192), f32),
            pltpu.VMEM((128, PD), bf16),
            pltpu.VMEM((LAYERS, 8, PD), f32),
            pltpu.VMEM((128, 192), f32),
            pltpu.VMEM((256, 192), f32),
            pltpu.VMEM((PD, 128), bf16),
            pltpu.VMEM((ROWS, D), bf16),
            pltpu.VMEM((ROWS, D), f32),
            pltpu.SemaphoreType.DMA((359,)),
            pltpu.SemaphoreType.DMA((359,)),
            pltpu.SemaphoreType.DMA((4,)),
        ],
        compiler_params=pltpu.CompilerParams(
            collective_id=0, has_side_effects=True, vmem_limit_bytes=127 * 512 * 1024
        ),
    )(
        hidden_in.T, grad_out.T, positions.reshape(NC, ROWS), freq, attn_gain, ffn_gain,
        w_gate, w_up, w_down, w_output, w_query, w_key, w_value,
    )
    shapes = (
        (D, ROWS), (D, ROWS), (LAYERS, 72), (LAYERS, 72, D), (LAYERS, 72, KV_HEADS * HEAD_DIM),
        (LAYERS, 72, KV_HEADS * HEAD_DIM), (LAYERS, 72, D), (LAYERS, 72), (LAYERS, 72, FF), (LAYERS, 72, FF),
        (LAYERS, 192, D),
    )
    houtT, ghidT, *rest = pl.pallas_call(
        unpack,
        out_shape=[jax.ShapeDtypeStruct(shape, f32 if n else bf16) for n, shape in enumerate(shapes)],
        in_specs=[pl.BlockSpec(memory_space=pltpu.VMEM)] * 4,
        out_specs=[pl.BlockSpec(memory_space=pltpu.VMEM)] * 11,
        compiler_params=pltpu.CompilerParams(vmem_limit_bytes=127 * 512 * 1024),
    )(*outs)
    return (houtT.T, ghidT.T, *rest)


def solution(mesh):
    placed = (
        P(("dp", "ctx"), None),
        P("dp"),
        P(None, "dp"),
        P(None, "dp", None),
        P(None, "dp", None),
        P(None, "dp", None),
        P(None, "dp", None),
        P(None, "dp"),
        P(None, "dp", None),
        P(None, "dp", None),
        P(None, "dp", None),
        P(("dp", "ctx"), None),
    )
    out = (
        P(("dp", "ctx"), None),
        P(("dp", "ctx"), None),
        P(None, "dp"),
        P(None, "dp", None),
        P(None, "dp", None),
        P(None, "dp", None),
        P(None, "dp", None),
        P(None, "dp"),
        P(None, "dp", None),
        P(None, "dp", None),
        P(None, "dp", None),
    )
    return jax.shard_map(body, mesh=mesh, in_specs=placed, out_specs=out, check_vma=False)
```
